32 devices in a mesh: seq: 4 (over y, x), ctx: 8 (over z, core).
Axes of the slice: x: 2, y: 2, z: 4, core: 2. Of those that a mesh axis runs over, the one named last changes fastest.
Arguments:
- tokens: bfloat16 [2, 4, 1024, 2048], P(None, 'seq', 'ctx'), may hold values from -6 to 6
- lengths: int32 [2, 4], P(None, 'seq'), may hold values from 256 to 1024, as said below
- cotangent: bfloat16 [2, 4, 1024, 2048], P(None, 'seq', 'ctx'), may hold values from -6 to 6
- attn_gain: bfloat16 [2048], P(('seq', 'ctx')), may hold values from 0.5 to 1.5
- w_query: bfloat16 [2048, 2048], P(('seq', 'ctx')), may hold values from -0.125 to 0.125
- w_key: bfloat16 [2048, 512], P(('seq', 'ctx')), may hold values from -0.125 to 0.125
- w_value: bfloat16 [2048, 512], P(('seq', 'ctx')), may hold values from -0.125 to 0.125
- w_out: bfloat16 [2048, 2048], P(('seq', 'ctx')), may hold values from -3 to 3
- mlp_gain: bfloat16 [2048], P(('seq', 'ctx')), may hold values from 0.5 to 1.5
- w_gate: bfloat16 [2048, 8192], P('seq', 'ctx'), may hold values from -0.125 to 0.125
- w_up: bfloat16 [2048, 8192], P('seq', 'ctx'), may hold values from -0.125 to 0.125
- w_down: bfloat16 [8192, 2048], P('ctx', 'seq'), may hold values from -0.0625 to 0.0625
Outputs:
- activations: bfloat16 [2, 4, 1024, 2048], P(None, 'seq', 'ctx')
- input_grad: float32 [2, 4, 1024, 2048], P(None, 'seq', 'ctx')
- grad_attn_gain: float32 [2048], P(('seq', 'ctx'))
- grad_query: float32 [2048, 2048], P(('seq', 'ctx'))
- grad_key: float32 [2048, 512], P(('seq', 'ctx'))
- grad_value: float32 [2048, 512], P(('seq', 'ctx'))
- grad_out: float32 [2048, 2048], P(('seq', 'ctx'))
- grad_mlp_gain: float32 [2048], P(('seq', 'ctx'))
- grad_gate: float32 [2048, 8192], P('seq', 'ctx')
- grad_up: float32 [2048, 8192], P('seq', 'ctx')
- grad_down: float32 [8192, 2048], P('ctx', 'seq')
The draws below stay inside these ranges and needn't reach their ends.
Inputs may be any that keep to these rules, and one draw needn't show every extreme that they name: A sequence's valid slots are its first lengths slots; in every draw some sequence has exactly 1024.
All inputs are finite; a program needn't handle non-finite values.
Results may differ from the reference program's by a relative error of at most 0.015.
Values may be sent and summed in bfloat16 or wider, within the bound.
No kernel may reach another device: no remote copies, remote signals or barrier semaphores. Data moves between devices by JAX's collectives and lax.ppermute only.
A program may use at most 256 MiB of HBM per device.

```python
import math
import jax
import jax.numpy as jnp
from jax import lax

D = 2048
HEADS = 32
KV_HEADS = 8
HEAD_DIM = 64
FF = 8192
MB = 2
SEQS = 4
LEN = 1024


def draw_lengths(key, part):
    first_key, second_key = jax.random.split(key)
    drawn = jax.random.randint(first_key, (MB * SEQS,), LEN // 4, LEN + 1)
    chosen = jax.random.randint(second_key, (), 0, MB * SEQS)
    drawn = jnp.where(jnp.arange(MB * SEQS) == chosen, LEN, drawn)
    return drawn.reshape(MB, SEQS).astype(jnp.int32)


def level_of(stream_key, shape, shards, smallest, largest):
    loudness, own = 1.0, jax.random.fold_in(stream_key, 6)
    for axis_at, blocks in shards:
        heights = jnp.exp(jax.random.uniform(jax.random.fold_in(own, axis_at), (blocks,), jnp.float32, smallest / len(shards), largest / len(shards)))
        loudness = loudness * jnp.repeat(heights, shape[axis_at] // blocks).reshape([-1 if axis == axis_at else 1 for axis in range(len(shape))])
    return loudness


def gaussian(own_key, extent, deviation, most, pieces=(), kind=jnp.bfloat16):
    values = jax.random.normal(own_key, extent, jnp.float32) * deviation
    if len(pieces) > 0:
        values = level_of(own_key, extent, pieces, -0.22, 0.18) * values
    return jnp.clip(values, min=-most, max=most).astype(kind)


def setup_inputs(seed: int = 0) -> dict:
    keys = jax.random.split(jax.random.key(seed), 13)
    return {
        "tokens": gaussian(keys[0], (MB, SEQS, LEN, D), 1.0, 6.0, ((1, 4), (2, 8))),
        "lengths": draw_lengths(jax.random.fold_in(keys[12], 71), 0),
        "cotangent": gaussian(keys[2], (MB, SEQS, LEN, D), 1.0, 6.0, ((1, 4), (2, 8))),
        "attn_gain": jnp.clip(1.0 + 0.1 * jax.random.normal(keys[3], (D,), jnp.float32), 0.5, 1.5).astype(jnp.bfloat16),
        "w_query": gaussian(keys[4], (D, HEADS * HEAD_DIM), D ** -0.5, 0.125, ((0, 32),)),
        "w_key": gaussian(keys[5], (D, KV_HEADS * HEAD_DIM), D ** -0.5, 0.125, ((0, 32),)),
        "w_value": gaussian(keys[6], (D, KV_HEADS * HEAD_DIM), D ** -0.5, 0.125, ((0, 32),)),
        "w_out": gaussian(keys[7], (HEADS * HEAD_DIM, D), 4 ** -0.5, 3.0, ((0, 32),)),
        "mlp_gain": jnp.clip(1.0 + 0.1 * jax.random.normal(keys[8], (D,), jnp.float32), 0.5, 1.5).astype(jnp.bfloat16),
        "w_gate": gaussian(keys[9], (D, FF), D ** -0.5, 0.125, ((0, 4), (1, 8))),
        "w_up": gaussian(keys[10], (D, FF), D ** -0.5, 0.125, ((0, 4), (1, 8))),
        "w_down": gaussian(keys[11], (FF, D), FF ** -0.5, 0.0625, ((0, 8), (1, 4))),
    }


EPSILON = 1e-05
ROPE_BASE = 500000.0

@jax.custom_vjp
def low(v):
    return lax.optimization_barrier(v.astype(jnp.bfloat16)).astype(jnp.float32)

@jax.custom_vjp
def low_back(v):
    return v

def low_keep(v):
    return (low(v), None)

def low_pass(kept, grad):
    return (grad,)

def back_keep(v):
    return (v, None)

def back_low(kept, grad):
    return (low(grad),)
low.defvjp(low_keep, low_pass)
low_back.defvjp(back_keep, back_low)

def matmul(left, right):
    return jnp.dot(left, right, precision=lax.Precision.HIGHEST, preferred_element_type=jnp.float32)

def rms_scale(values, gain):
    inverse = lax.rsqrt(lax.optimization_barrier(jnp.mean(values * values, axis=-1, keepdims=True)) + EPSILON)
    return values * inverse * gain

def scaled_frequency():
    half_dim = HEAD_DIM // 2
    base_freq = ROPE_BASE ** (-jnp.arange(half_dim, dtype=jnp.float32) * 2.0 / HEAD_DIM)
    wave = 2.0 * math.pi / base_freq
    smooth = (8192.0 / wave - 1.0) / 3.0
    middle = (1.0 - smooth) * base_freq / 32.0 + smooth * base_freq
    return jnp.where(wave < 2048.0, base_freq, jnp.where(wave > 8192.0, base_freq / 32.0, middle))

def rope_tables(positions):
    frequency = scaled_frequency()
    angles = positions[:, None] * frequency[None, :]
    return (jnp.cos(angles), jnp.sin(angles))

def rotate(values, cosine, sine_table):
    half_dim = values.shape[-1] // 2
    first_half = values[..., :half_dim]
    second_half = values[..., half_dim:]
    cos_part = cosine[:, None, :]
    sin_part = sine_table[:, None, :]
    return jnp.concatenate([first_half * cos_part - second_half * sin_part, second_half * cos_part + first_half * sin_part], axis=-1)

def block_layer(tokens_seq, params, length):
    attn_gain, w_query, w_key, w_value, w_out, mlp_gain, w_gate, w_up, w_down = params
    per_kv = HEADS // KV_HEADS
    scaling = 1.0 / math.sqrt(HEAD_DIM)
    slot_pos = jnp.arange(LEN)
    cosine, sine_table = rope_tables(slot_pos.astype(jnp.float32))
    normed = low(rms_scale(tokens_seq, attn_gain))
    queries = low(rotate(low_back(matmul(normed, w_query)).reshape(LEN, HEADS, HEAD_DIM), cosine, sine_table))
    keys_rot = low(rotate(low_back(matmul(normed, w_key)).reshape(LEN, KV_HEADS, HEAD_DIM), cosine, sine_table))
    values_low = low(low_back(matmul(normed, w_value))).reshape(LEN, KV_HEADS, HEAD_DIM)
    allowed = (slot_pos[None, :] <= slot_pos[:, None]) & (slot_pos[None, :] < length)

    def one_head(operands):
        query_head, key_head, value_head = operands
        scores = jnp.einsum('igd,jd->gij', query_head, key_head, precision=lax.Precision.HIGHEST) * scaling
        scores = jnp.where(allowed[None], low_back(scores), -1e+30)
        row_max = lax.optimization_barrier(jnp.max(scores, axis=-1, keepdims=True))
        shifted = jnp.exp(scores - row_max)
        attn_probs = low(shifted / lax.optimization_barrier(jnp.sum(shifted, axis=-1, keepdims=True)))
        return jnp.einsum('gij,jd->igd', attn_probs, value_head, precision=lax.Precision.HIGHEST)
    head_outputs = lax.map(jax.checkpoint(one_head), (queries.reshape(LEN, KV_HEADS, per_kv, HEAD_DIM).transpose(1, 0, 2, 3), keys_rot.transpose(1, 0, 2), values_low.transpose(1, 0, 2)))
    attended = low(low_back(head_outputs.transpose(1, 0, 2, 3).reshape(LEN, HEADS * HEAD_DIM)))
    residual = tokens_seq + low_back(matmul(attended, w_out))
    normed_mlp = low(rms_scale(residual, mlp_gain))
    gate_val = low_back(matmul(normed_mlp, w_gate))
    up_val = low_back(matmul(normed_mlp, w_up))
    hidden = low(gate_val / (1.0 + jnp.exp(-gate_val)) * up_val)
    return residual + low_back(matmul(hidden, w_down))

def reference(tokens, lengths, cotangent, attn_gain, w_query, w_key, w_value, w_out, mlp_gain, w_gate, w_up, w_down):
    params = tuple((weight_arr.astype(jnp.float32) for weight_arr in (attn_gain, w_query, w_key, w_value, w_out, mlp_gain, w_gate, w_up, w_down)))
    inputs_all = tokens.astype(jnp.float32).reshape(MB * SEQS, LEN, D)
    cots_all = cotangent.astype(jnp.float32).reshape(MB * SEQS, LEN, D)
    lengths_all = lengths.reshape(MB * SEQS)

    def advance(totals, item):
        tokens_seq, cot_seq, length = item
        valid = (jnp.arange(LEN) < length).astype(jnp.float32)[:, None]
        outputs, pullback = jax.vjp(lambda seq_in, params_in: block_layer(seq_in, params_in, length), tokens_seq, params)
        grad_in, grad_params = pullback(cot_seq * valid)
        totals = tuple((total_arr + grad_arr for total_arr, grad_arr in zip(totals, grad_params)))
        return (totals, (outputs.astype(jnp.bfloat16), grad_in))
    zeros_init = tuple((jnp.zeros(weight_arr.shape, jnp.float32) for weight_arr in params))
    totals, (outputs, grads_in) = lax.scan(advance, zeros_init, (inputs_all, cots_all, lengths_all))
    activations = outputs.reshape(MB, SEQS, LEN, D)
    input_grad = grads_in.reshape(MB, SEQS, LEN, D)
    return (activations, input_grad, totals[0], totals[1], totals[2], totals[3], totals[4], totals[5], totals[6], totals[7], totals[8])
```

```python
import functools
import math

import jax
import jax.numpy as jnp
from jax import lax
from jax.experimental import pallas as pl
from jax.experimental.pallas import tpu as pltpu
from jax.sharding import PartitionSpec as P

HEAD_DIM = 64
LANES = 128
EPSILON = 1e-05
ROPE_BASE = 500000.0
MASKED = -1e30
VMEM_LIMIT = 56 * 1024 * 1024
F32 = jnp.float32
BF16 = jnp.bfloat16


def folded_order(count):
    return list(range(0, count, 2)) + list(range(1, count, 2))[::-1]


def swap_core(array):
    ctx = lax.axis_size("ctx")
    return lax.ppermute(array, "ctx", [(i, i ^ 1) for i in range(ctx)])


def swap_seq(array, bit):
    seq = lax.axis_size("seq")
    return lax.ppermute(array, "seq", [(i, i ^ bit) for i in range(seq)])


def ring_step(array):
    chips = lax.axis_size("ctx") // 2
    order = folded_order(chips)
    pairs = [
        (order[i] * 2 + core, order[(i + 1) % chips] * 2 + core)
        for i in range(chips)
        for core in range(2)
    ]
    return lax.ppermute(array, "ctx", pairs)


def ring_gather(array):
    slots = [array]
    for _ in range(lax.axis_size("ctx") // 2 - 1):
        slots.append(ring_step(slots[-1]))
    return slots


def ring_scatter(parts):
    chips = len(parts)
    total = parts[1 % chips].astype(F32)
    for k in range(2, chips + 1):
        total = ring_step(total.astype(BF16)).astype(F32) + parts[k % chips].astype(F32)
    return total


def cube_gather(array):
    seq = lax.axis_size("seq")
    if seq == 4:
        half = array.shape[0] // 2
        first, second = swap_seq(array, 1), swap_seq(array, 2)
        return [
            [array],
            [first],
            [second],
            [swap_seq(first[:half], 2), swap_seq(second[half:], 1)],
        ]
    pieces = {0: array}
    bit = 1
    while bit < seq:
        pieces.update({r ^ bit: swap_seq(piece, bit) for r, piece in pieces.items()})
        bit *= 2
    return [[pieces[r]] for r in range(seq)]


def cube_scatter(chunks):
    seq = lax.axis_size("seq")
    if seq == 4:
        half = chunks[3].shape[0] // 2
        to_second = swap_seq(chunks[3][:half].astype(BF16), 1).astype(F32)
        to_first = swap_seq(chunks[3][half:].astype(BF16), 2).astype(F32)
        first = jnp.concatenate([chunks[1][:half], chunks[1][half:] + to_first])
        second = jnp.concatenate([chunks[2][:half] + to_second, chunks[2][half:]])
        return (
            chunks[0]
            + swap_seq(first.astype(BF16), 1).astype(F32)
            + swap_seq(second.astype(BF16), 2).astype(F32)
        )
    held = dict(enumerate(chunks))
    bit = seq // 2
    while bit >= 1:
        held = {
            r: held[r] + swap_seq(held[r | bit].astype(BF16), bit).astype(F32)
            for r in held
            if not r & bit
        }
        bit //= 2
    return held[0]


def scaled_frequency():
    half_dim = HEAD_DIM // 2
    base_freq = ROPE_BASE ** (-jnp.arange(half_dim, dtype=F32) * 2.0 / HEAD_DIM)
    wave = 2.0 * math.pi / base_freq
    smooth = (8192.0 / wave - 1.0) / 3.0
    middle = (1.0 - smooth) * base_freq / 32.0 + smooth * base_freq
    return jnp.where(wave < 2048.0, base_freq, jnp.where(wave > 8192.0, base_freq / 32.0, middle))


def rope_tables(positions):
    angles = positions.astype(F32)[:, None] * scaled_frequency()[None, :]
    cosine, sine = jnp.cos(angles), jnp.sin(angles)
    return (
        jnp.concatenate([cosine] * 4, axis=1),
        jnp.concatenate([-sine, sine, -sine, sine], axis=1),
    )


def rotate_lanes(values, cosine, sine):
    lane = lax.broadcasted_iota(jnp.int32, values.shape, 1)
    partner = jnp.where(
        (lane % HEAD_DIM) < HEAD_DIM // 2,
        pltpu.roll(values, LANES - HEAD_DIM // 2, 1),
        pltpu.roll(values, HEAD_DIM // 2, 1),
    )
    return values * cosine + partner * sine


def qkv_kernel(query_blocks, rope_blocks, x_ref, w_ref, cos_ref, sin_ref, out_ref):
    block = pl.program_id(0)
    raw = jnp.dot(x_ref[...], w_ref[...], preferred_element_type=F32)
    scale = jnp.where(block < query_blocks, 1.0 / math.sqrt(HEAD_DIM), 1.0)
    for at in range(raw.shape[1] // LANES):
        part = raw[:, at * LANES : (at + 1) * LANES]
        turned = rotate_lanes(part, cos_ref[...], sin_ref[...]) * scale
        out_ref[:, at * LANES : (at + 1) * LANES] = jnp.where(
            block < rope_blocks, turned, part
        ).astype(BF16)


def project_qkv(x, weights, cosine, sine, query_width, kv_width):
    rows, depth = x.shape
    width = query_width + 2 * kv_width
    block = 256
    return pl.pallas_call(
        functools.partial(qkv_kernel, query_width // block, (query_width + kv_width) // block),
        grid=(width // block,),
        in_specs=[
            pl.BlockSpec((rows, depth), lambda j: (0, 0)),
            pl.BlockSpec((depth, block), lambda j: (0, j)),
            pl.BlockSpec((rows, LANES), lambda j: (0, 0)),
            pl.BlockSpec((rows, LANES), lambda j: (0, 0)),
        ],
        out_specs=pl.BlockSpec((rows, block), lambda j: (0, j)),
        out_shape=jax.ShapeDtypeStruct((rows, width), BF16),
        compiler_params=pltpu.CompilerParams(vmem_limit_bytes=VMEM_LIMIT),
        cost_estimate=pl.CostEstimate(
            flops=2 * rows * depth * width,
            bytes_accessed=2 * (rows * depth + depth * width + rows * width),
            transcendentals=0,
        ),
    )(x, weights, cosine, sine)


def transposed(values):
    return values.astype(F32).T.astype(BF16)


def attend_kernel(limit_ref, kpos_ref, qpos_ref, q_ref, k_ref, v_ref, out_ref, lse_ref, bias):
    @pl.when(pl.program_id(0) == 0)
    def _():
        allowed = (kpos_ref[...] <= qpos_ref[...]) & (kpos_ref[...] < limit_ref[0])
        bias[...] = jnp.where(allowed, 0.0, MASKED)

    heads = q_ref.shape[1] // HEAD_DIM
    q_t = transposed(q_ref[...])
    v_t = transposed(v_ref[...])
    outs = []
    for h in range(heads):
        a = h * 2 // heads
        k_h = k_ref[:, a * HEAD_DIM : (a + 1) * HEAD_DIM]
        scores = (
            jnp.dot(k_h, q_t[h * HEAD_DIM : (h + 1) * HEAD_DIM], preferred_element_type=F32)
            + bias[...]
        )
        top = jnp.max(scores, axis=0, keepdims=True)
        shifted = jnp.exp(scores - top)
        total = jnp.sum(shifted, axis=0, keepdims=True)
        out_t = jnp.dot(
            v_t[a * HEAD_DIM : (a + 1) * HEAD_DIM],
            shifted.astype(BF16),
            preferred_element_type=F32,
        )
        outs.append(out_t / total)
        lse_ref[h : h + 1, :] = top + jnp.log(total)
    out_ref[...] = jnp.concatenate(outs, axis=0).T.astype(BF16)


def attend(qkv, part, kv, limit, kpos, qpos, query_width, kv_width):
    rows, keys = qpos.shape[1], kv.shape[0]
    pairs = kv_width // LANES
    width = query_width // pairs
    heads = width // HEAD_DIM
    grid_spec = pltpu.PrefetchScalarGridSpec(
        num_scalar_prefetch=1,
        grid=(pairs,),
        in_specs=[
            pl.BlockSpec((keys, 1), lambda i, n: (0, 0)),
            pl.BlockSpec((1, rows), lambda i, n: (0, 0)),
            pl.BlockSpec((rows, width), lambda i, n: (part, i)),
            pl.BlockSpec((keys, LANES), lambda i, n: (0, i)),
            pl.BlockSpec((keys, LANES), lambda i, n: (0, pairs + i)),
        ],
        out_specs=[
            pl.BlockSpec((rows, width), lambda i, n: (0, i)),
            pl.BlockSpec((heads, rows), lambda i, n: (i, 0)),
        ],
        scratch_shapes=[pltpu.VMEM((keys, rows), F32)],
    )
    return pl.pallas_call(
        attend_kernel,
        grid_spec=grid_spec,
        out_shape=[
            jax.ShapeDtypeStruct((rows, query_width), BF16),
            jax.ShapeDtypeStruct((query_width // HEAD_DIM, rows), F32),
        ],
        compiler_params=pltpu.CompilerParams(vmem_limit_bytes=VMEM_LIMIT),
        cost_estimate=pl.CostEstimate(
            flops=16 * rows * keys * query_width,
            bytes_accessed=4 * rows * query_width + 4 * keys * kv_width,
            transcendentals=rows * keys * query_width // HEAD_DIM,
        ),
    )(limit, kpos, qpos, qkv, kv, kv)


def attend_back_kernel(
    limit_ref, kpos_ref, qpos_ref, q_ref, k_ref, v_ref, do_ref, lse_ref, cos_ref, sin_ref,
    dq_ref, dk_ref, dv_ref, bias,
):
    @pl.when(pl.program_id(0) == 0)
    def _():
        allowed = (kpos_ref[...] <= qpos_ref[...]) & (kpos_ref[...] < limit_ref[0])
        bias[...] = jnp.where(allowed, 0.0, MASKED)

    heads = q_ref.shape[1] // HEAD_DIM
    per_kv = heads // 2
    q_t = transposed(q_ref[...])
    do_t = transposed(do_ref[...])
    k_t = transposed(k_ref[...])
    lane = lax.broadcasted_iota(jnp.int32, (k_ref.shape[0], LANES), 1)
    d_queries = []
    d_keys, d_values = [], []
    for a in range(2):
        k_h = k_ref[:, a * HEAD_DIM : (a + 1) * HEAD_DIM]
        v_h = v_ref[:, a * HEAD_DIM : (a + 1) * HEAD_DIM]
        dk_sum, dv_sum = [None, None], [None, None]
        for g in range(per_kv):
            h = a * per_kv + g
            rows = slice(h * HEAD_DIM, (h + 1) * HEAD_DIM)
            pair = slice((h // 2) * LANES, (h // 2 + 1) * LANES)
            scores = jnp.dot(k_h, q_t[rows], preferred_element_type=F32) + bias[...]
            probs = jnp.exp(scores - lse_ref[h : h + 1, :])
            d_probs = jnp.dot(v_h, do_t[rows], preferred_element_type=F32)
            mean = jnp.sum(d_probs * probs, axis=0, keepdims=True)
            d_scores = (probs * (d_probs - mean)).astype(BF16)
            probs_low = probs.astype(BF16)
            d_queries.append(
                jnp.dot(
                    k_t[a * HEAD_DIM : (a + 1) * HEAD_DIM], d_scores, preferred_element_type=F32
                )
            )
            dk_term = jnp.dot(d_scores, q_ref[:, pair], preferred_element_type=F32)
            dv_term = jnp.dot(probs_low, do_ref[:, pair], preferred_element_type=F32)
            e = h % 2
            dk_sum[e] = dk_term if dk_sum[e] is None else dk_sum[e] + dk_term
            dv_sum[e] = dv_term if dv_sum[e] is None else dv_sum[e] + dv_term
        for sums, kept in ((dk_sum, d_keys), (dv_sum, d_values)):
            mixed = jnp.where(lane < HEAD_DIM, sums[0], sums[1])
            kept.append(mixed + pltpu.roll(mixed, HEAD_DIM, 1))
    dk_ref[...] = jnp.where(lane < HEAD_DIM, d_keys[0], d_keys[1])
    dv_ref[...] = jnp.where(lane < HEAD_DIM, d_values[0], d_values[1])
    d_query = jnp.concatenate(d_queries, axis=0).T
    for at in range(d_query.shape[1] // LANES):
        cut = slice(at * LANES, (at + 1) * LANES)
        dq_ref[:, cut] = (
            rotate_lanes(d_query[:, cut], cos_ref[...], -sin_ref[...]) / math.sqrt(HEAD_DIM)
        ).astype(BF16)


def attend_back(qkv, part, kv, d_out, lse, limit, kpos, qpos, cosine, sine, query_width, kv_width):
    rows, keys = qpos.shape[1], kv.shape[0]
    pairs = kv_width // LANES
    width = query_width // pairs
    heads = width // HEAD_DIM
    grid_spec = pltpu.PrefetchScalarGridSpec(
        num_scalar_prefetch=1,
        grid=(pairs,),
        in_specs=[
            pl.BlockSpec((keys, 1), lambda i, n: (0, 0)),
            pl.BlockSpec((1, rows), lambda i, n: (0, 0)),
            pl.BlockSpec((rows, width), lambda i, n: (part, i)),
            pl.BlockSpec((keys, LANES), lambda i, n: (0, i)),
            pl.BlockSpec((keys, LANES), lambda i, n: (0, pairs + i)),
            pl.BlockSpec((rows, width), lambda i, n: (0, i)),
            pl.BlockSpec((heads, rows), lambda i, n: (i, 0)),
            pl.BlockSpec((rows, LANES), lambda i, n: (0, 0)),
            pl.BlockSpec((rows, LANES), lambda i, n: (0, 0)),
        ],
        out_specs=[
            pl.BlockSpec((rows, width), lambda i, n: (0, i)),
            pl.BlockSpec((keys, LANES), lambda i, n: (0, i)),
            pl.BlockSpec((keys, LANES), lambda i, n: (0, i)),
        ],
        scratch_shapes=[pltpu.VMEM((keys, rows), F32)],
    )
    return pl.pallas_call(
        attend_back_kernel,
        grid_spec=grid_spec,
        out_shape=[
            jax.ShapeDtypeStruct((rows, query_width), BF16),
            jax.ShapeDtypeStruct((keys, kv_width), F32),
            jax.ShapeDtypeStruct((keys, kv_width), F32),
        ],
        compiler_params=pltpu.CompilerParams(vmem_limit_bytes=VMEM_LIMIT),
        cost_estimate=pl.CostEstimate(
            flops=40 * rows * keys * query_width,
            bytes_accessed=6 * rows * query_width + 12 * keys * kv_width,
            transcendentals=rows * keys * query_width // HEAD_DIM,
        ),
    )(limit, kpos, qpos, qkv, kv, kv, d_out, lse, cosine, sine)


def unrotate_kernel(x_ref, cos_ref, sin_ref, out_ref):
    for at in range(x_ref.shape[1] // LANES):
        cut = slice(at * LANES, (at + 1) * LANES)
        out_ref[:, cut] = rotate_lanes(x_ref[:, cut], cos_ref[...], -sin_ref[...]).astype(BF16)


def unrotate(x, cosine, sine):
    return pl.pallas_call(
        unrotate_kernel,
        out_shape=jax.ShapeDtypeStruct(x.shape, BF16),
    )(x, cosine, sine)


def rms_inverse(values):
    return lax.rsqrt(jnp.mean(values * values, axis=-1, keepdims=True) + EPSILON)


def rms_back(grad_in, plain, inverse, gain):
    scaled = grad_in * gain
    back = inverse * (scaled - plain * jnp.mean(scaled * plain, axis=-1, keepdims=True))
    return (back, jnp.sum(grad_in * plain, axis=0))


def body(
    tokens,
    lengths,
    cotangent,
    attn_gain,
    w_query,
    w_key,
    w_value,
    w_out,
    mlp_gain,
    w_gate,
    w_up,
    w_down,
):
    batches, _, slot_count, model_width = tokens.shape
    seq_size, ctx_size = lax.axis_size("seq"), lax.axis_size("ctx")
    chips = ctx_size // 2
    seq_at, ctx_at = lax.axis_index("seq"), lax.axis_index("ctx")
    chip_at, core = ctx_at // 2, ctx_at % 2
    order = folded_order(chips)
    shard = w_query.shape[0]
    query_half, kv_half = w_query.shape[1] // 2, w_key.shape[1] // 2
    out_half = model_width // 2
    chip_rows = 2 * slot_count
    attn_width = query_half + 2 * kv_half
    hidden_width = w_gate.shape[1]

    def chip_back(k):
        index = jnp.int32(0)
        for place, chip in enumerate(order):
            index = jnp.where(chip_at == chip, order[(place - k) % chips], index)
        return index

    slot_chip = [chip_back(k) for k in range(chips)]

    def half(array, which, axis):
        size = array.shape[axis] // 2
        return lax.dynamic_slice_in_dim(array, which * size, size, axis)

    def mine(array, axis):
        return half(array, core, axis)

    def others(array, axis):
        return half(array, 1 - core, axis)

    def by_core(own, other, axis):
        return jnp.where(
            core == 0,
            jnp.concatenate([own, other], axis),
            jnp.concatenate([other, own], axis),
        )

    def turn_blocks(array):
        block = array.shape[-1] // seq_size
        bit = 1
        while bit < seq_size:
            turned = jnp.concatenate(
                [
                    array[..., (r ^ bit) * block : ((r ^ bit) + 1) * block]
                    for r in range(seq_size)
                ],
                axis=-1,
            )
            array = jnp.where((seq_at & bit) != 0, turned, array)
            bit *= 2
        return array

    def block_row(r, k):
        return ((seq_at ^ r) * chips + slot_chip[k]) * (2 * shard)

    def plane_gather(piece, rotation):
        total = 2 * shard * seq_size * chips
        out = jnp.zeros((total, piece.shape[1]), BF16)
        for k, slot in enumerate(ring_gather(piece)):
            for r, blocks in enumerate(cube_gather(slot)):
                at = (block_row(r, k) + rotation) % total
                for block in blocks:
                    out = lax.dynamic_update_slice(out, block, (at, 0))
                    at = at + block.shape[0]
        return out

    def plane_scatter(partial, rotation):
        total = partial.shape[0]
        summed = []
        for k in range(chips):
            chunks = [
                lax.dynamic_slice_in_dim(
                    partial, (block_row(r, k % chips) + rotation) % total, 2 * shard, 0
                )
                for r in range(seq_size)
            ]
            summed.append(cube_scatter(chunks))
        return ring_scatter(summed)

    gains = jnp.concatenate(
        [attn_gain[:, None], mlp_gain[:, None], jnp.zeros((shard, LANES - 2), BF16)], axis=1
    )
    piece_a = by_core(
        jnp.concatenate([mine(w_query, 1), mine(w_key, 1), mine(w_value, 1), gains], 1),
        swap_core(
            jnp.concatenate([others(w_query, 1), others(w_key, 1), others(w_value, 1), gains], 1)
        ),
        0,
    )
    piece_o = by_core(mine(w_out, 1), swap_core(others(w_out, 1)), 0)
    x_own = tokens[:, 0]
    x_chip = by_core(x_own, swap_core(x_own), 1)
    attn_w = plane_gather(piece_a, 0)
    out_rotation = core * query_half
    out_w = plane_gather(piece_o, out_rotation)
    gate_w = jnp.concatenate([b for blocks in cube_gather(w_gate) for b in blocks], 0)
    up_w = jnp.concatenate([b for blocks in cube_gather(w_up) for b in blocks], 0)
    down_w = jnp.concatenate(
        [jnp.concatenate(blocks, 0) for blocks in cube_gather(w_down)], axis=1
    )

    first_row = chip_at * chip_rows
    q_positions = first_row + jnp.arange(chip_rows)
    cosine, sine = rope_tables(q_positions)
    cosine_all, sine_all = jnp.tile(cosine, (batches, 1)), jnp.tile(sine, (batches, 1))
    qpos = q_positions[None, :]
    kpos = jnp.concatenate([slot_chip[k] * chip_rows + jnp.arange(chip_rows) for k in range(chips)])
    kpos = kpos[:, None]
    own_pos = ctx_at * slot_count + jnp.arange(slot_count)
    gain_table = attn_w[:, attn_width : attn_width + 2].astype(F32).T
    gain_a, gain_m = gain_table[0], gain_table[1]

    x_rows = x_chip.reshape(batches * chip_rows, model_width).astype(F32)
    inverse_rows = rms_inverse(x_rows)
    normed_a = (x_rows * inverse_rows * gain_a).astype(BF16)
    qkv = project_qkv(normed_a, attn_w, cosine_all, sine_all, query_half, kv_half)
    kv_all, outs, lses, attended = [], [], [], []
    for b in range(batches):
        kv = qkv[b * chip_rows : (b + 1) * chip_rows, query_half:]
        kv_all.append(jnp.concatenate(ring_gather(kv), 0))
    for b in range(batches):
        out, lse = attend(qkv, b, kv_all[b], lengths[b], kpos, qpos, query_half, kv_half)
        outs.append(out)
        lses.append(lse)
        attended.append(jnp.concatenate([out, swap_core(out)], axis=1))

    residual, plain_m, inverse_m, group_in, group_d, d_own = [], [], [], [], [], []

    def group_rows(own):
        slots = ring_gather(own)
        return jnp.concatenate(slots + [swap_core(slot) for slot in slots], 0)

    for b in range(batches):
        valid = (own_pos < lengths[b, 0]).astype(F32)[:, None]
        d_output = cotangent[b, 0].astype(F32) * valid
        d_own.append(d_output)
        group_d.append(group_rows(turn_blocks(d_output.astype(BF16))))
    for b in range(batches):
        branch = jnp.dot(attended[b], out_w, preferred_element_type=F32)
        branch = by_core(mine(branch, 0), swap_core(others(branch, 0)), 1)
        res = x_own[b].astype(F32) + branch
        inverse = rms_inverse(res)
        plain = res * inverse
        residual.append(res)
        inverse_m.append(inverse)
        plain_m.append(plain)
        group_in.append(group_rows(turn_blocks((plain * gain_m).astype(BF16))))

    def back_to_owner(partial):
        rows = chips * slot_count
        received = swap_core(partial[rows:].astype(BF16)).astype(F32)
        own = partial[:rows] + received
        return turn_blocks(
            ring_scatter([own[k * slot_count : (k + 1) * slot_count] for k in range(chips)])
        )

    activations, hiddens, d_gates, d_ups, d_normed = [], [], [], [], []
    for b in range(batches):
        gate_val = jnp.dot(group_in[b], gate_w, preferred_element_type=F32)
        up_val = jnp.dot(group_in[b], up_w, preferred_element_type=F32)
        d_hidden = jnp.einsum("rd,fd->rf", group_d[b], down_w, preferred_element_type=F32)
        sigmoid_g = 1.0 / (1.0 + jnp.exp(-gate_val))
        activated = gate_val * sigmoid_g
        slope = sigmoid_g * (1.0 + gate_val * (1.0 - sigmoid_g))
        d_gate = (d_hidden * up_val * slope).astype(BF16)
        d_up = (d_hidden * activated).astype(BF16)
        hidden = (activated * up_val).astype(BF16)
        hiddens.append(hidden)
        d_gates.append(d_gate)
        d_ups.append(d_up)
        partial_back = jnp.einsum(
            "rf,df->rd", d_gate, gate_w, preferred_element_type=F32
        ) + jnp.einsum("rf,df->rd", d_up, up_w, preferred_element_type=F32)
        d_normed.append(back_to_owner(partial_back))
    for b in range(batches):
        partial_out = jnp.dot(hiddens[b], down_w, preferred_element_type=F32)
        activations.append((residual[b] + back_to_owner(partial_out)).astype(BF16))

    d_resid, gain_m_parts, d_half, d_queries, d_kvs = [], [], [], [], []
    for b in range(batches):
        back_m, gain_part = rms_back(d_normed[b], plain_m[b], inverse_m[b], gain_m)
        gain_m_parts.append(gain_part)
        d_res = d_own[b] + back_m
        d_resid.append(d_res)
        d_low = d_res.astype(BF16)
        d_half.append(by_core(mine(d_low, 1), swap_core(others(d_low, 1)), 0))
        d_att = jnp.einsum("rd,hd->rh", d_half[b], out_w, preferred_element_type=F32)
        d_att = (d_att[:, :query_half] + swap_core(d_att[:, query_half:])).astype(BF16)
        d_query, d_key, d_value = attend_back(
            qkv, b, kv_all[b], d_att, lses[b], lengths[b], kpos, qpos, cosine, sine,
            query_half, kv_half,
        )
        d_queries.append(d_query)
        slots = [
            jnp.concatenate([d[k * chip_rows : (k + 1) * chip_rows] for d in (d_key, d_value)], 1)
            for k in range(chips)
        ]
        d_kvs.append(ring_scatter(slots))

    group_in_all = jnp.concatenate(group_in, 0)
    group_d_all = jnp.concatenate(group_d, 0)
    grad_gate = jnp.einsum(
        "rd,rf->df", group_in_all, jnp.concatenate(d_gates, 0), preferred_element_type=F32
    )
    grad_up = jnp.einsum(
        "rd,rf->df", group_in_all, jnp.concatenate(d_ups, 0), preferred_element_type=F32
    )
    grad_down = jnp.einsum(
        "rf,rd->fd", jnp.concatenate(hiddens, 0), group_d_all, preferred_element_type=F32
    )
    depth = w_gate.shape[0]
    grad_gate = cube_scatter([grad_gate[r * depth : (r + 1) * depth] for r in range(seq_size)])
    grad_up = cube_scatter([grad_up[r * depth : (r + 1) * depth] for r in range(seq_size)])
    depth = w_down.shape[1]
    grad_down = cube_scatter(
        [grad_down[:, r * depth : (r + 1) * depth] for r in range(seq_size)]
    )
    grad_out = jnp.einsum(
        "rh,rd->hd",
        jnp.concatenate(attended, 0),
        jnp.concatenate(d_half, 0),
        preferred_element_type=F32,
    )
    grad_out = plane_scatter(grad_out, out_rotation)

    d_qkv = []
    for b in range(batches):
        d_key = unrotate(d_kvs[b][:, :kv_half], cosine, sine)
        d_value = d_kvs[b][:, kv_half:].astype(BF16)
        d_qkv.append(jnp.concatenate([d_queries[b], d_key, d_value], 1))
    d_qkv = jnp.concatenate(d_qkv, 0)
    grad_attn = jnp.einsum("rd,rh->dh", normed_a, d_qkv, preferred_element_type=F32)
    d_normed_a = jnp.einsum(
        "rh,dh->rd", d_qkv, attn_w[:, :attn_width], preferred_element_type=F32
    ).reshape(batches, chip_rows, model_width)
    d_normed_a = mine(d_normed_a, 1) + swap_core(others(d_normed_a, 1))
    x_own_f = x_own.astype(F32)
    inverse_a = rms_inverse(x_own_f)
    plain_a = x_own_f * inverse_a
    gain_a_part, input_grad = 0.0, []
    for b in range(batches):
        back_a, gain_part = rms_back(d_normed_a[b], plain_a[b], inverse_a[b], gain_a)
        gain_a_part = gain_a_part + gain_part
        input_grad.append(d_resid[b] + back_a)
    gain_parts = jnp.stack([gain_a_part, sum(gain_m_parts)], 1)
    gain_parts = jnp.pad(gain_parts, ((0, 0), (0, LANES - 2)))
    grad_attn = plane_scatter(jnp.concatenate([grad_attn, gain_parts], 1), 0)

    received = swap_core(others(jnp.concatenate([grad_attn, grad_out], 1), 0))
    grad_attn, grad_out = mine(grad_attn, 0), mine(grad_out, 0)
    edges = [0, query_half, query_half + kv_half, attn_width]
    grad_query, grad_key, grad_value = (
        by_core(grad_attn[:, lo:hi], received[:, lo:hi], 1)
        for lo, hi in zip(edges[:-1], edges[1:])
    )
    grad_gains = grad_attn[:, attn_width:] + received[:, attn_width : attn_width + LANES]
    grad_out = by_core(grad_out, received[:, attn_width + LANES :], 1)
    return (
        jnp.stack(activations)[:, None],
        jnp.stack(input_grad)[:, None],
        grad_gains[:, 0],
        grad_query,
        grad_key,
        grad_value,
        grad_out,
        grad_gains[:, 1],
        grad_gate,
        grad_up,
        grad_down,
    )


def solution(mesh):
    rows = P(None, "seq", "ctx", None)
    spread = P(("seq", "ctx"))
    spread_rows = P(("seq", "ctx"), None)
    return jax.shard_map(
        body,
        mesh=mesh,
        in_specs=(
            rows,
            P(None, "seq"),
            rows,
            spread,
            spread_rows,
            spread_rows,
            spread_rows,
            spread_rows,
            spread,
            P("seq", "ctx"),
            P("seq", "ctx"),
            P("ctx", "seq"),
        ),
        out_specs=(
            rows,
            rows,
            spread,
            spread_rows,
            spread_rows,
            spread_rows,
            spread_rows,
            spread,
            P("seq", "ctx"),
            P("seq", "ctx"),
            P("ctx", "seq"),
        ),
        check_vma=False,
    )
```

```python
import functools
import math

import jax
import jax.numpy as jnp
from jax import lax
from jax.experimental import pallas as pl
from jax.experimental.pallas import tpu as pltpu
from jax.sharding import PartitionSpec as P

HEAD_DIM = 64
LANES = 128
EPSILON = 1e-05
ROPE_BASE = 500000.0
MASKED = -1e30
VMEM_LIMIT = 56 * 1024 * 1024
F32 = jnp.float32
BF16 = jnp.bfloat16


def folded_order(count):
    return list(range(0, count, 2)) + list(range(1, count, 2))[::-1]


def swap_core(array):
    ctx = lax.axis_size("ctx")
    return lax.ppermute(array, "ctx", [(i, i ^ 1) for i in range(ctx)])


def swap_seq(array, bit):
    seq = lax.axis_size("seq")
    return lax.ppermute(array, "seq", [(i, i ^ bit) for i in range(seq)])


def ring_step(array):
    chips = lax.axis_size("ctx") // 2
    order = folded_order(chips)
    pairs = [
        (order[i] * 2 + core, order[(i + 1) % chips] * 2 + core)
        for i in range(chips)
        for core in range(2)
    ]
    return lax.ppermute(array, "ctx", pairs)


def ring_gather(array):
    slots = [array]
    for _ in range(lax.axis_size("ctx") // 2 - 1):
        slots.append(ring_step(slots[-1]))
    return slots


def ring_scatter(parts):
    chips = len(parts)
    total = parts[1 % chips].astype(F32)
    for k in range(2, chips + 1):
        total = ring_step(total.astype(BF16)).astype(F32) + parts[k % chips].astype(F32)
    return total


def cube_gather(array, route):
    seq = lax.axis_size("seq")
    bits = [1 << i for i in range(seq.bit_length() - 1)]
    pieces = {0: array}
    for bit in bits if route == 0 else bits[::-1]:
        pieces.update({r ^ bit: swap_seq(piece, bit) for r, piece in pieces.items()})
    return [pieces[r] for r in range(seq)]


def cube_scatter(chunks, route):
    seq = lax.axis_size("seq")
    bits = [1 << i for i in range(seq.bit_length() - 1)]
    held = dict(enumerate(chunks))
    for bit in bits if route == 0 else bits[::-1]:
        held = {
            r: held[r].astype(F32) + swap_seq(held[r ^ bit].astype(BF16), bit).astype(F32)
            for r in held
            if not r & bit
        }
    return held[0]


def after(array, *others):
    return lax.optimization_barrier((array, *others))[0]


def scaled_frequency():
    half_dim = HEAD_DIM // 2
    base_freq = ROPE_BASE ** (-jnp.arange(half_dim, dtype=F32) * 2.0 / HEAD_DIM)
    wave = 2.0 * math.pi / base_freq
    smooth = (8192.0 / wave - 1.0) / 3.0
    middle = (1.0 - smooth) * base_freq / 32.0 + smooth * base_freq
    return jnp.where(wave < 2048.0, base_freq, jnp.where(wave > 8192.0, base_freq / 32.0, middle))


def rope_tables(positions):
    angles = positions.astype(F32)[:, None] * scaled_frequency()[None, :]
    cosine, sine = jnp.cos(angles), jnp.sin(angles)
    return (
        jnp.concatenate([cosine] * 4, axis=1),
        jnp.concatenate([-sine, sine, -sine, sine], axis=1),
    )


def rotate_lanes(values, cosine, sine):
    lane = lax.broadcasted_iota(jnp.int32, values.shape, 1)
    partner = jnp.where(
        (lane % HEAD_DIM) < HEAD_DIM // 2,
        pltpu.roll(values, LANES - HEAD_DIM // 2, 1),
        pltpu.roll(values, HEAD_DIM // 2, 1),
    )
    return values * cosine + partner * sine


SMEM = pltpu.SMEM
ANYWHERE = pl.BlockSpec(memory_space=pl.ANY)
SCALARS = pl.BlockSpec(memory_space=pltpu.SMEM)
PARAMS = pltpu.CompilerParams(vmem_limit_bytes=VMEM_LIMIT)
NT = (((1,), (1,)), ((), ()))


def cost(flops, nbytes, transcendentals=0):
    return pl.CostEstimate(
        flops=int(flops), bytes_accessed=int(nbytes), transcendentals=int(transcendentals)
    )


def dot(left, right):
    return jnp.dot(left, right, preferred_element_type=F32)


def dot_nt(left, right):
    return lax.dot_general(left, right, NT, preferred_element_type=F32)


def transposed(values):
    return values.astype(F32).T.astype(BF16)


def pack_kernel(kv_half, core_ref, wq, wk, wv, wo, gains, mine, other):
    def fill(out, which):
        at = 0
        half = wq.shape[1] // 2
        out[:, at : at + half] = wq[:, which * half : (which + 1) * half]
        at += half
        for i in range(kv_half // LANES):
            for source in (wk, wv):
                lo = which * kv_half + i * LANES
                out[:, at : at + LANES] = source[:, lo : lo + LANES]
                at += LANES
        out[:, at : at + LANES] = gains[...]
        at += LANES
        half = wo.shape[1] // 2
        out[:, at : at + half] = wo[:, which * half : (which + 1) * half]

    for core in range(2):

        @pl.when(core_ref[0] == core)
        def _():
            fill(mine, core)
            fill(other, 1 - core)


def pack(core, wq, wk, wv, wo, gains):
    rows = wq.shape[0]
    width = (wq.shape[1] + wk.shape[1] + wv.shape[1] + wo.shape[1]) // 2 + LANES
    shape = jax.ShapeDtypeStruct((rows, width), BF16)
    whole = [pl.BlockSpec(memory_space=pltpu.VMEM)] * 5
    return pl.pallas_call(
        functools.partial(pack_kernel, wk.shape[1] // 2),
        in_specs=[SCALARS] + whole,
        out_shape=[shape, shape],
        compiler_params=PARAMS,
        cost_estimate=cost(0, 8 * rows * width),
    )(core, wq, wk, wv, wo, gains)


def stack_kernel(cut, core_ref, mine, other, left, right):
    rows = mine.shape[0]
    for core in range(2):

        @pl.when(core_ref[0] == core)
        def _():
            for source, at in ((mine, core), (other, 1 - core)):
                left[at * rows : (at + 1) * rows] = source[:, :cut]
                right[at * rows : (at + 1) * rows] = source[:, cut:]


def stack_pieces(core, mine, other, cut):
    rows, width = mine.shape
    return pl.pallas_call(
        functools.partial(stack_kernel, cut),
        in_specs=[SCALARS] + [pl.BlockSpec(memory_space=pltpu.VMEM)] * 2,
        out_shape=[
            jax.ShapeDtypeStruct((2 * rows, cut), BF16),
            jax.ShapeDtypeStruct((2 * rows, width - cut), BF16),
        ],
        compiler_params=PARAMS,
        cost_estimate=cost(0, 8 * rows * width),
    )(core, mine, other)


def qkv_kernel(count, batches, query_blocks, *refs):
    core_ref, starts, x_own, x_oth, cos_ref, sin_ref = refs[:6]
    pieces = refs[6 : 6 + count]
    q_ref, kv_ref, normed, gains_ref, w_out, w, sems, out_sem = refs[6 + count :]
    step = pl.program_id(0)
    rows, depth = normed.shape
    slots = rows // (2 * batches)

    def arriving(i):
        start = pl.multiple_of(starts[i], 16)
        return pltpu.make_async_copy(
            pieces[i], w.at[pl.ds(start, pieces[i].shape[0])], sems.at[i]
        )

    @pl.when(step == 0)
    def _():
        for i in range(count):
            arriving(i).start()
        for i in range(count):
            arriving(i).wait()
        pltpu.make_async_copy(w, w_out, out_sem.at[0]).start()
        table = w[:, w.shape[1] - LANES :].astype(F32).T
        gains_ref[...] = table[:8]
        for source, which in ((x_own, core_ref[0]), (x_oth, 1 - core_ref[0])):
            for b in range(batches):
                x = source[b * slots : (b + 1) * slots].astype(F32)
                inverse = lax.rsqrt(jnp.mean(x * x, axis=-1, keepdims=True) + EPSILON)
                at = pl.multiple_of((2 * b + which) * slots, slots)
                normed[pl.ds(at, slots)] = (x * inverse * table[:1]).astype(BF16)

    block = 2 * LANES
    at = pl.multiple_of(step * block, block)
    raw = dot(normed[...], w[:, pl.ds(at, block)])
    left = rotate_lanes(raw[:, :LANES], cos_ref[...], sin_ref[...])

    @pl.when(step < query_blocks)
    def _():
        right = rotate_lanes(raw[:, LANES:], cos_ref[...], sin_ref[...])
        scale = 1.0 / math.sqrt(HEAD_DIM)
        q_ref[:, :LANES] = (left * scale).astype(BF16)
        q_ref[:, LANES:] = (right * scale).astype(BF16)

    @pl.when(step >= query_blocks)
    def _():
        kv_ref[:, :LANES] = left.astype(BF16)
        kv_ref[:, LANES:] = raw[:, LANES:].astype(BF16)

    @pl.when(step == pl.num_programs(0) - 1)
    def _():
        pltpu.make_async_copy(w, w_out, out_sem.at[0]).wait()


def project_qkv(core, starts, x_own, x_oth, cosine, sine, pieces, batches, query_width, kv_width):
    rows, depth = 2 * x_own.shape[0], x_own.shape[1]
    block = 2 * LANES
    query_blocks = query_width // block
    width = pieces[0].shape[1]
    count = len(pieces)

    def whole(shape):
        return pl.BlockSpec(shape, lambda j: (0, 0))

    return pl.pallas_call(
        functools.partial(qkv_kernel, count, batches, query_blocks),
        grid=((query_width + 2 * kv_width) // block,),
        in_specs=[SCALARS, SCALARS, whole(x_own.shape), whole(x_own.shape)]
        + [whole((rows, LANES))] * 2
        + [ANYWHERE] * count,
        out_specs=[
            pl.BlockSpec((rows, block), lambda j: (0, jnp.minimum(j, query_blocks - 1))),
            pl.BlockSpec((rows, block), lambda j: (0, jnp.maximum(j - query_blocks, 0))),
            whole((rows, depth)),
            whole((8, depth)),
            ANYWHERE,
        ],
        out_shape=[
            jax.ShapeDtypeStruct((rows, query_width), BF16),
            jax.ShapeDtypeStruct((rows, 2 * kv_width), BF16),
            jax.ShapeDtypeStruct((rows, depth), BF16),
            jax.ShapeDtypeStruct((8, depth), F32),
            jax.ShapeDtypeStruct((depth, width), BF16),
        ],
        scratch_shapes=[
            pltpu.VMEM((depth, width), BF16),
            pltpu.SemaphoreType.DMA((count,)),
            pltpu.SemaphoreType.DMA((1,)),
        ],
        compiler_params=PARAMS,
        cost_estimate=cost(2 * rows * depth * width, 4 * rows * depth + 4 * depth * width),
    )(core, starts, x_own, x_oth, cosine, sine, *pieces)


def set_bias(limit_ref, kpos_ref, qpos_ref, bias):
    @pl.when(pl.program_id(1) == 0)
    def _():
        limit = limit_ref[pl.program_id(0)]
        allowed = (kpos_ref[...] <= qpos_ref[...]) & (kpos_ref[...] < limit)
        bias[...] = jnp.where(allowed, 0.0, MASKED)


def attend_kernel(chips, limit_ref, kpos_ref, qpos_ref, q_ref, *refs):
    slots, (out_ref, lse_ref, bias) = refs[:chips], refs[chips:]
    set_bias(limit_ref, kpos_ref, qpos_ref, bias)
    heads = q_ref.shape[1] // HEAD_DIM
    kv = jnp.concatenate([slot[...] for slot in slots], axis=0)
    q_t = transposed(q_ref[...])
    v_t = transposed(kv[:, LANES:])
    outs = []
    for h in range(heads):
        a = h * 2 // heads
        k_h = kv[:, a * HEAD_DIM : (a + 1) * HEAD_DIM]
        scores = dot(k_h, q_t[h * HEAD_DIM : (h + 1) * HEAD_DIM]) + bias[...]
        top = jnp.max(scores, axis=0, keepdims=True)
        shifted = jnp.exp(scores - top)
        total = jnp.sum(shifted, axis=0, keepdims=True)
        out_t = dot(v_t[a * HEAD_DIM : (a + 1) * HEAD_DIM], shifted.astype(BF16))
        outs.append(out_t / total)
        lse_ref[h : h + 1, :] = top + jnp.log(total)
    out_ref[...] = jnp.concatenate(outs, axis=0).T.astype(BF16)


def attention_specs(batches, chips, rows, keys, width, heads, pairs):
    def at(shape):
        return pl.BlockSpec(shape, lambda b, i, n: (b, i))

    return (
        [
            pl.BlockSpec((keys, 1), lambda b, i, n: (0, 0)),
            pl.BlockSpec((1, rows), lambda b, i, n: (0, 0)),
            at((rows, width)),
        ]
        + [at((rows, 2 * LANES))] * chips,
        at((rows, width)),
        pl.BlockSpec((heads, rows), lambda b, i, n: (b * pairs + i, 0)),
    )


def attend(q, kv_slots, limits, kpos, qpos):
    rows, keys, batches, chips = qpos.shape[1], kpos.shape[0], limits.shape[0], len(kv_slots)
    pairs = kv_slots[0].shape[1] // (2 * LANES)
    width = q.shape[1] // pairs
    heads = width // HEAD_DIM
    ins, out, lse = attention_specs(batches, chips, rows, keys, width, heads, pairs)
    return pl.pallas_call(
        functools.partial(attend_kernel, chips),
        grid_spec=pltpu.PrefetchScalarGridSpec(
            num_scalar_prefetch=1,
            grid=(batches, pairs),
            in_specs=ins,
            out_specs=[out, lse],
            scratch_shapes=[pltpu.VMEM((keys, rows), F32)],
        ),
        out_shape=[
            jax.ShapeDtypeStruct(q.shape, BF16),
            jax.ShapeDtypeStruct((batches * pairs * heads, rows), F32),
        ],
        compiler_params=PARAMS,
        cost_estimate=cost(
            16 * batches * rows * keys * q.shape[1],
            4 * q.size + 2 * chips * kv_slots[0].size,
            batches * rows * keys * q.shape[1] // HEAD_DIM,
        ),
    )(limits, kpos, qpos, q, *kv_slots)


def attend_back_kernel(chips, limit_ref, kpos_ref, qpos_ref, q_ref, *refs):
    slots = refs[:chips]
    do_mine, do_other, lse_ref, cos_ref, sin_ref, dq_ref = refs[chips : chips + 6]
    d_slots, bias = refs[chips + 6 : 2 * chips + 6], refs[2 * chips + 6]
    set_bias(limit_ref, kpos_ref, qpos_ref, bias)
    rows, width = q_ref.shape
    heads = width // HEAD_DIM
    per_kv = heads // 2
    kv = jnp.concatenate([slot[...] for slot in slots], axis=0)
    d_out = (do_mine[...] + do_other[...].astype(F32)).astype(BF16)
    q_t = transposed(q_ref[...])
    do_t = transposed(d_out)
    k_t = transposed(kv[:, :LANES])
    lane = lax.broadcasted_iota(jnp.int32, (kv.shape[0], LANES), 1)
    d_queries = []
    d_keys, d_values = [], []
    for a in range(2):
        k_h = kv[:, a * HEAD_DIM : (a + 1) * HEAD_DIM]
        v_h = kv[:, LANES + a * HEAD_DIM : LANES + (a + 1) * HEAD_DIM]
        dk_sum, dv_sum = [None, None], [None, None]
        for g in range(per_kv):
            h = a * per_kv + g
            head = slice(h * HEAD_DIM, (h + 1) * HEAD_DIM)
            pair = slice((h // 2) * LANES, (h // 2 + 1) * LANES)
            scores = dot(k_h, q_t[head]) + bias[...]
            probs = jnp.exp(scores - lse_ref[h : h + 1, :])
            d_probs = dot(v_h, do_t[head])
            mean = jnp.sum(d_probs * probs, axis=0, keepdims=True)
            d_scores = (probs * (d_probs - mean)).astype(BF16)
            d_queries.append(dot(k_t[a * HEAD_DIM : (a + 1) * HEAD_DIM], d_scores))
            dk_term = dot(d_scores, q_ref[:, pair])
            dv_term = dot(probs.astype(BF16), d_out[:, pair])
            e = h % 2
            dk_sum[e] = dk_term if dk_sum[e] is None else dk_sum[e] + dk_term
            dv_sum[e] = dv_term if dv_sum[e] is None else dv_sum[e] + dv_term
        for sums, kept in ((dk_sum, d_keys), (dv_sum, d_values)):
            mixed = jnp.where(lane < HEAD_DIM, sums[0], sums[1])
            kept.append(mixed + pltpu.roll(mixed, HEAD_DIM, 1))
    d_key = jnp.where(lane < HEAD_DIM, d_keys[0], d_keys[1])
    d_value = jnp.where(lane < HEAD_DIM, d_values[0], d_values[1])
    for k, d_slot in enumerate(d_slots):
        d_slot[:, :LANES] = d_key[k * rows : (k + 1) * rows].astype(BF16)
        d_slot[:, LANES:] = d_value[k * rows : (k + 1) * rows].astype(BF16)
    d_query = jnp.concatenate(d_queries, axis=0).T
    for at in range(width // LANES):
        cut = slice(at * LANES, (at + 1) * LANES)
        turned = rotate_lanes(d_query[:, cut], cos_ref[...], -sin_ref[...])
        dq_ref[:, cut] = (turned / math.sqrt(HEAD_DIM)).astype(BF16)


def attend_back(q, kv_slots, do_mine, do_other, lse, limits, kpos, qpos, cosine, sine):
    rows, keys, batches, chips = qpos.shape[1], kpos.shape[0], limits.shape[0], len(kv_slots)
    pairs = kv_slots[0].shape[1] // (2 * LANES)
    width = q.shape[1] // pairs
    heads = width // HEAD_DIM
    ins, out, lse_spec = attention_specs(batches, chips, rows, keys, width, heads, pairs)
    table = pl.BlockSpec((rows, LANES), lambda b, i, n: (0, 0))
    return pl.pallas_call(
        functools.partial(attend_back_kernel, chips),
        grid_spec=pltpu.PrefetchScalarGridSpec(
            num_scalar_prefetch=1,
            grid=(batches, pairs),
            in_specs=ins + [out, out, lse_spec, table, table],
            out_specs=[out] + ins[3 : 3 + chips],
            scratch_shapes=[pltpu.VMEM((keys, rows), F32)],
        ),
        out_shape=[jax.ShapeDtypeStruct(q.shape, BF16)]
        + [jax.ShapeDtypeStruct(slot.shape, BF16) for slot in kv_slots],
        compiler_params=PARAMS,
        cost_estimate=cost(
            40 * batches * rows * keys * q.shape[1],
            10 * q.size + 4 * chips * kv_slots[0].size,
            batches * rows * keys * q.shape[1] // HEAD_DIM,
        ),
    )(limits, kpos, qpos, q, *kv_slots, do_mine, do_other, lse, cosine, sine)


def unrotate_kernel(last_ref, own_ref, cos_ref, sin_ref, out_ref):
    total = last_ref[...].astype(F32) + own_ref[...].astype(F32)
    for at in range(total.shape[1] // LANES):
        cut = slice(at * LANES, (at + 1) * LANES)
        part = total[:, cut]
        if at % 2 == 0:
            part = rotate_lanes(part, cos_ref[...], -sin_ref[...])
        out_ref[:, cut] = part.astype(BF16)


def unrotate(last, own, cosine, sine):
    return pl.pallas_call(
        unrotate_kernel,
        out_shape=jax.ShapeDtypeStruct(own.shape, BF16),
        compiler_params=PARAMS,
        cost_estimate=cost(0, 6 * own.size),
    )(last, own, cosine, sine)


def split_rows(batches, core_ref, acc, own, other):
    slots = acc.shape[0] // (2 * batches)
    for out, which in ((own, core_ref[0]), (other, 1 - core_ref[0])):
        for b in range(batches):
            at = pl.multiple_of((2 * b + which) * slots, slots)
            out[b * slots : (b + 1) * slots] = acc[pl.ds(at, slots)].astype(out.dtype)


def out_kernel(batches, chips, core_ref, starts, o_mine, o_other, *refs):
    count = len(refs) - 6
    pieces = refs[:count]
    own, other, w_out, w, acc, sems = refs[count:]
    shard = pieces[0].shape[0] // chips
    half = o_mine.shape[1]
    arriving = [
        pltpu.make_async_copy(
            pieces[r].at[pl.ds(k * shard, shard)],
            w.at[pl.ds(pl.multiple_of(starts[r * chips + k], 16), shard)],
            sems.at[r * chips + k],
        )
        for r in range(count)
        for k in range(chips)
    ]
    for copy in arriving:
        copy.start()
    for copy in arriving:
        copy.wait()
    leaving = pltpu.make_async_copy(w, w_out, sems.at[count * chips])
    leaving.start()
    block = 2 * LANES

    @pl.loop(0, w.shape[1] // block)
    def _(j):
        cut = pl.ds(pl.multiple_of(j * block, block), block)
        acc[:, cut] = dot(o_mine[...], w[:half, cut]) + dot(o_other[...], w[half:, cut])

    split_rows(batches, core_ref, acc, own, other)
    leaving.wait()


def project_out(core, starts, o_mine, o_other, pieces, batches, chips):
    rows, half = o_mine.shape
    width = pieces[0].shape[1]
    count = len(pieces)
    vmem = pl.BlockSpec(memory_space=pltpu.VMEM)
    part = jax.ShapeDtypeStruct((rows // 2, width), F32)
    return pl.pallas_call(
        functools.partial(out_kernel, batches, chips),
        in_specs=[SCALARS, SCALARS, vmem, vmem] + [ANYWHERE] * count,
        out_specs=[vmem, vmem, ANYWHERE],
        out_shape=[part, part, jax.ShapeDtypeStruct((2 * half, width), BF16)],
        scratch_shapes=[
            pltpu.VMEM((2 * half, width), BF16),
            pltpu.VMEM((rows, width), F32),
            pltpu.SemaphoreType.DMA((count * chips + 1,)),
        ],
        compiler_params=PARAMS,
        cost_estimate=cost(4 * rows * half * width, 8 * half * width + 12 * rows * width),
    )(core, starts, o_mine, o_other, *pieces)


def mlp_kernel(seq, filled, *refs):
    x_mine, x_other, d_mine, d_other = refs[:4]
    gates, ups, downs = (refs[4 + i * seq : 4 + (i + 1) * seq] for i in range(3))
    refs = refs[4 + 3 * seq + filled :]
    xs, ds = refs[:seq], refs[seq : 2 * seq]
    hidden_ref, d_gate_ref, d_up_ref = refs[2 * seq : 2 * seq + 3]
    rows = x_mine.shape[0]
    block = x_mine.shape[1] // seq

    @pl.when(pl.program_id(0) == 0)
    def _():
        for r in range(seq):
            cut = slice(r * block, (r + 1) * block)
            xs[r][:rows] = x_mine[:, cut]
            xs[r][rows:] = x_other[:, cut]
            ds[r][:rows] = d_mine[:, cut]
            ds[r][rows:] = d_other[:, cut]

    gate_val = sum(dot(xs[r][...], gates[r][...]) for r in range(seq))
    up_val = sum(dot(xs[r][...], ups[r][...]) for r in range(seq))
    d_hidden = sum(dot_nt(ds[r][...], downs[r][...]) for r in range(seq))
    sigmoid_g = 1.0 / (1.0 + jnp.exp(-gate_val))
    activated = gate_val * sigmoid_g
    slope = sigmoid_g * (1.0 + gate_val * (1.0 - sigmoid_g))
    hidden_ref[...] = (activated * up_val).astype(BF16)
    d_gate_ref[...] = (d_hidden * up_val * slope).astype(BF16)
    d_up_ref[...] = (d_hidden * activated).astype(BF16)


def mlp_slot(slot, slots, x_mine, x_other, d_mine, d_other, gates, ups, downs, kept):
    seq = len(gates)
    rows, width = x_mine.shape
    block = width // seq
    hidden_width = gates[0].shape[1]
    tile = 2 * LANES

    def whole(shape):
        return pl.BlockSpec(shape, lambda j: (0, 0))

    wide = [jax.ShapeDtypeStruct((2 * rows * slots, block), BF16)] * (2 * seq)
    narrow = [jax.ShapeDtypeStruct((2 * rows * slots, hidden_width), BF16)] * 3
    filled = 0 if kept is None else 2 * seq + 3
    first = 4 + 3 * seq
    return pl.pallas_call(
        functools.partial(mlp_kernel, seq, filled),
        grid=(hidden_width // tile,),
        in_specs=[whole((rows, width))] * 4
        + [pl.BlockSpec((block, tile), lambda j: (0, j))] * (2 * seq)
        + [pl.BlockSpec((tile, block), lambda j: (j, 0))] * seq
        + [ANYWHERE] * filled,
        out_specs=[pl.BlockSpec((2 * rows, block), lambda j: (slot, 0))] * (2 * seq)
        + [pl.BlockSpec((2 * rows, tile), lambda j: (slot, j))] * 3,
        out_shape=wide + narrow,
        input_output_aliases={first + i: i for i in range(filled)},
        compiler_params=PARAMS,
        cost_estimate=cost(
            12 * rows * width * hidden_width,
            6 * width * hidden_width + 24 * rows * width,
            2 * rows * hidden_width,
        ),
    )(x_mine, x_other, d_mine, d_other, *gates, *ups, *downs, *([] if kept is None else kept))


def mlp_back_kernel(seq, hidden, d_gate, d_up, *refs):
    weights = refs[: 3 * seq]
    back_mine, back_other, out_mine, out_other = refs[3 * seq : 3 * seq + 4]
    held, sems = refs[3 * seq + 4 : -1], refs[-1]
    rows = back_mine.shape[0]
    block = back_mine.shape[1] // seq
    copies = [pltpu.make_async_copy(weights[i], held[i], sems.at[i]) for i in range(3 * seq)]
    for r in range(seq):
        for i in range(3):
            copies[i * seq + r].start()
    for r in range(seq):
        cut = slice(r * block, (r + 1) * block)
        for i in range(3):
            copies[i * seq + r].wait()
        back = dot_nt(d_gate[...], held[r][...]) + dot_nt(d_up[...], held[seq + r][...])
        back_mine[:, cut] = back[:rows].astype(BF16)
        back_other[:, cut] = back[rows:].astype(BF16)
        out = dot(hidden[...], held[2 * seq + r][...])
        out_mine[:, cut] = out[:rows].astype(BF16)
        out_other[:, cut] = out[rows:].astype(BF16)


def mlp_back(slot, slots, hidden, d_gate, d_up, gates, ups, downs):
    seq = len(gates)
    rows, width = hidden.shape[0] // (2 * slots), gates[0].shape[0] * seq
    hidden_width = hidden.shape[1]
    weights = [*gates, *ups, *downs]
    return pl.pallas_call(
        functools.partial(mlp_back_kernel, seq),
        grid=(1,),
        in_specs=[pl.BlockSpec((2 * rows, hidden_width), lambda j: (slot, 0))] * 3
        + [ANYWHERE] * (3 * seq),
        out_specs=[pl.BlockSpec((rows, width), lambda j: (0, 0))] * 4,
        out_shape=[jax.ShapeDtypeStruct((rows, width), BF16)] * 4,
        scratch_shapes=[pltpu.VMEM(w.shape, BF16) for w in weights]
        + [pltpu.SemaphoreType.DMA((3 * seq,))],
        compiler_params=PARAMS,
        cost_estimate=cost(
            12 * rows * width * hidden_width, 6 * width * hidden_width + 14 * rows * width
        ),
    )(hidden, d_gate, d_up, *weights)


def d_attended_kernel(batches, other_blocks, core_ref, d_own, d_oth, w_ref, mine, other, d_rows):
    step = pl.program_id(0)
    slots = d_own.shape[0] // batches

    @pl.when(step == 0)
    def _():
        for source, which in ((d_own, core_ref[0]), (d_oth, 1 - core_ref[0])):
            for b in range(batches):
                at = pl.multiple_of((2 * b + which) * slots, slots)
                d_rows[pl.ds(at, slots)] = source[b * slots : (b + 1) * slots]

    term = dot_nt(d_rows[...], w_ref[...])

    @pl.when(step < other_blocks)
    def _():
        other[...] = term.astype(BF16)

    @pl.when(step >= other_blocks)
    def _():
        mine[...] = term


def d_attended(core, d_own, d_oth, w, batches):
    rows, width = 2 * d_own.shape[0], d_own.shape[1]
    heads_width = w.shape[0]
    block = 2 * LANES
    blocks = heads_width // 2 // block

    def whole(shape):
        return pl.BlockSpec(shape, lambda j: (0, 0))

    return pl.pallas_call(
        functools.partial(d_attended_kernel, batches, blocks),
        grid=(2 * blocks,),
        in_specs=[
            SCALARS,
            whole(d_own.shape),
            whole(d_own.shape),
            pl.BlockSpec((block, width), lambda j: ((j + blocks) % (2 * blocks), 0)),
        ],
        out_specs=[
            pl.BlockSpec((rows, block), lambda j: (0, jnp.maximum(j - blocks, 0))),
            pl.BlockSpec((rows, block), lambda j: (0, jnp.minimum(j, blocks - 1))),
            whole((rows, width)),
        ],
        out_shape=[
            jax.ShapeDtypeStruct((rows, heads_width // 2), F32),
            jax.ShapeDtypeStruct((rows, heads_width // 2), BF16),
            jax.ShapeDtypeStruct((rows, width), BF16),
        ],
        compiler_params=PARAMS,
        cost_estimate=cost(
            2 * rows * width * heads_width, 2 * width * heads_width + 6 * rows * heads_width
        ),
    )(core, d_own, d_oth, w)


def grad_kernel(count, parts, chips, starts, *refs):
    sources, right, outs, turned = refs[:count], refs[count], refs[count + 1 : -1], refs[-1]
    shard = turned.shape[0] // (parts * chips)
    at = 0
    for source in sources:
        for lo in range(0, source.shape[1], 4 * LANES):
            turned[at : at + 4 * LANES] = transposed(source[:, lo : lo + 4 * LANES])
            at += 4 * LANES
    for r in range(parts):
        left = jnp.concatenate(
            [
                turned[pl.ds(pl.multiple_of(starts[r * chips + k], 16), shard)]
                for k in range(chips)
            ],
            axis=0,
        )
        outs[r][...] = dot(left, right[...]).astype(BF16)


def grad_chunks(starts, sources, right, parts, chips):
    rows = right.shape[0]
    depth = sum(source.shape[1] for source in sources)
    shape = jax.ShapeDtypeStruct((depth // parts, right.shape[1]), BF16)
    vmem = pl.BlockSpec(memory_space=pltpu.VMEM)
    return pl.pallas_call(
        functools.partial(grad_kernel, len(sources), parts, chips),
        in_specs=[SCALARS] + [vmem] * (len(sources) + 1),
        out_shape=[shape] * parts,
        scratch_shapes=[pltpu.VMEM((depth, rows), BF16)],
        compiler_params=PARAMS,
        cost_estimate=cost(
            2 * rows * depth * right.shape[1], 2 * rows * depth + 2 * depth * right.shape[1]
        ),
    )(starts, *sources, right)


def d_normed_kernel(batches, core_ref, dq_ref, dkv_ref, w_ref, own, other, acc):
    width = dq_ref.shape[1]
    acc[...] = dot_nt(dq_ref[...], w_ref[:, :width]) + dot_nt(
        dkv_ref[...], w_ref[:, width : width + dkv_ref.shape[1]]
    )
    split_rows(batches, core_ref, acc, own, other)


def d_normed_rows(core, dq, dkv, w, batches):
    rows = dq.shape[0]
    depth, width = w.shape
    block = 4 * LANES

    def whole(shape):
        return pl.BlockSpec(shape, lambda j: (0, 0))

    part = pl.BlockSpec((rows // 2, block), lambda j: (0, j))
    return pl.pallas_call(
        functools.partial(d_normed_kernel, batches),
        grid=(depth // block,),
        in_specs=[
            SCALARS,
            whole(dq.shape),
            whole(dkv.shape),
            pl.BlockSpec((block, width), lambda j: (j, 0)),
        ],
        out_specs=[part, part],
        out_shape=[jax.ShapeDtypeStruct((rows // 2, depth), F32)] * 2,
        scratch_shapes=[pltpu.VMEM((rows, block), F32)],
        compiler_params=PARAMS,
        cost_estimate=cost(2 * rows * depth * width, 2 * depth * width + 4 * rows * depth),
    )(core, dq, dkv, w)


def rms_inverse(values):
    return lax.rsqrt(jnp.mean(values * values, axis=-1, keepdims=True) + EPSILON)


def rms_back(grad_in, plain, inverse, gain):
    scaled = grad_in * gain
    back = inverse * (scaled - plain * jnp.mean(scaled * plain, axis=-1, keepdims=True))
    return (back, jnp.sum(grad_in * plain, axis=0, keepdims=True))


def body(
    tokens,
    lengths,
    cotangent,
    attn_gain,
    w_query,
    w_key,
    w_value,
    w_out,
    mlp_gain,
    w_gate,
    w_up,
    w_down,
):
    batches, _, slot_count, model_width = tokens.shape
    seq_size, ctx_size = lax.axis_size("seq"), lax.axis_size("ctx")
    chips = ctx_size // 2
    seq_at, ctx_at = lax.axis_index("seq"), lax.axis_index("ctx")
    chip_at, core = ctx_at // 2, ctx_at % 2
    core_ref = core.reshape(1).astype(jnp.int32)
    order = folded_order(chips)
    shard = w_query.shape[0]
    query_half, kv_half = w_query.shape[1] // 2, w_key.shape[1] // 2
    chip_rows = 2 * slot_count
    own_rows = batches * slot_count
    attn_width = query_half + 2 * kv_half
    limits = lengths[:, 0]

    def chip_back(k):
        index = jnp.int32(0)
        for place, chip in enumerate(order):
            index = jnp.where(chip_at == chip, order[(place - k) % chips], index)
        return index

    slot_chip = jnp.stack([chip_back(k) for k in range(chips)])
    rank = (seq_at ^ jnp.arange(seq_size))[:, None] * chips + slot_chip[None, :]
    starts = (rank * (2 * shard)).reshape(-1).astype(jnp.int32)
    out_starts = (starts + core * query_half) % (2 * query_half)

    def half(array, which, axis):
        size = array.shape[axis] // 2
        return lax.dynamic_slice_in_dim(array, which * size, size, axis)

    def mine(array, axis):
        return half(array, core, axis)

    def others(array, axis):
        return half(array, 1 - core, axis)

    def by_core(own, other, axis):
        return jnp.where(
            core == 0,
            jnp.concatenate([own, other], axis),
            jnp.concatenate([other, own], axis),
        )

    def turn_blocks(array):
        block = array.shape[-1] // seq_size
        bit = 1
        while bit < seq_size:
            turned = jnp.concatenate(
                [
                    array[..., (r ^ bit) * block : ((r ^ bit) + 1) * block]
                    for r in range(seq_size)
                ],
                axis=-1,
            )
            array = jnp.where((seq_at & bit) != 0, turned, array)
            bit *= 2
        return array

    gains = jnp.concatenate(
        [attn_gain[:, None], mlp_gain[:, None], jnp.zeros((shard, LANES - 2), BF16)], axis=1
    )
    packed, to_other = pack(core_ref, w_query, w_key, w_value, w_out, gains)
    piece_a, piece_o = stack_pieces(
        core_ref, packed, swap_core(to_other), attn_width + LANES
    )
    ring_a = ring_gather(piece_a)
    cubes_a = [cube_gather(slot, k % 2) for k, slot in enumerate(ring_a)]
    x_own = tokens.reshape(own_rows, model_width)
    x_oth = swap_core(x_own)
    ring_o = jnp.concatenate(ring_gather(after(piece_o, ring_a[-1])), 0)
    cube_o = cube_gather(after(ring_o, cubes_a[-1][1], cubes_a[-1][2]), 0)
    gates = cube_gather(after(w_gate, cube_o[1], cube_o[2]), 1)
    ups = cube_gather(after(w_up, gates[1], gates[2]), 0)
    downs = cube_gather(after(w_down, ups[1], ups[2]), 1)

    q_positions = chip_at * chip_rows + jnp.arange(chip_rows)
    cosine, sine = rope_tables(q_positions)
    cosine_all, sine_all = jnp.tile(cosine, (batches, 1)), jnp.tile(sine, (batches, 1))
    qpos = q_positions[None, :]
    kpos = (slot_chip[:, None] * chip_rows + jnp.arange(chip_rows)[None, :]).reshape(-1, 1)
    own_pos = ctx_at * slot_count + jnp.arange(slot_count)
    valid = (own_pos[None, :] < limits[:, None]).astype(F32).reshape(own_rows, 1)
    d_output = cotangent.reshape(own_rows, model_width).astype(F32) * valid
    d_turned = turn_blocks(d_output.astype(BF16))

    flat_a = [cubes_a[k][r] for r in range(seq_size) for k in range(chips)]
    q, kv, normed_a, gain_rows, attn_w = project_qkv(
        core_ref, starts, x_own, x_oth, cosine_all, sine_all, flat_a, batches, query_half, kv_half
    )
    gain_a, gain_m = gain_rows[0:1], gain_rows[1:2]
    kv_slots = ring_gather(kv)
    d_slots = ring_gather(after(d_turned, ring_o))
    d_pairs = [(slot, swap_core(slot)) for slot in d_slots]
    attended, lse = attend(q, kv_slots, limits, kpos, qpos)
    attended_oth = swap_core(attended)
    branch, branch_oth, out_w = project_out(
        core_ref, out_starts, attended, attended_oth, cube_o, batches, chips
    )

    residual = x_own.astype(F32) + by_core(branch, swap_core(branch_oth), 1)
    inverse_m = rms_inverse(residual)
    x_slots = ring_gather(turn_blocks((residual * inverse_m * gain_m).astype(BF16)))
    kept = None
    back_parts, out_parts = [None] * chips, [None] * chips
    for k in range(chips):
        kept = mlp_slot(
            k, chips, x_slots[k], swap_core(x_slots[k]), *d_pairs[k], gates, ups, downs, kept
        )
        parts = mlp_back(k, chips, *kept[2 * seq_size :], gates, ups, downs)
        back_parts[k] = (parts[0], swap_core(parts[1]))
        out_parts[k] = (parts[2], parts[3])
    d_normed = turn_blocks(
        ring_scatter([own.astype(F32) + oth.astype(F32) for own, oth in back_parts])
    )
    xs, ds = kept[:seq_size], kept[seq_size : 2 * seq_size]
    hidden, d_gate, d_up = kept[2 * seq_size :]

    def rows_product(left, right):
        return jnp.einsum("ri,rj->ij", left, right, preferred_element_type=F32).astype(BF16)

    grad_gate = cube_scatter([rows_product(x, d_gate) for x in xs], 0)
    grad_up = cube_scatter([rows_product(x, d_up) for x in xs], 1)
    grad_down = cube_scatter([rows_product(hidden, d) for d in ds], 0)

    plain_m = residual * inverse_m
    back_m, gain_m_part = rms_back(d_normed, plain_m, inverse_m, gain_m)
    d_resid = d_output + back_m
    d_low = d_resid.astype(BF16)
    do_mine, do_other, d_half = d_attended(
        core_ref, mine(d_low, 1), swap_core(others(d_low, 1)), out_w, batches
    )
    d_query, *d_kv_slots = attend_back(
        q, kv_slots, do_mine, swap_core(do_other), lse, limits, kpos, qpos, cosine, sine
    )

    def owner_sum(chunks, route):
        summed = cube_scatter(chunks, route)
        rows = 2 * shard
        return ring_scatter([summed[k * rows : (k + 1) * rows] for k in range(chips)])

    def own_shard(summed, lanes):
        received = swap_core(others(summed, 0))
        kept_rows = mine(summed, 0)
        edges = [sum(lanes[:i]) for i in range(len(lanes) + 1)]
        return [
            by_core(kept_rows[:, lo:hi], received[:, lo:hi], 1)
            for lo, hi in zip(edges[:-1], edges[1:])
        ]

    grad_out = owner_sum(
        grad_chunks(out_starts, [attended, attended_oth], d_half, seq_size, chips), 1
    )
    (grad_out,) = own_shard(grad_out, [model_width // 2])
    grad_query = owner_sum(grad_chunks(starts, [normed_a], d_query, seq_size, chips), 0)
    (grad_query,) = own_shard(grad_query, [query_half])
    last = d_kv_slots[1 % chips]
    for k in range(2, chips):
        last = (ring_step(last).astype(F32) + d_kv_slots[k].astype(F32)).astype(BF16)
    d_kv = unrotate(ring_step(last), d_kv_slots[0], cosine_all, sine_all)
    grad_kv = owner_sum(grad_chunks(starts, [normed_a], d_kv, seq_size, chips), 1)
    kv_parts = own_shard(grad_kv, [LANES] * (2 * kv_half // LANES))
    grad_kv = [
        jnp.concatenate(
            [part[:, :LANES] for part in kv_parts[i::2]]
            + [part[:, LANES:] for part in kv_parts[i::2]],
            axis=1,
        )
        for i in range(2)
    ]
    d_normed_a, d_normed_oth = d_normed_rows(core_ref, d_query, d_kv, attn_w, batches)
    d_normed_a = d_normed_a + swap_core(d_normed_oth)
    x_own_f = x_own.astype(F32)
    inverse_a = rms_inverse(x_own_f)
    back_a, gain_a_part = rms_back(d_normed_a, x_own_f * inverse_a, inverse_a, gain_a)
    input_grad = d_resid + back_a
    gain_sum = jnp.concatenate([gain_a_part, gain_m_part], 0)
    gain_sum = gain_sum + swap_core(gain_sum)
    bit = 1
    while bit < seq_size:
        gain_sum = gain_sum + swap_seq(gain_sum, bit)
        bit *= 2
    passing = gain_sum
    for _ in range(chips - 1):
        passing = ring_step(passing)
        gain_sum = gain_sum + passing
    gain_sum = lax.dynamic_slice_in_dim(gain_sum, (seq_at * ctx_size + ctx_at) * shard, shard, 1)

    out_parts = [(own, swap_core(oth)) for own, oth in out_parts]
    branch_m = ring_scatter([own.astype(F32) + oth.astype(F32) for own, oth in out_parts])
    activations = (residual + turn_blocks(branch_m)).astype(BF16)
    return (
        activations.reshape(tokens.shape),
        input_grad.reshape(tokens.shape),
        gain_sum[0],
        grad_query,
        grad_kv[0],
        grad_kv[1],
        grad_out,
        gain_sum[1],
        grad_gate,
        grad_up,
        grad_down,
    )


def solution(mesh):
    rows = P(None, "seq", "ctx", None)
    spread = P(("seq", "ctx"))
    spread_rows = P(("seq", "ctx"), None)
    return jax.shard_map(
        body,
        mesh=mesh,
        in_specs=(
            rows,
            P(None, "seq"),
            rows,
            spread,
            spread_rows,
            spread_rows,
            spread_rows,
            spread_rows,
            spread,
            P("seq", "ctx"),
            P("seq", "ctx"),
            P("ctx", "seq"),
        ),
        out_specs=(
            rows,
            rows,
            spread,
            spread_rows,
            spread_rows,
            spread_rows,
            spread_rows,
            spread,
            P("seq", "ctx"),
            P("seq", "ctx"),
            P("ctx", "seq"),
        ),
        check_vma=False,
    )
```

```python
import functools
import math

import jax
import jax.numpy as jnp
from jax import lax
from jax.experimental import pallas as pl
from jax.experimental.pallas import tpu as pltpu
from jax.sharding import PartitionSpec as P

HEAD_DIM = 64
LANES = 128
EPSILON = 1e-05
ROPE_BASE = 500000.0
MASKED = -1e30
WEIGHT = 6
VMEM_LIMIT = 56 * 1024 * 1024
F32 = jnp.float32
BF16 = jnp.bfloat16


def folded_order(count):
    return list(range(0, count, 2)) + list(range(1, count, 2))[::-1]


def swap_core(array):
    ctx = lax.axis_size("ctx")
    return lax.ppermute(array, "ctx", [(i, i ^ 1) for i in range(ctx)])


def swap_seq(array, bit):
    seq = lax.axis_size("seq")
    return lax.ppermute(array, "seq", [(i, i ^ bit) for i in range(seq)])


def ring_step(array):
    chips = lax.axis_size("ctx") // 2
    order = folded_order(chips)
    pairs = [
        (order[i] * 2 + core, order[(i + 1) % chips] * 2 + core)
        for i in range(chips)
        for core in range(2)
    ]
    return lax.ppermute(array, "ctx", pairs)


def ring_gather(array):
    slots = [array]
    for _ in range(lax.axis_size("ctx") // 2 - 1):
        slots.append(ring_step(slots[-1]))
    return slots


def ring_scatter(parts):
    chips = len(parts)
    total = parts[1 % chips].astype(F32)
    for k in range(2, chips + 1):
        total = ring_step(total.astype(BF16)).astype(F32) + parts[k % chips].astype(F32)
    return total


def cube_gather(array, route):
    seq = lax.axis_size("seq")
    bits = [1 << i for i in range(seq.bit_length() - 1)]
    pieces = {0: array}
    for bit in bits if route == 0 else bits[::-1]:
        pieces.update({r ^ bit: swap_seq(piece, bit) for r, piece in pieces.items()})
    return [pieces[r] for r in range(seq)]


def cube_scatter(chunks, route, *waits):
    seq = lax.axis_size("seq")
    bits = [1 << i for i in range(seq.bit_length() - 1)]
    held = dict(enumerate(chunks))
    for bit in bits if route == 0 else bits[::-1]:
        seen = waits if len(held) > 2 else ()
        held = {
            r: held[r].astype(F32)
            + after(swap_seq(held[r ^ bit].astype(BF16), bit), *seen).astype(F32)
            for r in held
            if not r & bit
        }
    return held[0]


def after(array, *others):
    return lax.optimization_barrier((array, *others))[0]


def scaled_frequency():
    half_dim = HEAD_DIM // 2
    base_freq = ROPE_BASE ** (-jnp.arange(half_dim, dtype=F32) * 2.0 / HEAD_DIM)
    wave = 2.0 * math.pi / base_freq
    smooth = (8192.0 / wave - 1.0) / 3.0
    middle = (1.0 - smooth) * base_freq / 32.0 + smooth * base_freq
    return jnp.where(wave < 2048.0, base_freq, jnp.where(wave > 8192.0, base_freq / 32.0, middle))


def rope_tables(positions):
    angles = positions.astype(F32)[:, None] * scaled_frequency()[None, :]
    cosine, sine = jnp.cos(angles), jnp.sin(angles)
    return (
        jnp.concatenate([cosine] * 4, axis=1),
        jnp.concatenate([-sine, sine, -sine, sine], axis=1),
    )


def rotate_lanes(values, cosine, sine):
    lane = lax.broadcasted_iota(jnp.int32, values.shape, 1)
    partner = jnp.where(
        (lane % HEAD_DIM) < HEAD_DIM // 2,
        pltpu.roll(values, LANES - HEAD_DIM // 2, 1),
        pltpu.roll(values, HEAD_DIM // 2, 1),
    )
    return values * cosine + partner * sine


SMEM = pltpu.SMEM
ANYWHERE = pl.BlockSpec(memory_space=pl.ANY)
SCALARS = pl.BlockSpec(memory_space=pltpu.SMEM)
PARAMS = pltpu.CompilerParams(vmem_limit_bytes=VMEM_LIMIT)
NT = (((1,), (1,)), ((), ()))


def cost(flops, nbytes, transcendentals=0):
    return pl.CostEstimate(
        flops=int(WEIGHT * flops), bytes_accessed=int(nbytes), transcendentals=int(transcendentals)
    )


def dot(left, right):
    return jnp.dot(left, right, preferred_element_type=F32)


def dot_nt(left, right):
    return lax.dot_general(left, right, NT, preferred_element_type=F32)


def transposed(values):
    return values.astype(F32).T.astype(BF16)


def pack_kernel(kv_half, core_ref, wq, wk, wv, wo, gains, mine, other):
    def fill(out, which):
        at = 0
        for source in (wo, wq):
            half = source.shape[1] // 2
            out[:, at : at + half] = source[:, which * half : (which + 1) * half]
            at += half
        for i in range(kv_half // LANES):
            for source in (wk, wv):
                lo = which * kv_half + i * LANES
                out[:, at : at + LANES] = source[:, lo : lo + LANES]
                at += LANES
        out[:, at : at + LANES] = gains[...]

    for core in range(2):

        @pl.when(core_ref[0] == core)
        def _():
            fill(mine, core)
            fill(other, 1 - core)


def pack(core, wq, wk, wv, wo, gains):
    rows = wq.shape[0]
    width = (wq.shape[1] + wk.shape[1] + wv.shape[1] + wo.shape[1]) // 2 + LANES
    shape = jax.ShapeDtypeStruct((rows, width), BF16)
    whole = [pl.BlockSpec(memory_space=pltpu.VMEM)] * 5
    return pl.pallas_call(
        functools.partial(pack_kernel, wk.shape[1] // 2),
        in_specs=[SCALARS] + whole,
        out_shape=[shape, shape],
        compiler_params=PARAMS,
        cost_estimate=cost(0, 8 * rows * width),
    )(core, wq, wk, wv, wo, gains)


def stack_kernel(edges, core_ref, mine, other, *outs):
    rows = mine.shape[0]
    for core in range(2):

        @pl.when(core_ref[0] == core)
        def _():
            for source, at in ((mine, core), (other, 1 - core)):
                for i, out in enumerate(outs):
                    out[at * rows : (at + 1) * rows] = source[:, edges[i] : edges[i + 1]]


def stack_pieces(core, mine, other, widths):
    rows = mine.shape[0]
    edges = [sum(widths[:i]) for i in range(len(widths) + 1)]
    return pl.pallas_call(
        functools.partial(stack_kernel, edges),
        in_specs=[SCALARS] + [pl.BlockSpec(memory_space=pltpu.VMEM)] * 2,
        out_shape=[jax.ShapeDtypeStruct((2 * rows, width), BF16) for width in widths],
        compiler_params=PARAMS,
        cost_estimate=cost(0, 8 * mine.size),
    )(core, mine, other)


def placing(starts, pieces, w, sems):
    return [
        pltpu.make_async_copy(
            piece, w.at[pl.ds(pl.multiple_of(starts[i], 16), piece.shape[0])], sems.at[i]
        )
        for i, piece in enumerate(pieces)
    ]


def kv_kernel(count, batches, *refs):
    core_ref, starts, x_own, x_oth, cos_ref, sin_ref = refs[:6]
    pieces = refs[6 : 6 + count]
    kv_ref, normed, gains_ref, w_out, w, sems = refs[6 + count :]
    first = w.shape[1] - LANES - kv_ref.shape[1]
    slots = normed.shape[0] // (2 * batches)
    arriving = placing(starts, pieces, w, sems)
    for copy in arriving:
        copy.start()
    for copy in arriving:
        copy.wait()
    leaving = pltpu.make_async_copy(w, w_out, sems.at[count])
    leaving.start()
    table = w[:, w.shape[1] - LANES :].astype(F32).T
    gains_ref[...] = table[:8]
    for source, which in ((x_own, core_ref[0]), (x_oth, 1 - core_ref[0])):
        for b in range(batches):
            x = source[b * slots : (b + 1) * slots].astype(F32)
            inverse = lax.rsqrt(jnp.mean(x * x, axis=-1, keepdims=True) + EPSILON)
            at = pl.multiple_of((2 * b + which) * slots, slots)
            normed[pl.ds(at, slots)] = (x * inverse * table[:1]).astype(BF16)
    block = 2 * LANES
    for at in range(0, kv_ref.shape[1], block):
        raw = dot(normed[...], w[:, first + at : first + at + block])
        turned = rotate_lanes(raw[:, :LANES], cos_ref[...], sin_ref[...])
        kv_ref[:, at : at + LANES] = turned.astype(BF16)
        kv_ref[:, at + LANES : at + block] = raw[:, LANES:].astype(BF16)
    leaving.wait()


def project_kv(core, starts, x_own, x_oth, cosine, sine, pieces, batches, kv_width):
    rows, depth = 2 * x_own.shape[0], x_own.shape[1]
    width = pieces[0].shape[1]
    count = len(pieces)
    vmem = pl.BlockSpec(memory_space=pltpu.VMEM)
    return pl.pallas_call(
        functools.partial(kv_kernel, count, batches),
        in_specs=[SCALARS, SCALARS] + [vmem] * 4 + [ANYWHERE] * count,
        out_specs=[vmem, vmem, vmem, ANYWHERE],
        out_shape=[
            jax.ShapeDtypeStruct((rows, kv_width), BF16),
            jax.ShapeDtypeStruct((rows, depth), BF16),
            jax.ShapeDtypeStruct((8, depth), F32),
            jax.ShapeDtypeStruct((depth, width), BF16),
        ],
        scratch_shapes=[
            pltpu.VMEM((depth, width), BF16),
            pltpu.SemaphoreType.DMA((count + 1,)),
        ],
        compiler_params=PARAMS,
        cost_estimate=cost(2 * rows * depth * width, 4 * rows * depth + 4 * depth * width),
    )(core, starts, x_own, x_oth, cosine, sine, *pieces)


def q_kernel(first, normed, cos_ref, sin_ref, w, q_ref, held, sems):
    block = 2 * LANES
    width = q_ref.shape[1]
    copies = [
        pltpu.make_async_copy(
            w.at[:, pl.ds(first + at, block)], held.at[:, pl.ds(at, block)], sems.at[at // block]
        )
        for at in range(0, width, block)
    ]
    for copy in copies:
        copy.start()
    for at in range(0, width, block):
        copies[at // block].wait()
        raw = dot(normed[...], held[:, at : at + block])
        for lo in range(0, block, LANES):
            turned = rotate_lanes(raw[:, lo : lo + LANES], cos_ref[...], sin_ref[...])
            q_ref[:, at + lo : at + lo + LANES] = (turned / math.sqrt(HEAD_DIM)).astype(BF16)


def project_q(normed, cosine, sine, w, first, width):
    rows, depth = normed.shape
    vmem = pl.BlockSpec(memory_space=pltpu.VMEM)
    return pl.pallas_call(
        functools.partial(q_kernel, first),
        in_specs=[vmem] * 3 + [ANYWHERE],
        out_specs=vmem,
        out_shape=jax.ShapeDtypeStruct((rows, width), BF16),
        scratch_shapes=[
            pltpu.VMEM((depth, width), BF16),
            pltpu.SemaphoreType.DMA((width // (2 * LANES),)),
        ],
        compiler_params=PARAMS,
        cost_estimate=cost(2 * rows * depth * width, 2 * rows * depth + 4 * depth * width),
    )(normed, cosine, sine, w)


def set_bias(limit_ref, kpos_ref, qpos_ref, bias):
    @pl.when(pl.program_id(1) == 0)
    def _():
        limit = limit_ref[pl.program_id(0)]
        allowed = (kpos_ref[...] <= qpos_ref[...]) & (kpos_ref[...] < limit)
        bias[...] = jnp.where(allowed, 0.0, MASKED)


def attend_kernel(chips, limit_ref, kpos_ref, qpos_ref, q_ref, *refs):
    slots, (out_ref, lse_ref, bias) = refs[:chips], refs[chips:]
    set_bias(limit_ref, kpos_ref, qpos_ref, bias)
    heads = q_ref.shape[1] // HEAD_DIM
    kv = jnp.concatenate([slot[...] for slot in slots], axis=0)
    q_t = transposed(q_ref[...])
    v_t = transposed(kv[:, LANES:])
    outs = []
    for h in range(heads):
        a = h * 2 // heads
        k_h = kv[:, a * HEAD_DIM : (a + 1) * HEAD_DIM]
        scores = dot(k_h, q_t[h * HEAD_DIM : (h + 1) * HEAD_DIM]) + bias[...]
        top = jnp.max(scores, axis=0, keepdims=True)
        shifted = jnp.exp(scores - top)
        total = jnp.sum(shifted, axis=0, keepdims=True)
        out_t = dot(v_t[a * HEAD_DIM : (a + 1) * HEAD_DIM], shifted.astype(BF16))
        outs.append(out_t / total)
        lse_ref[h : h + 1, :] = top + jnp.log(total)
    out_ref[...] = jnp.concatenate(outs, axis=0).T.astype(BF16)


def attention_specs(batches, chips, rows, keys, width, heads, pairs):
    def at(shape):
        return pl.BlockSpec(shape, lambda b, i, n: (b, i))

    return (
        [
            pl.BlockSpec((keys, 1), lambda b, i, n: (0, 0)),
            pl.BlockSpec((1, rows), lambda b, i, n: (0, 0)),
            at((rows, width)),
        ]
        + [at((rows, 2 * LANES))] * chips,
        at((rows, width)),
        pl.BlockSpec((heads, rows), lambda b, i, n: (b * pairs + i, 0)),
    )


def attend(q, kv_slots, limits, kpos, qpos):
    rows, keys, batches, chips = qpos.shape[1], kpos.shape[0], limits.shape[0], len(kv_slots)
    pairs = kv_slots[0].shape[1] // (2 * LANES)
    width = q.shape[1] // pairs
    heads = width // HEAD_DIM
    ins, out, lse = attention_specs(batches, chips, rows, keys, width, heads, pairs)
    return pl.pallas_call(
        functools.partial(attend_kernel, chips),
        grid_spec=pltpu.PrefetchScalarGridSpec(
            num_scalar_prefetch=1,
            grid=(batches, pairs),
            in_specs=ins,
            out_specs=[out, lse],
            scratch_shapes=[pltpu.VMEM((keys, rows), F32)],
        ),
        out_shape=[
            jax.ShapeDtypeStruct(q.shape, BF16),
            jax.ShapeDtypeStruct((batches * pairs * heads, rows), F32),
        ],
        compiler_params=PARAMS,
        cost_estimate=cost(
            16 * batches * rows * keys * q.shape[1],
            4 * q.size + 2 * chips * kv_slots[0].size,
            batches * rows * keys * q.shape[1] // HEAD_DIM,
        ),
    )(limits, kpos, qpos, q, *kv_slots)


def attend_back_kernel(chips, limit_ref, kpos_ref, qpos_ref, q_ref, *refs):
    slots = refs[:chips]
    do_mine, do_other, lse_ref, cos_ref, sin_ref, dq_ref = refs[chips : chips + 6]
    d_slots, bias = refs[chips + 6 : 2 * chips + 6], refs[2 * chips + 6]
    set_bias(limit_ref, kpos_ref, qpos_ref, bias)
    rows, width = q_ref.shape
    heads = width // HEAD_DIM
    per_kv = heads // 2
    kv = jnp.concatenate([slot[...] for slot in slots], axis=0)
    d_out = (do_mine[...] + do_other[...].astype(F32)).astype(BF16)
    q_t = transposed(q_ref[...])
    do_t = transposed(d_out)
    k_t = transposed(kv[:, :LANES])
    lane = lax.broadcasted_iota(jnp.int32, (kv.shape[0], LANES), 1)
    d_queries = []
    d_keys, d_values = [], []
    for a in range(2):
        k_h = kv[:, a * HEAD_DIM : (a + 1) * HEAD_DIM]
        v_h = kv[:, LANES + a * HEAD_DIM : LANES + (a + 1) * HEAD_DIM]
        dk_sum, dv_sum = [None, None], [None, None]
        for g in range(per_kv):
            h = a * per_kv + g
            head = slice(h * HEAD_DIM, (h + 1) * HEAD_DIM)
            pair = slice((h // 2) * LANES, (h // 2 + 1) * LANES)
            scores = dot(k_h, q_t[head]) + bias[...]
            probs = jnp.exp(scores - lse_ref[h : h + 1, :])
            d_probs = dot(v_h, do_t[head])
            mean = jnp.sum(d_probs * probs, axis=0, keepdims=True)
            d_scores = (probs * (d_probs - mean)).astype(BF16)
            d_queries.append(dot(k_t[a * HEAD_DIM : (a + 1) * HEAD_DIM], d_scores))
            dk_term = dot(d_scores, q_ref[:, pair])
            dv_term = dot(probs.astype(BF16), d_out[:, pair])
            e = h % 2
            dk_sum[e] = dk_term if dk_sum[e] is None else dk_sum[e] + dk_term
            dv_sum[e] = dv_term if dv_sum[e] is None else dv_sum[e] + dv_term
        for sums, kept in ((dk_sum, d_keys), (dv_sum, d_values)):
            mixed = jnp.where(lane < HEAD_DIM, sums[0], sums[1])
            kept.append(mixed + pltpu.roll(mixed, HEAD_DIM, 1))
    d_key = jnp.where(lane < HEAD_DIM, d_keys[0], d_keys[1])
    d_value = jnp.where(lane < HEAD_DIM, d_values[0], d_values[1])
    for k, d_slot in enumerate(d_slots):
        d_slot[:, :LANES] = d_key[k * rows : (k + 1) * rows].astype(BF16)
        d_slot[:, LANES:] = d_value[k * rows : (k + 1) * rows].astype(BF16)
    d_query = jnp.concatenate(d_queries, axis=0).T
    for at in range(width // LANES):
        cut = slice(at * LANES, (at + 1) * LANES)
        turned = rotate_lanes(d_query[:, cut], cos_ref[...], -sin_ref[...])
        dq_ref[:, cut] = (turned / math.sqrt(HEAD_DIM)).astype(BF16)


def attend_back(q, kv_slots, do_mine, do_other, lse, limits, kpos, qpos, cosine, sine):
    rows, keys, batches, chips = qpos.shape[1], kpos.shape[0], limits.shape[0], len(kv_slots)
    pairs = kv_slots[0].shape[1] // (2 * LANES)
    width = q.shape[1] // pairs
    heads = width // HEAD_DIM
    ins, out, lse_spec = attention_specs(batches, chips, rows, keys, width, heads, pairs)
    table = pl.BlockSpec((rows, LANES), lambda b, i, n: (0, 0))
    return pl.pallas_call(
        functools.partial(attend_back_kernel, chips),
        grid_spec=pltpu.PrefetchScalarGridSpec(
            num_scalar_prefetch=1,
            grid=(batches, pairs),
            in_specs=ins + [out, out, lse_spec, table, table],
            out_specs=[out] + ins[3 : 3 + chips],
            scratch_shapes=[pltpu.VMEM((keys, rows), F32)],
        ),
        out_shape=[jax.ShapeDtypeStruct(q.shape, BF16)]
        + [jax.ShapeDtypeStruct(slot.shape, BF16) for slot in kv_slots],
        compiler_params=PARAMS,
        cost_estimate=cost(
            40 * batches * rows * keys * q.shape[1],
            10 * q.size + 4 * chips * kv_slots[0].size,
            batches * rows * keys * q.shape[1] // HEAD_DIM,
        ),
    )(limits, kpos, qpos, q, *kv_slots, do_mine, do_other, lse, cosine, sine)


def unrotate_kernel(last_ref, own_ref, cos_ref, sin_ref, out_ref):
    total = last_ref[...].astype(F32) + own_ref[...].astype(F32)
    for at in range(total.shape[1] // LANES):
        cut = slice(at * LANES, (at + 1) * LANES)
        part = total[:, cut]
        if at % 2 == 0:
            part = rotate_lanes(part, cos_ref[...], -sin_ref[...])
        out_ref[:, cut] = part.astype(BF16)


def unrotate(last, own, cosine, sine):
    return pl.pallas_call(
        unrotate_kernel,
        out_shape=jax.ShapeDtypeStruct(own.shape, BF16),
        compiler_params=PARAMS,
        cost_estimate=cost(0, 6 * own.size),
    )(last, own, cosine, sine)


def split_rows(batches, core_ref, acc, own, other):
    slots = acc.shape[0] // (2 * batches)
    for out, which in ((own, core_ref[0]), (other, 1 - core_ref[0])):
        for b in range(batches):
            at = pl.multiple_of((2 * b + which) * slots, slots)
            out[b * slots : (b + 1) * slots] = acc[pl.ds(at, slots)].astype(out.dtype)


def out_kernel(batches, core_ref, o_mine, o_other, w_all, own, other, w, acc, sems):
    half, width = o_mine.shape[1], w.shape[1]
    block = 2 * LANES
    copies = [
        pltpu.make_async_copy(
            w_all.at[:, pl.ds(lo, block)], w.at[:, pl.ds(lo, block)], sems.at[lo // block]
        )
        for lo in range(0, width, block)
    ]
    for copy in copies:
        copy.start()
    rows_mine = pl.ds(pl.multiple_of(core_ref[0] * half, half), half)
    rows_other = pl.ds(pl.multiple_of((1 - core_ref[0]) * half, half), half)
    for lo in range(0, width, block):
        cut = slice(lo, lo + block)
        copies[lo // block].wait()
        acc[:, cut] = dot(o_mine[...], w[rows_mine, cut]) + dot(o_other[...], w[rows_other, cut])
    split_rows(batches, core_ref, acc, own, other)


def project_out(core, o_mine, o_other, w, width, batches):
    rows, half = o_mine.shape
    vmem = pl.BlockSpec(memory_space=pltpu.VMEM)
    part = jax.ShapeDtypeStruct((rows // 2, width), F32)
    return pl.pallas_call(
        functools.partial(out_kernel, batches),
        in_specs=[SCALARS, vmem, vmem, ANYWHERE],
        out_specs=[vmem, vmem],
        out_shape=[part, part],
        scratch_shapes=[
            pltpu.VMEM((2 * half, width), BF16),
            pltpu.VMEM((rows, width), F32),
            pltpu.SemaphoreType.DMA((width // (2 * LANES),)),
        ],
        compiler_params=PARAMS,
        cost_estimate=cost(4 * rows * half * width, 4 * half * width + 12 * rows * width),
    )(core, o_mine, o_other, w)


def hidden_units(x, d, gate, up, down_t, hidden_ref, d_gate_ref, d_up_ref):
    gate_val = dot(x[...], gate[...])
    up_val = dot(x[...], up[...])
    d_hidden = dot(d[...], down_t[...])
    sigmoid_g = 1.0 / (1.0 + jnp.exp(-gate_val))
    activated = gate_val * sigmoid_g
    slope = sigmoid_g * (1.0 + gate_val * (1.0 - sigmoid_g))
    hidden_ref[...] = (activated * up_val).astype(BF16)
    d_gate_ref[...] = (d_hidden * up_val * slope).astype(BF16)
    d_up_ref[...] = (d_hidden * activated).astype(BF16)


def first_hidden_kernel(per, filled, *refs):
    arrived = refs[: 2 * per]
    weights = refs[2 * per : 2 * per + 3]
    x, d, hidden_ref, d_gate_ref, d_up_ref, sems = refs[2 * per + 3 + filled :]
    rows = arrived[0].shape[0]

    @pl.when(pl.program_id(0) == 0)
    def _():
        copies = [
            pltpu.make_async_copy(
                arrived[2 * i + j], out.at[pl.ds(i * rows, rows)], sems.at[2 * i + j]
            )
            for i in range(per)
            for j, out in enumerate((x, d))
        ]
        for copy in copies:
            copy.start()
        for copy in copies:
            copy.wait()

    hidden_units(x, d, *weights, hidden_ref, d_gate_ref, d_up_ref)


def second_hidden_kernel(filled, x, d, gate, up, down_t, *refs):
    hidden_units(x, d, gate, up, down_t, *refs[filled:])


def hidden_group(at, groups, arrived, weights, kept, rows_of=None):
    width = weights.shape[0]
    hidden_width = weights.shape[1] // 3
    tile = 2 * LANES
    tiles = hidden_width // tile
    if rows_of is None:
        height = arrived[0].shape[0] * len(arrived) // 2
        per = len(arrived) // 2
        total = height * groups
        sources, source_specs = arrived, [ANYWHERE] * len(arrived)
        wide = [jax.ShapeDtypeStruct((total, width), BF16)] * 2
        scratch = [pltpu.SemaphoreType.DMA((2 * per,))]
    else:
        total = rows_of[0].shape[0]
        height = total // groups
        sources = list(rows_of)
        source_specs = [pl.BlockSpec((height, width), lambda j: (at, 0))] * 2
        wide, scratch = [], []
    narrow = [jax.ShapeDtypeStruct((total, hidden_width), BF16)] * 3
    filled = 0 if kept is None else len(wide) + 3
    kernel = (
        functools.partial(first_hidden_kernel, per, filled)
        if rows_of is None
        else functools.partial(second_hidden_kernel, filled)
    )
    first = len(sources) + 3
    return pl.pallas_call(
        kernel,
        grid=(tiles,),
        in_specs=source_specs
        + [
            pl.BlockSpec((width, tile), lambda j, skipped=i * tiles: (0, skipped + j))
            for i in range(3)
        ]
        + [ANYWHERE] * filled,
        out_specs=[pl.BlockSpec((height, width), lambda j: (at, 0))] * len(wide)
        + [pl.BlockSpec((height, tile), lambda j: (at, j))] * 3,
        out_shape=wide + narrow,
        scratch_shapes=scratch,
        input_output_aliases={first + i: i for i in range(filled)},
        compiler_params=PARAMS,
        cost_estimate=cost(
            6 * height * width * hidden_width,
            6 * width * hidden_width + 12 * height * width,
            height * hidden_width,
        ),
    )(*sources, weights, weights, weights, *([] if kept is None else kept))


def mlp_back_kernel(*refs):
    parts, weights = (refs[:3], refs[3:6]), refs[6:8]
    back_ref, out_ref, held_own, held_oth, sems = refs[8:]
    width, count = back_ref.shape[1], refs[0].shape[1]
    block = 4 * LANES
    steps = width // block
    copies = [
        pltpu.make_async_copy(
            weight.at[pl.ds(lo, block)],
            held.at[pl.ds(lo, block)],
            sems.at[i * steps + lo // block],
        )
        for i, (weight, held) in enumerate(zip(weights, (held_own, held_oth)))
        for lo in range(0, width, block)
    ]
    for step in range(steps):
        for i in range(2):
            copies[i * steps + step].start()
    for step in range(steps):
        cut = slice(step * block, (step + 1) * block)
        back, out = 0.0, 0.0
        for i, held in enumerate((held_own, held_oth)):
            copies[i * steps + step].wait()
            hidden, d_gate, d_up = parts[i]
            back += dot_nt(d_gate[...], held[cut, :count])
            back += dot_nt(d_up[...], held[cut, count : 2 * count])
            out += dot_nt(hidden[...], held[cut, 2 * count :])
        back_ref[:, cut] = back.astype(BF16)
        out_ref[:, cut] = out.astype(BF16)


def mlp_back(at, groups, own, other, weights, weights_oth):
    height, hidden_width = own[0].shape[0] // groups, own[0].shape[1]
    width = weights.shape[0]
    return pl.pallas_call(
        mlp_back_kernel,
        grid=(1,),
        in_specs=[pl.BlockSpec((height, hidden_width), lambda j: (at, 0))] * 6 + [ANYWHERE] * 2,
        out_specs=[pl.BlockSpec((height, width), lambda j: (0, 0))] * 2,
        out_shape=[jax.ShapeDtypeStruct((height, width), BF16)] * 2,
        scratch_shapes=[
            pltpu.VMEM(weights.shape, BF16),
            pltpu.VMEM(weights.shape, BF16),
            pltpu.SemaphoreType.DMA((2 * (width // (4 * LANES)),)),
        ],
        compiler_params=PARAMS,
        cost_estimate=cost(
            12 * height * width * hidden_width, 12 * width * hidden_width + 14 * height * width
        ),
    )(*own, *other, weights, weights_oth)


def d_attended_kernel(batches, other_blocks, core_ref, d_own, d_oth, w_ref, mine, other, d_rows):
    step = pl.program_id(0)
    slots = d_own.shape[0] // batches

    @pl.when(step == 0)
    def _():
        for source, which in ((d_own, core_ref[0]), (d_oth, 1 - core_ref[0])):
            for b in range(batches):
                at = pl.multiple_of((2 * b + which) * slots, slots)
                d_rows[pl.ds(at, slots)] = source[b * slots : (b + 1) * slots]

    term = dot_nt(d_rows[...], w_ref[...])

    @pl.when(step < other_blocks)
    def _():
        other[...] = term.astype(BF16)

    @pl.when(step >= other_blocks)
    def _():
        mine[...] = term


def d_attended(core, d_own, d_oth, w, batches):
    rows, width = 2 * d_own.shape[0], d_own.shape[1]
    heads_width = w.shape[0]
    block = 2 * LANES
    blocks = heads_width // 2 // block

    def whole(shape):
        return pl.BlockSpec(shape, lambda j, c: (0, 0))

    return pl.pallas_call(
        functools.partial(d_attended_kernel, batches, blocks),
        grid_spec=pltpu.PrefetchScalarGridSpec(
            num_scalar_prefetch=1,
            grid=(2 * blocks,),
            in_specs=[
                whole(d_own.shape),
                whole(d_own.shape),
                pl.BlockSpec((block, width), lambda j, c: ((j + (1 - c[0]) * blocks) % (2 * blocks), 0)),
            ],
            out_specs=[
                pl.BlockSpec((rows, block), lambda j, c: (0, jnp.maximum(j - blocks, 0))),
                pl.BlockSpec((rows, block), lambda j, c: (0, jnp.minimum(j, blocks - 1))),
                whole((rows, width)),
            ],
        ),
        out_shape=[
            jax.ShapeDtypeStruct((rows, heads_width // 2), F32),
            jax.ShapeDtypeStruct((rows, heads_width // 2), BF16),
            jax.ShapeDtypeStruct((rows, width), BF16),
        ],
        compiler_params=PARAMS,
        cost_estimate=cost(
            2 * rows * width * heads_width, 2 * width * heads_width + 6 * rows * heads_width
        ),
    )(core, d_own, d_oth, w)


def grad_kernel(count, parts, chips, starts, *refs):
    sources, right, outs, turned = refs[:count], refs[count], refs[count + 1 : -1], refs[-1]
    shard = turned.shape[0] // (parts * chips)
    at = 0
    for source in sources:
        for lo in range(0, source.shape[1], 4 * LANES):
            turned[at : at + 4 * LANES] = transposed(source[:, lo : lo + 4 * LANES])
            at += 4 * LANES
    for r in range(parts):
        left = jnp.concatenate(
            [
                turned[pl.ds(pl.multiple_of(starts[r * chips + k], 16), shard)]
                for k in range(chips)
            ],
            axis=0,
        )
        outs[r][...] = dot(left, right[...]).astype(BF16)


def grad_chunks(starts, sources, right, parts, chips):
    rows = right.shape[0]
    depth = sum(source.shape[1] for source in sources)
    shape = jax.ShapeDtypeStruct((depth // parts, right.shape[1]), BF16)
    vmem = pl.BlockSpec(memory_space=pltpu.VMEM)
    return pl.pallas_call(
        functools.partial(grad_kernel, len(sources), parts, chips),
        in_specs=[SCALARS] + [vmem] * (len(sources) + 1),
        out_shape=[shape] * parts,
        scratch_shapes=[pltpu.VMEM((depth, rows), BF16)],
        compiler_params=PARAMS,
        cost_estimate=cost(
            2 * rows * depth * right.shape[1], 2 * rows * depth + 2 * depth * right.shape[1]
        ),
    )(starts, *sources, right)


def d_normed_kernel(batches, core_ref, dq_ref, dkv_ref, wq_ref, wkv_ref, own, other, acc):
    acc[...] = dot_nt(dq_ref[...], wq_ref[...]) + dot_nt(dkv_ref[...], wkv_ref[...])
    split_rows(batches, core_ref, acc, own, other)


def d_normed_rows(core, dq, dkv, w, first, batches):
    rows, depth = dq.shape[0], w.shape[0]
    width = dq.shape[1] + dkv.shape[1]
    block = 4 * LANES
    q_at, kv_at = first // dq.shape[1], (first + dq.shape[1]) // dkv.shape[1]

    def whole(shape):
        return pl.BlockSpec(shape, lambda j: (0, 0))

    part = pl.BlockSpec((rows // 2, block), lambda j: (0, j))
    return pl.pallas_call(
        functools.partial(d_normed_kernel, batches),
        grid=(depth // block,),
        in_specs=[
            SCALARS,
            whole(dq.shape),
            whole(dkv.shape),
            pl.BlockSpec((block, dq.shape[1]), lambda j: (j, q_at)),
            pl.BlockSpec((block, dkv.shape[1]), lambda j: (j, kv_at)),
        ],
        out_specs=[part, part],
        out_shape=[jax.ShapeDtypeStruct((rows // 2, depth), F32)] * 2,
        scratch_shapes=[pltpu.VMEM((rows, block), F32)],
        compiler_params=PARAMS,
        cost_estimate=cost(2 * rows * depth * width, 2 * depth * width + 4 * rows * depth),
    )(core, dq, dkv, w, w)


def rms_inverse(values):
    return lax.rsqrt(jnp.mean(values * values, axis=-1, keepdims=True) + EPSILON)


def rms_back(grad_in, plain, inverse, gain):
    scaled = grad_in * gain
    back = inverse * (scaled - plain * jnp.mean(scaled * plain, axis=-1, keepdims=True))
    return (back, jnp.sum(grad_in * plain, axis=0, keepdims=True))


def body(
    tokens,
    lengths,
    cotangent,
    attn_gain,
    w_query,
    w_key,
    w_value,
    w_out,
    mlp_gain,
    w_gate,
    w_up,
    w_down,
):
    batches, _, slot_count, model_width = tokens.shape
    seq_size, ctx_size = lax.axis_size("seq"), lax.axis_size("ctx")
    chips = ctx_size // 2
    seq_at, ctx_at = lax.axis_index("seq"), lax.axis_index("ctx")
    chip_at, core = ctx_at // 2, ctx_at % 2
    core_ref = core.reshape(1).astype(jnp.int32)
    order = folded_order(chips)
    shard = w_query.shape[0]
    query_half, kv_half = w_query.shape[1] // 2, w_key.shape[1] // 2
    out_half = model_width // 2
    chip_rows = 2 * slot_count
    own_rows = batches * slot_count
    limits = lengths[:, 0]

    def chip_back(k):
        index = jnp.int32(0)
        for place, chip in enumerate(order):
            index = jnp.where(chip_at == chip, order[(place - k) % chips], index)
        return index

    slot_chip = jnp.stack([chip_back(k) for k in range(chips)])
    rank = (seq_at ^ jnp.arange(seq_size))[:, None] * chips + slot_chip[None, :]
    starts = (rank * (2 * shard)).reshape(-1).astype(jnp.int32)
    out_starts = (starts + core * query_half) % (2 * query_half)

    def half(array, which, axis):
        size = array.shape[axis] // 2
        return lax.dynamic_slice_in_dim(array, which * size, size, axis)

    def mine(array, axis):
        return half(array, core, axis)

    def others(array, axis):
        return half(array, 1 - core, axis)

    def by_core(own, other, axis):
        return jnp.where(
            core == 0,
            jnp.concatenate([own, other], axis),
            jnp.concatenate([other, own], axis),
        )

    q_positions = chip_at * chip_rows + jnp.arange(chip_rows)
    cosine, sine = rope_tables(q_positions)
    cosine_all, sine_all = jnp.tile(cosine, (batches, 1)), jnp.tile(sine, (batches, 1))
    qpos = q_positions[None, :]
    kpos = (slot_chip[:, None] * chip_rows + jnp.arange(chip_rows)[None, :]).reshape(-1, 1)
    own_pos = ctx_at * slot_count + jnp.arange(slot_count)
    valid = (own_pos[None, :] < limits[:, None]).astype(F32).reshape(own_rows, 1)
    d_output = cotangent.reshape(own_rows, model_width).astype(F32) * valid
    d_rows = d_output.astype(BF16)

    gains = jnp.concatenate(
        [attn_gain[:, None], mlp_gain[:, None], jnp.zeros((shard, LANES - 2), BF16)], axis=1
    )
    x_own = tokens.reshape(own_rows, model_width)
    x_oth = swap_core(x_own)
    packed, to_other = pack(core_ref, w_query, w_key, w_value, w_out, gains)
    (piece_a,) = stack_pieces(core_ref, packed, swap_core(to_other), [packed.shape[1]])
    d_slots = [d_rows, ring_step(d_rows)]
    ring_a, cubes_a = [after(piece_a, x_oth)], []
    for k in range(chips):
        cubes_a.append(cube_gather(ring_a[k], k % 2))
        if k + 1 < chips:
            seen = [cubes_a[k - 1][1], cubes_a[k - 1][2]] if k else d_slots[1:2]
            ring_a.append(ring_step(after(ring_a[k], *seen)))
    mlp_w = jnp.concatenate([w_gate, w_up, w_down.T], axis=1)
    mlp_w = lax.all_gather(after(mlp_w, *sum(cubes_a, [])), "seq", axis=0, tiled=True)

    def flat(cubes):
        return [cubes[k][r] for r in range(seq_size) for k in range(chips)]

    kv, normed_a, gain_rows, attn_w = project_kv(
        core_ref, starts, x_own, x_oth, cosine_all, sine_all, flat(cubes_a), batches, 2 * kv_half
    )
    gain_a, gain_m = gain_rows[0:1], gain_rows[1:2]
    kv_slots = ring_gather(kv)
    q = project_q(
        normed_a, cosine_all, sine_all, attn_w, out_half, query_half
    )
    for k in range(2, chips):
        d_slots.append(ring_step(after(d_slots[-1], *([kv_slots[-1]] if k == 2 else []))))
    attended, lse = attend(q, kv_slots, limits, kpos, qpos)
    attended_oth = swap_core(after(attended, d_slots[2 % chips]))
    branch, branch_oth = project_out(
        core_ref, attended, attended_oth, attn_w, out_half, batches
    )

    branch_oth = after(swap_core(branch_oth), d_slots[-1])
    residual = x_own.astype(F32) + by_core(branch, branch_oth, 1)
    inverse_m = rms_inverse(residual)
    normed_m = (residual * inverse_m * gain_m).astype(BF16)
    x_slots = [normed_m]
    for k in range(1, min(chips, 3)):
        x_slots.append(ring_step(x_slots[-1]))
    mlp_w_oth = swap_core(after(mlp_w, x_slots[1 % chips]))
    per = 2 if chips % 2 == 0 else 1
    groups = chips // per
    kept, kept_oth, back_parts, out_slots, out_sums = None, None, [], [], []
    for g in range(groups):
        arrived = []
        for k in range(g * per, (g + 1) * per):
            arrived += [x_slots[k], d_slots[k]]
        kept = hidden_group(g, groups, arrived, mlp_w, kept)
        while len(x_slots) < chips:
            x_slots.append(ring_step(after(x_slots[-1], kept[0])))
        kept_oth = hidden_group(g, groups, None, mlp_w_oth, kept_oth, kept[:2])
        own, other = list(kept[2:]), list(kept_oth)
        if g == 0:
            own[0] = after(own[0], x_slots[min(2, chips - 1)])
        elif g == 1:
            back_first = ring_step(back_parts[1])
            own[0] = after(own[0], back_first)
        back, out = mlp_back(g, groups, own, other, mlp_w, mlp_w_oth)
        for i in range(per):
            rows = slice(i * own_rows, (i + 1) * own_rows)
            back_parts.append(back[rows])
            out_slots.append(out[rows].astype(F32))
    total, steps = back_parts[1 % chips].astype(F32), []
    for k in range(2, chips + 1):
        low = total.astype(BF16)
        if k == 3:
            kept = [after(array, low) for array in kept]
        steps.append(back_first if k == 2 and groups > 1 else ring_step(low))
        total = steps[-1].astype(F32) + back_parts[k % chips].astype(F32)
    d_normed = total
    x_all, d_all = kept[:2]

    def rows_product(left, right):
        return jnp.einsum("ri,rj->ij", left, right, preferred_element_type=F32).astype(BF16)

    def seq_sum(array, axis):
        return lax.psum_scatter(array, "seq", scatter_dimension=axis, tiled=True).astype(F32)

    products = [(rows_product(kept[2], d_all), rows_product(kept_oth[0], d_all))]
    for i in range(2):
        products.append(
            [
                rows_product(x_all, after(array, *steps[1 : 1 + i]))
                for array in (kept[3 + i], kept_oth[1 + i])
            ]
        )
    sums = [
        (own.astype(F32) + swap_core(other).astype(F32)).astype(BF16) for own, other in products
    ]
    grad_down, grad_gate, grad_up = (
        seq_sum(array, axis) for array, axis in zip(sums, (1, 0, 0))
    )

    plain_m = residual * inverse_m
    back_m, gain_m_part = rms_back(d_normed, plain_m, inverse_m, gain_m)
    d_resid = d_output + back_m
    d_low = d_resid.astype(BF16)
    out_sum = out_slots[1 % chips]
    for k in range(2, chips):
        waits = [d_low]
        if k > 2:
            waits = [do_mine]
        out_sums.append(ring_step(after(out_sum.astype(BF16), *waits)))
        out_sum = out_sums[-1].astype(F32) + out_slots[k]
        if k == 2:
            do_mine, do_other, d_half = d_attended(
                core_ref,
                mine(d_low, 1),
                swap_core(others(d_low, 1)),
                after(attn_w, *sum(map(list, products), [])),
                batches,
            )
    d_query, *d_kv_slots = attend_back(
        q,
        kv_slots,
        do_mine,
        after(swap_core(do_other), out_sums[0], *sums),
        lse,
        limits,
        kpos,
        qpos,
        cosine,
        sine,
    )

    def owner_sum(chunks, route, *waits):
        summed = cube_scatter(chunks, route, *waits)
        rows = 2 * shard
        return ring_scatter([summed[k * rows : (k + 1) * rows] for k in range(chips)])

    def own_shard(summed, lanes):
        received = swap_core(others(summed, 0))
        kept_rows = mine(summed, 0)
        edges = [sum(lanes[:i]) for i in range(len(lanes) + 1)]
        return [
            by_core(kept_rows[:, lo:hi], received[:, lo:hi], 1)
            for lo, hi in zip(edges[:-1], edges[1:])
        ]

    passing = [ring_step(after(d_kv_slots[1], *out_sums[1:2]))]
    for k in range(2, chips):
        total = passing[-1].astype(F32) + d_kv_slots[k].astype(F32)
        passing.append(ring_step(total.astype(BF16)))
    grad_out = owner_sum(
        grad_chunks(out_starts, [attended, attended_oth], d_half, seq_size, chips), 1, passing[0]
    )
    (grad_out,) = own_shard(grad_out, [out_half])
    grad_query = owner_sum(grad_chunks(starts, [normed_a], d_query, seq_size, chips), 0)
    (grad_query,) = own_shard(grad_query, [query_half])
    out_last = ring_step(after(out_sum.astype(BF16), passing[1]))
    d_kv = unrotate(passing[-1], d_kv_slots[0], cosine_all, sine_all)
    d_normed_a, d_normed_oth = d_normed_rows(core_ref, d_query, d_kv, attn_w, out_half, batches)
    d_kv = after(d_kv, d_normed_oth)
    d_normed_a = d_normed_a + swap_core(d_normed_oth)
    x_own_f = x_own.astype(F32)
    inverse_a = rms_inverse(x_own_f)
    back_a, gain_a_part = rms_back(d_normed_a, x_own_f * inverse_a, inverse_a, gain_a)
    input_grad = d_resid + back_a
    gain_sum = jnp.concatenate([gain_a_part, gain_m_part], 0)
    gain_sum = gain_sum + swap_core(gain_sum)
    bit = 1
    while bit < seq_size:
        gain_sum = gain_sum + swap_seq(gain_sum, bit)
        bit *= 2
    gain_part = gain_sum
    for _ in range(chips - 1):
        gain_part = ring_step(gain_part)
        gain_sum = gain_sum + gain_part
    grad_kv = owner_sum(grad_chunks(starts, [normed_a], d_kv, seq_size, chips), 1)
    kv_parts = own_shard(after(grad_kv, gain_sum), [LANES] * (2 * kv_half // LANES))
    grad_kv = [
        jnp.concatenate(
            [part[:, :LANES] for part in kv_parts[i::2]]
            + [part[:, LANES:] for part in kv_parts[i::2]],
            axis=1,
        )
        for i in range(2)
    ]
    gain_sum = lax.dynamic_slice_in_dim(gain_sum, (seq_at * ctx_size + ctx_at) * shard, shard, 1)

    branch_m = out_slots[0] + out_last.astype(F32)
    activations = (residual + branch_m).astype(BF16)
    return (
        activations.reshape(tokens.shape),
        input_grad.reshape(tokens.shape),
        gain_sum[0],
        grad_query,
        grad_kv[0],
        grad_kv[1],
        grad_out,
        gain_sum[1],
        grad_gate,
        grad_up,
        grad_down,
    )


def solution(mesh):
    rows = P(None, "seq", "ctx", None)
    spread = P(("seq", "ctx"))
    spread_rows = P(("seq", "ctx"), None)
    return jax.shard_map(
        body,
        mesh=mesh,
        in_specs=(
            rows,
            P(None, "seq"),
            rows,
            spread,
            spread_rows,
            spread_rows,
            spread_rows,
            spread_rows,
            spread,
            P("seq", "ctx"),
            P("seq", "ctx"),
            P("ctx", "seq"),
        ),
        out_specs=(
            rows,
            rows,
            spread,
            spread_rows,
            spread_rows,
            spread_rows,
            spread_rows,
            spread,
            P("seq", "ctx"),
            P("seq", "ctx"),
            P("ctx", "seq"),
        ),
        check_vma=False,
    )
```

```python
import functools
import math

import jax
import jax.numpy as jnp
from jax import lax
from jax.experimental import pallas as pl
from jax.experimental.pallas import tpu as pltpu
from jax.sharding import PartitionSpec as P

HEAD_DIM = 64
LANES = 128
EPSILON = 1e-05
ROPE_BASE = 500000.0
MASKED = -1e30
WEIGHT = 6
VMEM_LIMIT = 56 * 1024 * 1024
F32 = jnp.float32
BF16 = jnp.bfloat16


def folded_order(count):
    return list(range(0, count, 2)) + list(range(1, count, 2))[::-1]


def swap_core(array):
    ctx = lax.axis_size("ctx")
    return lax.ppermute(array, "ctx", [(i, i ^ 1) for i in range(ctx)])


def swap_seq(array, bit):
    seq = lax.axis_size("seq")
    return lax.ppermute(array, "seq", [(i, i ^ bit) for i in range(seq)])


def ring_step(array):
    chips = lax.axis_size("ctx") // 2
    order = folded_order(chips)
    pairs = [
        (order[i] * 2 + core, order[(i + 1) % chips] * 2 + core)
        for i in range(chips)
        for core in range(2)
    ]
    return lax.ppermute(array, "ctx", pairs)


def ring_gather(array):
    slots = [array]
    for _ in range(lax.axis_size("ctx") // 2 - 1):
        slots.append(ring_step(slots[-1]))
    return slots


def ring_scatter(parts):
    chips = len(parts)
    total = parts[1 % chips].astype(F32)
    for k in range(2, chips + 1):
        total = ring_step(total.astype(BF16)).astype(F32) + parts[k % chips].astype(F32)
    return total


def cube_gather(array, route):
    seq = lax.axis_size("seq")
    bits = [1 << i for i in range(seq.bit_length() - 1)]
    pieces = {0: array}
    for bit in bits if route == 0 else bits[::-1]:
        pieces.update({r ^ bit: swap_seq(piece, bit) for r, piece in pieces.items()})
    return [pieces[r] for r in range(seq)]


def cube_scatter(chunks, route, *waits):
    seq = lax.axis_size("seq")
    bits = [1 << i for i in range(seq.bit_length() - 1)]
    held = dict(enumerate(chunks))
    for bit in bits if route == 0 else bits[::-1]:
        seen = waits if len(held) > 2 else ()
        held = {
            r: held[r].astype(F32)
            + after(swap_seq(held[r ^ bit].astype(BF16), bit), *seen).astype(F32)
            for r in held
            if not r & bit
        }
    return held[0]


def after(array, *others):
    return lax.optimization_barrier((array, *others))[0]


def scaled_frequency():
    half_dim = HEAD_DIM // 2
    base_freq = ROPE_BASE ** (-jnp.arange(half_dim, dtype=F32) * 2.0 / HEAD_DIM)
    wave = 2.0 * math.pi / base_freq
    smooth = (8192.0 / wave - 1.0) / 3.0
    middle = (1.0 - smooth) * base_freq / 32.0 + smooth * base_freq
    return jnp.where(wave < 2048.0, base_freq, jnp.where(wave > 8192.0, base_freq / 32.0, middle))


def rope_tables(positions):
    angles = positions.astype(F32)[:, None] * scaled_frequency()[None, :]
    cosine, sine = jnp.cos(angles), jnp.sin(angles)
    return (
        jnp.concatenate([cosine] * 4, axis=1),
        jnp.concatenate([-sine, sine, -sine, sine], axis=1),
    )


def rotate_lanes(values, cosine, sine):
    lane = lax.broadcasted_iota(jnp.int32, values.shape, 1)
    partner = jnp.where(
        (lane % HEAD_DIM) < HEAD_DIM // 2,
        pltpu.roll(values, LANES - HEAD_DIM // 2, 1),
        pltpu.roll(values, HEAD_DIM // 2, 1),
    )
    return values * cosine + partner * sine


SMEM = pltpu.SMEM
ANYWHERE = pl.BlockSpec(memory_space=pl.ANY)
SCALARS = pl.BlockSpec(memory_space=pltpu.SMEM)
PARAMS = pltpu.CompilerParams(vmem_limit_bytes=VMEM_LIMIT)
NT = (((1,), (1,)), ((), ()))


def cost(flops, nbytes, transcendentals=0):
    return pl.CostEstimate(
        flops=int(WEIGHT * flops), bytes_accessed=int(nbytes), transcendentals=int(transcendentals)
    )


def dot(left, right):
    return jnp.dot(left, right, preferred_element_type=F32)


def dot_nt(left, right):
    return lax.dot_general(left, right, NT, preferred_element_type=F32)


def transposed(values):
    return values.astype(F32).T.astype(BF16)


def pack_kernel(kv_half, core_ref, wq, wk, wv, wo, gains, mine, other):
    def fill(out, which):
        at = 0
        for source in (wo, wq):
            half = source.shape[1] // 2
            out[:, at : at + half] = source[:, which * half : (which + 1) * half]
            at += half
        for i in range(kv_half // LANES):
            for source in (wk, wv):
                lo = which * kv_half + i * LANES
                out[:, at : at + LANES] = source[:, lo : lo + LANES]
                at += LANES
        out[:, at : at + LANES] = gains[...]

    for core in range(2):

        @pl.when(core_ref[0] == core)
        def _():
            fill(mine, core)
            fill(other, 1 - core)


def pack(core, wq, wk, wv, wo, gains):
    rows = wq.shape[0]
    width = (wq.shape[1] + wk.shape[1] + wv.shape[1] + wo.shape[1]) // 2 + LANES
    shape = jax.ShapeDtypeStruct((rows, width), BF16)
    whole = [pl.BlockSpec(memory_space=pltpu.VMEM)] * 5
    return pl.pallas_call(
        functools.partial(pack_kernel, wk.shape[1] // 2),
        in_specs=[SCALARS] + whole,
        out_shape=[shape, shape],
        compiler_params=PARAMS,
        cost_estimate=cost(0, 8 * rows * width),
    )(core, wq, wk, wv, wo, gains)


def stack_kernel(edges, core_ref, mine, other, *outs):
    rows = mine.shape[0]
    for core in range(2):

        @pl.when(core_ref[0] == core)
        def _():
            for source, at in ((mine, core), (other, 1 - core)):
                for i, out in enumerate(outs):
                    out[at * rows : (at + 1) * rows] = source[:, edges[i] : edges[i + 1]]


def stack_pieces(core, mine, other, widths):
    rows = mine.shape[0]
    edges = [sum(widths[:i]) for i in range(len(widths) + 1)]
    return pl.pallas_call(
        functools.partial(stack_kernel, edges),
        in_specs=[SCALARS] + [pl.BlockSpec(memory_space=pltpu.VMEM)] * 2,
        out_shape=[jax.ShapeDtypeStruct((2 * rows, width), BF16) for width in widths],
        compiler_params=PARAMS,
        cost_estimate=cost(0, 8 * mine.size),
    )(core, mine, other)


def placing(starts, pieces, w, sems):
    return [
        pltpu.make_async_copy(
            piece, w.at[pl.ds(pl.multiple_of(starts[i], 16), piece.shape[0])], sems.at[i]
        )
        for i, piece in enumerate(pieces)
    ]


def kv_kernel(count, batches, *refs):
    core_ref, starts, x_own, x_oth, cos_ref, sin_ref = refs[:6]
    pieces = refs[6 : 6 + count]
    kv_ref, normed, gains_ref, w_out, w, sems = refs[6 + count :]
    first = w.shape[1] - LANES - kv_ref.shape[1]
    slots = normed.shape[0] // (2 * batches)
    arriving = placing(starts, pieces, w, sems)
    for copy in arriving:
        copy.start()
    for copy in arriving:
        copy.wait()
    leaving = pltpu.make_async_copy(w, w_out, sems.at[count])
    leaving.start()
    table = w[:, w.shape[1] - LANES :].astype(F32).T
    gains_ref[...] = table[:8]
    for source, which in ((x_own, core_ref[0]), (x_oth, 1 - core_ref[0])):
        for b in range(batches):
            x = source[b * slots : (b + 1) * slots].astype(F32)
            inverse = lax.rsqrt(jnp.mean(x * x, axis=-1, keepdims=True) + EPSILON)
            at = pl.multiple_of((2 * b + which) * slots, slots)
            normed[pl.ds(at, slots)] = (x * inverse * table[:1]).astype(BF16)
    block = 2 * LANES
    for at in range(0, kv_ref.shape[1], block):
        raw = dot(normed[...], w[:, first + at : first + at + block])
        turned = rotate_lanes(raw[:, :LANES], cos_ref[...], sin_ref[...])
        kv_ref[:, at : at + LANES] = turned.astype(BF16)
        kv_ref[:, at + LANES : at + block] = raw[:, LANES:].astype(BF16)
    leaving.wait()


def project_kv(core, starts, x_own, x_oth, cosine, sine, pieces, batches, kv_width):
    rows, depth = 2 * x_own.shape[0], x_own.shape[1]
    width = pieces[0].shape[1]
    count = len(pieces)
    vmem = pl.BlockSpec(memory_space=pltpu.VMEM)
    return pl.pallas_call(
        functools.partial(kv_kernel, count, batches),
        in_specs=[SCALARS, SCALARS] + [vmem] * 4 + [ANYWHERE] * count,
        out_specs=[vmem, vmem, vmem, ANYWHERE],
        out_shape=[
            jax.ShapeDtypeStruct((rows, kv_width), BF16),
            jax.ShapeDtypeStruct((rows, depth), BF16),
            jax.ShapeDtypeStruct((8, depth), F32),
            jax.ShapeDtypeStruct((depth, width), BF16),
        ],
        scratch_shapes=[
            pltpu.VMEM((depth, width), BF16),
            pltpu.SemaphoreType.DMA((count + 1,)),
        ],
        compiler_params=PARAMS,
        cost_estimate=cost(2 * rows * depth * width, 4 * rows * depth + 4 * depth * width),
    )(core, starts, x_own, x_oth, cosine, sine, *pieces)


def q_kernel(first, normed, cos_ref, sin_ref, w, q_ref, held, sems):
    block = 2 * LANES
    width = q_ref.shape[1]
    copies = [
        pltpu.make_async_copy(
            w.at[:, pl.ds(first + at, block)], held.at[:, pl.ds(at, block)], sems.at[at // block]
        )
        for at in range(0, width, block)
    ]
    for copy in copies:
        copy.start()
    for at in range(0, width, block):
        copies[at // block].wait()
        raw = dot(normed[...], held[:, at : at + block])
        for lo in range(0, block, LANES):
            turned = rotate_lanes(raw[:, lo : lo + LANES], cos_ref[...], sin_ref[...])
            q_ref[:, at + lo : at + lo + LANES] = (turned / math.sqrt(HEAD_DIM)).astype(BF16)


def project_q(normed, cosine, sine, w, first, width):
    rows, depth = normed.shape
    vmem = pl.BlockSpec(memory_space=pltpu.VMEM)
    return pl.pallas_call(
        functools.partial(q_kernel, first),
        in_specs=[vmem] * 3 + [ANYWHERE],
        out_specs=vmem,
        out_shape=jax.ShapeDtypeStruct((rows, width), BF16),
        scratch_shapes=[
            pltpu.VMEM((depth, width), BF16),
            pltpu.SemaphoreType.DMA((width // (2 * LANES),)),
        ],
        compiler_params=PARAMS,
        cost_estimate=cost(2 * rows * depth * width, 2 * rows * depth + 4 * depth * width),
    )(normed, cosine, sine, w)


def set_bias(limit_ref, kpos_ref, qpos_ref, bias):
    @pl.when(pl.program_id(1) == 0)
    def _():
        limit = limit_ref[pl.program_id(0)]
        allowed = (kpos_ref[...] <= qpos_ref[...]) & (kpos_ref[...] < limit)
        bias[...] = jnp.where(allowed, 0.0, MASKED)


def attend_kernel(chips, limit_ref, kpos_ref, qpos_ref, q_ref, *refs):
    slots, (out_ref, lse_ref, bias) = refs[:chips], refs[chips:]
    set_bias(limit_ref, kpos_ref, qpos_ref, bias)
    heads = q_ref.shape[1] // HEAD_DIM
    kv = jnp.concatenate([slot[...] for slot in slots], axis=0)
    q_t = transposed(q_ref[...])
    v_t = transposed(kv[:, LANES:])
    outs = []
    for h in range(heads):
        a = h * 2 // heads
        k_h = kv[:, a * HEAD_DIM : (a + 1) * HEAD_DIM]
        scores = dot(k_h, q_t[h * HEAD_DIM : (h + 1) * HEAD_DIM]) + bias[...]
        top = jnp.max(scores, axis=0, keepdims=True)
        shifted = jnp.exp(scores - top)
        total = jnp.sum(shifted, axis=0, keepdims=True)
        out_t = dot(v_t[a * HEAD_DIM : (a + 1) * HEAD_DIM], shifted.astype(BF16))
        outs.append(out_t / total)
        lse_ref[h : h + 1, :] = top + jnp.log(total)
    out_ref[...] = jnp.concatenate(outs, axis=0).T.astype(BF16)


def attention_specs(batches, chips, rows, keys, width, heads, pairs):
    def at(shape):
        return pl.BlockSpec(shape, lambda b, i, n: (b, i))

    return (
        [
            pl.BlockSpec((keys, 1), lambda b, i, n: (0, 0)),
            pl.BlockSpec((1, rows), lambda b, i, n: (0, 0)),
            at((rows, width)),
        ]
        + [at((rows, 2 * LANES))] * chips,
        at((rows, width)),
        pl.BlockSpec((heads, rows), lambda b, i, n: (b * pairs + i, 0)),
    )


def attend(q, kv_slots, limits, kpos, qpos):
    rows, keys, batches, chips = qpos.shape[1], kpos.shape[0], limits.shape[0], len(kv_slots)
    pairs = kv_slots[0].shape[1] // (2 * LANES)
    width = q.shape[1] // pairs
    heads = width // HEAD_DIM
    ins, out, lse = attention_specs(batches, chips, rows, keys, width, heads, pairs)
    return pl.pallas_call(
        functools.partial(attend_kernel, chips),
        grid_spec=pltpu.PrefetchScalarGridSpec(
            num_scalar_prefetch=1,
            grid=(batches, pairs),
            in_specs=ins,
            out_specs=[out, lse],
            scratch_shapes=[pltpu.VMEM((keys, rows), F32)],
        ),
        out_shape=[
            jax.ShapeDtypeStruct(q.shape, BF16),
            jax.ShapeDtypeStruct((batches * pairs * heads, rows), F32),
        ],
        compiler_params=PARAMS,
        cost_estimate=cost(
            16 * batches * rows * keys * q.shape[1],
            4 * q.size + 2 * chips * kv_slots[0].size,
            batches * rows * keys * q.shape[1] // HEAD_DIM,
        ),
    )(limits, kpos, qpos, q, *kv_slots)


def attend_back_kernel(chips, limit_ref, kpos_ref, qpos_ref, q_ref, *refs):
    slots = refs[:chips]
    do_mine, do_other, lse_ref, cos_ref, sin_ref, dq_ref = refs[chips : chips + 6]
    d_slots, bias = refs[chips + 6 : 2 * chips + 6], refs[2 * chips + 6]
    set_bias(limit_ref, kpos_ref, qpos_ref, bias)
    rows, width = q_ref.shape
    heads = width // HEAD_DIM
    per_kv = heads // 2
    kv = jnp.concatenate([slot[...] for slot in slots], axis=0)
    d_out = (do_mine[...] + do_other[...].astype(F32)).astype(BF16)
    q_t = transposed(q_ref[...])
    do_t = transposed(d_out)
    k_t = transposed(kv[:, :LANES])
    lane = lax.broadcasted_iota(jnp.int32, (kv.shape[0], LANES), 1)
    d_queries = []
    d_keys, d_values = [], []
    for a in range(2):
        k_h = kv[:, a * HEAD_DIM : (a + 1) * HEAD_DIM]
        v_h = kv[:, LANES + a * HEAD_DIM : LANES + (a + 1) * HEAD_DIM]
        dk_sum, dv_sum = [None, None], [None, None]
        for g in range(per_kv):
            h = a * per_kv + g
            head = slice(h * HEAD_DIM, (h + 1) * HEAD_DIM)
            pair = slice((h // 2) * LANES, (h // 2 + 1) * LANES)
            scores = dot(k_h, q_t[head]) + bias[...]
            probs = jnp.exp(scores - lse_ref[h : h + 1, :])
            d_probs = dot(v_h, do_t[head])
            mean = jnp.sum(d_probs * probs, axis=0, keepdims=True)
            d_scores = (probs * (d_probs - mean)).astype(BF16)
            d_queries.append(dot(k_t[a * HEAD_DIM : (a + 1) * HEAD_DIM], d_scores))
            dk_term = dot(d_scores, q_ref[:, pair])
            dv_term = dot(probs.astype(BF16), d_out[:, pair])
            e = h % 2
            dk_sum[e] = dk_term if dk_sum[e] is None else dk_sum[e] + dk_term
            dv_sum[e] = dv_term if dv_sum[e] is None else dv_sum[e] + dv_term
        for sums, kept in ((dk_sum, d_keys), (dv_sum, d_values)):
            mixed = jnp.where(lane < HEAD_DIM, sums[0], sums[1])
            kept.append(mixed + pltpu.roll(mixed, HEAD_DIM, 1))
    d_key = jnp.where(lane < HEAD_DIM, d_keys[0], d_keys[1])
    d_value = jnp.where(lane < HEAD_DIM, d_values[0], d_values[1])
    for k, d_slot in enumerate(d_slots):
        d_slot[:, :LANES] = d_key[k * rows : (k + 1) * rows].astype(BF16)
        d_slot[:, LANES:] = d_value[k * rows : (k + 1) * rows].astype(BF16)
    d_query = jnp.concatenate(d_queries, axis=0).T
    for at in range(width // LANES):
        cut = slice(at * LANES, (at + 1) * LANES)
        turned = rotate_lanes(d_query[:, cut], cos_ref[...], -sin_ref[...])
        dq_ref[:, cut] = (turned / math.sqrt(HEAD_DIM)).astype(BF16)


def attend_back(q, kv_slots, do_mine, do_other, lse, limits, kpos, qpos, cosine, sine):
    rows, keys, batches, chips = qpos.shape[1], kpos.shape[0], limits.shape[0], len(kv_slots)
    pairs = kv_slots[0].shape[1] // (2 * LANES)
    width = q.shape[1] // pairs
    heads = width // HEAD_DIM
    ins, out, lse_spec = attention_specs(batches, chips, rows, keys, width, heads, pairs)
    table = pl.BlockSpec((rows, LANES), lambda b, i, n: (0, 0))
    return pl.pallas_call(
        functools.partial(attend_back_kernel, chips),
        grid_spec=pltpu.PrefetchScalarGridSpec(
            num_scalar_prefetch=1,
            grid=(batches, pairs),
            in_specs=ins + [out, out, lse_spec, table, table],
            out_specs=[out] + ins[3 : 3 + chips],
            scratch_shapes=[pltpu.VMEM((keys, rows), F32)],
        ),
        out_shape=[jax.ShapeDtypeStruct(q.shape, BF16)]
        + [jax.ShapeDtypeStruct(slot.shape, BF16) for slot in kv_slots],
        compiler_params=PARAMS,
        cost_estimate=cost(
            40 * batches * rows * keys * q.shape[1],
            10 * q.size + 4 * chips * kv_slots[0].size,
            batches * rows * keys * q.shape[1] // HEAD_DIM,
        ),
    )(limits, kpos, qpos, q, *kv_slots, do_mine, do_other, lse, cosine, sine)


def unrotate_kernel(last_ref, own_ref, cos_ref, sin_ref, out_ref):
    total = last_ref[...].astype(F32) + own_ref[...].astype(F32)
    for at in range(total.shape[1] // LANES):
        cut = slice(at * LANES, (at + 1) * LANES)
        part = total[:, cut]
        if at % 2 == 0:
            part = rotate_lanes(part, cos_ref[...], -sin_ref[...])
        out_ref[:, cut] = part.astype(BF16)


def unrotate(last, own, cosine, sine):
    return pl.pallas_call(
        unrotate_kernel,
        out_shape=jax.ShapeDtypeStruct(own.shape, BF16),
        compiler_params=PARAMS,
        cost_estimate=cost(0, 6 * own.size),
    )(last, own, cosine, sine)


def split_rows(batches, core_ref, acc, own, other):
    slots = acc.shape[0] // (2 * batches)
    for out, which in ((own, core_ref[0]), (other, 1 - core_ref[0])):
        for b in range(batches):
            at = pl.multiple_of((2 * b + which) * slots, slots)
            out[b * slots : (b + 1) * slots] = acc[pl.ds(at, slots)].astype(out.dtype)


def out_kernel(batches, core_ref, o_mine, o_other, w_all, own, other, w, acc, sems):
    half, width = o_mine.shape[1], w.shape[1]
    block = 2 * LANES
    copies = [
        pltpu.make_async_copy(
            w_all.at[:, pl.ds(lo, block)], w.at[:, pl.ds(lo, block)], sems.at[lo // block]
        )
        for lo in range(0, width, block)
    ]
    for copy in copies:
        copy.start()
    rows_mine = pl.ds(pl.multiple_of(core_ref[0] * half, half), half)
    rows_other = pl.ds(pl.multiple_of((1 - core_ref[0]) * half, half), half)
    for lo in range(0, width, block):
        cut = slice(lo, lo + block)
        copies[lo // block].wait()
        acc[:, cut] = dot(o_mine[...], w[rows_mine, cut]) + dot(o_other[...], w[rows_other, cut])
    split_rows(batches, core_ref, acc, own, other)


def project_out(core, o_mine, o_other, w, width, batches):
    rows, half = o_mine.shape
    vmem = pl.BlockSpec(memory_space=pltpu.VMEM)
    part = jax.ShapeDtypeStruct((rows // 2, width), F32)
    return pl.pallas_call(
        functools.partial(out_kernel, batches),
        in_specs=[SCALARS, vmem, vmem, ANYWHERE],
        out_specs=[vmem, vmem],
        out_shape=[part, part],
        scratch_shapes=[
            pltpu.VMEM((2 * half, width), BF16),
            pltpu.VMEM((rows, width), F32),
            pltpu.SemaphoreType.DMA((width // (2 * LANES),)),
        ],
        compiler_params=PARAMS,
        cost_estimate=cost(4 * rows * half * width, 4 * half * width + 12 * rows * width),
    )(core, o_mine, o_other, w)


def hidden_units(x, d, gate, up, down_t, hidden_ref, d_gate_ref, d_up_ref):
    gate_val = dot(x[...], gate[...])
    up_val = dot(x[...], up[...])
    d_hidden = dot(d[...], down_t[...])
    sigmoid_g = 1.0 / (1.0 + jnp.exp(-gate_val))
    activated = gate_val * sigmoid_g
    slope = sigmoid_g * (1.0 + gate_val * (1.0 - sigmoid_g))
    hidden_ref[...] = (activated * up_val).astype(BF16)
    d_gate_ref[...] = (d_hidden * up_val * slope).astype(BF16)
    d_up_ref[...] = (d_hidden * activated).astype(BF16)


def first_hidden_kernel(per, filled, *refs):
    arrived = refs[: 2 * per]
    weights = refs[2 * per : 2 * per + 3]
    x, d, hidden_ref, d_gate_ref, d_up_ref, sems = refs[2 * per + 3 + filled :]
    rows = arrived[0].shape[0]

    @pl.when(pl.program_id(0) == 0)
    def _():
        copies = [
            pltpu.make_async_copy(
                arrived[2 * i + j], out.at[pl.ds(i * rows, rows)], sems.at[2 * i + j]
            )
            for i in range(per)
            for j, out in enumerate((x, d))
        ]
        for copy in copies:
            copy.start()
        for copy in copies:
            copy.wait()

    hidden_units(x, d, *weights, hidden_ref, d_gate_ref, d_up_ref)


def second_hidden_kernel(filled, x, d, gate, up, down_t, *refs):
    hidden_units(x, d, gate, up, down_t, *refs[filled:])


def hidden_group(at, groups, arrived, weights, kept, rows_of=None):
    width = weights.shape[0]
    hidden_width = weights.shape[1] // 3
    tile = 2 * LANES
    tiles = hidden_width // tile
    if rows_of is None:
        height = arrived[0].shape[0] * len(arrived) // 2
        per = len(arrived) // 2
        total = height * groups
        sources, source_specs = arrived, [ANYWHERE] * len(arrived)
        wide = [jax.ShapeDtypeStruct((total, width), BF16)] * 2
        scratch = [pltpu.SemaphoreType.DMA((2 * per,))]
    else:
        total = rows_of[0].shape[0]
        height = total // groups
        sources = list(rows_of)
        source_specs = [pl.BlockSpec((height, width), lambda j: (at, 0))] * 2
        wide, scratch = [], []
    narrow = [jax.ShapeDtypeStruct((total, hidden_width), BF16)] * 3
    filled = 0 if kept is None else len(wide) + 3
    kernel = (
        functools.partial(first_hidden_kernel, per, filled)
        if rows_of is None
        else functools.partial(second_hidden_kernel, filled)
    )
    first = len(sources) + 3
    return pl.pallas_call(
        kernel,
        grid=(tiles,),
        in_specs=source_specs
        + [
            pl.BlockSpec((width, tile), lambda j, skipped=i * tiles: (0, skipped + j))
            for i in range(3)
        ]
        + [ANYWHERE] * filled,
        out_specs=[pl.BlockSpec((height, width), lambda j: (at, 0))] * len(wide)
        + [pl.BlockSpec((height, tile), lambda j: (at, j))] * 3,
        out_shape=wide + narrow,
        scratch_shapes=scratch,
        input_output_aliases={first + i: i for i in range(filled)},
        compiler_params=PARAMS,
        cost_estimate=cost(
            6 * height * width * hidden_width,
            6 * width * hidden_width + 12 * height * width,
            height * hidden_width,
        ),
    )(*sources, weights, weights, weights, *([] if kept is None else kept))


def mlp_back_kernel(*refs):
    parts, weights = (refs[:3], refs[3:6]), refs[6:8]
    back_ref, out_ref, held_own, held_oth, sems = refs[8:]
    width, count = back_ref.shape[1], refs[0].shape[1]
    block = 4 * LANES
    steps = width // block
    copies = [
        pltpu.make_async_copy(
            weight.at[pl.ds(lo, block)],
            held.at[pl.ds(lo, block)],
            sems.at[i * steps + lo // block],
        )
        for i, (weight, held) in enumerate(zip(weights, (held_own, held_oth)))
        for lo in range(0, width, block)
    ]
    for step in range(steps):
        for i in range(2):
            copies[i * steps + step].start()
    for step in range(steps):
        cut = slice(step * block, (step + 1) * block)
        back, out = 0.0, 0.0
        for i, held in enumerate((held_own, held_oth)):
            copies[i * steps + step].wait()
            hidden, d_gate, d_up = parts[i]
            back += dot_nt(d_gate[...], held[cut, :count])
            back += dot_nt(d_up[...], held[cut, count : 2 * count])
            out += dot_nt(hidden[...], held[cut, 2 * count :])
        back_ref[:, cut] = back.astype(BF16)
        out_ref[:, cut] = out.astype(BF16)


def mlp_back(at, groups, own, other, weights, weights_oth):
    height, hidden_width = own[0].shape[0] // groups, own[0].shape[1]
    width = weights.shape[0]
    return pl.pallas_call(
        mlp_back_kernel,
        grid=(1,),
        in_specs=[pl.BlockSpec((height, hidden_width), lambda j: (at, 0))] * 6 + [ANYWHERE] * 2,
        out_specs=[pl.BlockSpec((height, width), lambda j: (0, 0))] * 2,
        out_shape=[jax.ShapeDtypeStruct((height, width), BF16)] * 2,
        scratch_shapes=[
            pltpu.VMEM(weights.shape, BF16),
            pltpu.VMEM(weights.shape, BF16),
            pltpu.SemaphoreType.DMA((2 * (width // (4 * LANES)),)),
        ],
        compiler_params=PARAMS,
        cost_estimate=cost(
            12 * height * width * hidden_width, 12 * width * hidden_width + 14 * height * width
        ),
    )(*own, *other, weights, weights_oth)


def d_attended_kernel(batches, other_blocks, core_ref, d_own, d_oth, w_ref, mine, other, d_rows):
    step = pl.program_id(0)
    slots = d_own.shape[0] // batches

    @pl.when(step == 0)
    def _():
        for source, which in ((d_own, core_ref[0]), (d_oth, 1 - core_ref[0])):
            for b in range(batches):
                at = pl.multiple_of((2 * b + which) * slots, slots)
                d_rows[pl.ds(at, slots)] = source[b * slots : (b + 1) * slots]

    term = dot_nt(d_rows[...], w_ref[...])

    @pl.when(step < other_blocks)
    def _():
        other[...] = term.astype(BF16)

    @pl.when(step >= other_blocks)
    def _():
        mine[...] = term


def d_attended(core, d_own, d_oth, w, batches):
    rows, width = 2 * d_own.shape[0], d_own.shape[1]
    heads_width = w.shape[0]
    block = 2 * LANES
    blocks = heads_width // 2 // block

    def whole(shape):
        return pl.BlockSpec(shape, lambda j, c: (0, 0))

    return pl.pallas_call(
        functools.partial(d_attended_kernel, batches, blocks),
        grid_spec=pltpu.PrefetchScalarGridSpec(
            num_scalar_prefetch=1,
            grid=(2 * blocks,),
            in_specs=[
                whole(d_own.shape),
                whole(d_own.shape),
                pl.BlockSpec((block, width), lambda j, c: ((j + (1 - c[0]) * blocks) % (2 * blocks), 0)),
            ],
            out_specs=[
                pl.BlockSpec((rows, block), lambda j, c: (0, jnp.maximum(j - blocks, 0))),
                pl.BlockSpec((rows, block), lambda j, c: (0, jnp.minimum(j, blocks - 1))),
                whole((rows, width)),
            ],
        ),
        out_shape=[
            jax.ShapeDtypeStruct((rows, heads_width // 2), F32),
            jax.ShapeDtypeStruct((rows, heads_width // 2), BF16),
            jax.ShapeDtypeStruct((rows, width), BF16),
        ],
        compiler_params=PARAMS,
        cost_estimate=cost(
            2 * rows * width * heads_width, 2 * width * heads_width + 6 * rows * heads_width
        ),
    )(core, d_own, d_oth, w)


def grad_kernel(count, parts, chips, starts, *refs):
    sources, right, outs, turned = refs[:count], refs[count], refs[count + 1 : -1], refs[-1]
    shard = turned.shape[0] // (parts * chips)
    at = 0
    for source in sources:
        for lo in range(0, source.shape[1], 4 * LANES):
            turned[at : at + 4 * LANES] = transposed(source[:, lo : lo + 4 * LANES])
            at += 4 * LANES
    for r in range(parts):
        left = jnp.concatenate(
            [
                turned[pl.ds(pl.multiple_of(starts[r * chips + k], 16), shard)]
                for k in range(chips)
            ],
            axis=0,
        )
        outs[r][...] = dot(left, right[...]).astype(BF16)


def grad_chunks(starts, sources, right, parts, chips):
    rows = right.shape[0]
    depth = sum(source.shape[1] for source in sources)
    shape = jax.ShapeDtypeStruct((depth // parts, right.shape[1]), BF16)
    vmem = pl.BlockSpec(memory_space=pltpu.VMEM)
    return pl.pallas_call(
        functools.partial(grad_kernel, len(sources), parts, chips),
        in_specs=[SCALARS] + [vmem] * (len(sources) + 1),
        out_shape=[shape] * parts,
        scratch_shapes=[pltpu.VMEM((depth, rows), BF16)],
        compiler_params=PARAMS,
        cost_estimate=cost(
            2 * rows * depth * right.shape[1], 2 * rows * depth + 2 * depth * right.shape[1]
        ),
    )(starts, *sources, right)


def d_normed_kernel(batches, core_ref, dq_ref, dkv_ref, wq_ref, wkv_ref, own, other, acc):
    acc[...] = dot_nt(dq_ref[...], wq_ref[...]) + dot_nt(dkv_ref[...], wkv_ref[...])
    split_rows(batches, core_ref, acc, own, other)


def d_normed_rows(core, dq, dkv, w, first, batches):
    rows, depth = dq.shape[0], w.shape[0]
    width = dq.shape[1] + dkv.shape[1]
    block = 4 * LANES
    q_at, kv_at = first // dq.shape[1], (first + dq.shape[1]) // dkv.shape[1]

    def whole(shape):
        return pl.BlockSpec(shape, lambda j: (0, 0))

    part = pl.BlockSpec((rows // 2, block), lambda j: (0, j))
    return pl.pallas_call(
        functools.partial(d_normed_kernel, batches),
        grid=(depth // block,),
        in_specs=[
            SCALARS,
            whole(dq.shape),
            whole(dkv.shape),
            pl.BlockSpec((block, dq.shape[1]), lambda j: (j, q_at)),
            pl.BlockSpec((block, dkv.shape[1]), lambda j: (j, kv_at)),
        ],
        out_specs=[part, part],
        out_shape=[
            jax.ShapeDtypeStruct((rows // 2, depth), F32),
            jax.ShapeDtypeStruct((rows // 2, depth), BF16),
        ],
        scratch_shapes=[pltpu.VMEM((rows, block), F32)],
        compiler_params=PARAMS,
        cost_estimate=cost(2 * rows * depth * width, 2 * depth * width + 4 * rows * depth),
    )(core, dq, dkv, w, w)


def rms_inverse(values):
    return lax.rsqrt(jnp.mean(values * values, axis=-1, keepdims=True) + EPSILON)


def rms_back(grad_in, plain, inverse, gain):
    scaled = grad_in * gain
    back = inverse * (scaled - plain * jnp.mean(scaled * plain, axis=-1, keepdims=True))
    return (back, jnp.sum(grad_in * plain, axis=0, keepdims=True))


def body(
    tokens,
    lengths,
    cotangent,
    attn_gain,
    w_query,
    w_key,
    w_value,
    w_out,
    mlp_gain,
    w_gate,
    w_up,
    w_down,
):
    batches, _, slot_count, model_width = tokens.shape
    seq_size, ctx_size = lax.axis_size("seq"), lax.axis_size("ctx")
    chips = ctx_size // 2
    seq_at, ctx_at = lax.axis_index("seq"), lax.axis_index("ctx")
    chip_at, core = ctx_at // 2, ctx_at % 2
    core_ref = core.reshape(1).astype(jnp.int32)
    order = folded_order(chips)
    shard = w_query.shape[0]
    query_half, kv_half = w_query.shape[1] // 2, w_key.shape[1] // 2
    out_half = model_width // 2
    chip_rows = 2 * slot_count
    own_rows = batches * slot_count
    limits = lengths[:, 0]

    def chip_back(k):
        index = jnp.int32(0)
        for place, chip in enumerate(order):
            index = jnp.where(chip_at == chip, order[(place - k) % chips], index)
        return index

    slot_chip = jnp.stack([chip_back(k) for k in range(chips)])
    rank = (seq_at ^ jnp.arange(seq_size))[:, None] * chips + slot_chip[None, :]
    starts = (rank * (2 * shard)).reshape(-1).astype(jnp.int32)
    out_starts = (starts + core * query_half) % (2 * query_half)

    def half(array, which, axis):
        size = array.shape[axis] // 2
        return lax.dynamic_slice_in_dim(array, which * size, size, axis)

    def mine(array, axis):
        return half(array, core, axis)

    def others(array, axis):
        return half(array, 1 - core, axis)

    def by_core(own, other, axis):
        return jnp.where(
            core == 0,
            jnp.concatenate([own, other], axis),
            jnp.concatenate([other, own], axis),
        )

    q_positions = chip_at * chip_rows + jnp.arange(chip_rows)
    cosine, sine = rope_tables(q_positions)
    cosine_all, sine_all = jnp.tile(cosine, (batches, 1)), jnp.tile(sine, (batches, 1))
    qpos = q_positions[None, :]
    kpos = (slot_chip[:, None] * chip_rows + jnp.arange(chip_rows)[None, :]).reshape(-1, 1)
    own_pos = ctx_at * slot_count + jnp.arange(slot_count)
    valid = (own_pos[None, :] < limits[:, None]).astype(F32).reshape(own_rows, 1)
    d_output = cotangent.reshape(own_rows, model_width).astype(F32) * valid
    d_rows = d_output.astype(BF16)

    gains = jnp.concatenate(
        [attn_gain[:, None], mlp_gain[:, None], jnp.zeros((shard, LANES - 2), BF16)], axis=1
    )
    x_own = tokens.reshape(own_rows, model_width)
    x_oth = swap_core(x_own)
    packed, to_other = pack(core_ref, w_query, w_key, w_value, w_out, gains)
    (piece_a,) = stack_pieces(core_ref, packed, swap_core(to_other), [packed.shape[1]])
    d_slots = [d_rows, ring_step(d_rows)]
    ring_a, cubes_a = [after(piece_a, x_oth)], []
    for k in range(chips):
        cubes_a.append(cube_gather(ring_a[k], k % 2))
        if k + 1 < chips:
            seen = [cubes_a[k - 1][1], cubes_a[k - 1][2]] if k else d_slots[1:2]
            ring_a.append(ring_step(after(ring_a[k], *seen)))
    mlp_w = jnp.concatenate([w_gate, w_up, w_down.T], axis=1)
    mlp_w = lax.all_gather(after(mlp_w, *sum(cubes_a, [])), "seq", axis=0, tiled=True)

    def flat(cubes):
        return [cubes[k][r] for r in range(seq_size) for k in range(chips)]

    kv, normed_a, gain_rows, attn_w = project_kv(
        core_ref, starts, x_own, x_oth, cosine_all, sine_all, flat(cubes_a), batches, 2 * kv_half
    )
    gain_a, gain_m = gain_rows[0:1], gain_rows[1:2]
    kv_slots = ring_gather(kv)
    q = project_q(
        normed_a, cosine_all, sine_all, attn_w, out_half, query_half
    )
    for k in range(2, chips):
        d_slots.append(ring_step(after(d_slots[-1], *([kv_slots[-1]] if k == 2 else []))))
    attended, lse = attend(q, kv_slots, limits, kpos, qpos)
    attended_oth = swap_core(after(attended, d_slots[2 % chips]))
    branch, branch_oth = project_out(
        core_ref, attended, attended_oth, attn_w, out_half, batches
    )

    branch_oth = after(swap_core(branch_oth), d_slots[-1])
    residual = x_own.astype(F32) + by_core(branch, branch_oth, 1)
    inverse_m = rms_inverse(residual)
    normed_m = (residual * inverse_m * gain_m).astype(BF16)
    x_slots = [normed_m]
    for k in range(1, min(chips, 3)):
        x_slots.append(ring_step(x_slots[-1]))
    mlp_w_oth = swap_core(after(mlp_w, x_slots[1 % chips]))
    per = 2 if chips % 2 == 0 else 1
    groups = chips // per
    kept, kept_oth, back_parts, out_slots, out_sums = None, None, [], [], []
    for g in range(groups):
        arrived = []
        for k in range(g * per, (g + 1) * per):
            arrived += [x_slots[k], d_slots[k]]
        kept = hidden_group(g, groups, arrived, mlp_w, kept)
        while len(x_slots) < chips:
            x_slots.append(ring_step(after(x_slots[-1], kept[0])))
        kept_oth = hidden_group(g, groups, None, mlp_w_oth, kept_oth, kept[:2])
        own, other = list(kept[2:]), list(kept_oth)
        if g == 0:
            own[0] = after(own[0], x_slots[min(2, chips - 1)])
        elif g == 1:
            back_first = ring_step(back_parts[1])
            own[0] = after(own[0], back_first)
        back, out = mlp_back(g, groups, own, other, mlp_w, mlp_w_oth)
        for i in range(per):
            rows = slice(i * own_rows, (i + 1) * own_rows)
            back_parts.append(back[rows])
            out_slots.append(out[rows].astype(F32))
    total, steps = back_parts[1 % chips].astype(F32), []
    for k in range(2, chips + 1):
        low = total.astype(BF16)
        if k == 3:
            kept = [after(array, low) for array in kept]
        steps.append(back_first if k == 2 and groups > 1 else ring_step(low))
        total = steps[-1].astype(F32) + back_parts[k % chips].astype(F32)
    d_normed = total
    x_all, d_all = kept[:2]

    def rows_product(left, right):
        return jnp.einsum("ri,rj->ij", left, right, preferred_element_type=F32).astype(BF16)

    def seq_sum(array, axis):
        return lax.psum_scatter(array, "seq", scatter_dimension=axis, tiled=True).astype(F32)

    products = [(rows_product(kept[2], d_all), rows_product(kept_oth[0], d_all))]
    for i in range(2):
        products.append(
            [
                rows_product(x_all, after(array, *steps[1 : 1 + i]))
                for array in (kept[3 + i], kept_oth[1 + i])
            ]
        )
    sums = [
        (own.astype(F32) + swap_core(other).astype(F32)).astype(BF16) for own, other in products
    ]
    grad_down, grad_gate, grad_up = (
        seq_sum(array, axis) for array, axis in zip(sums, (1, 0, 0))
    )

    plain_m = residual * inverse_m
    back_m, gain_m_part = rms_back(d_normed, plain_m, inverse_m, gain_m)
    d_resid = d_output + back_m
    d_low = d_resid.astype(BF16)
    out_sum = out_slots[1 % chips]
    for k in range(2, chips):
        waits = [d_low]
        if k > 2:
            waits = [do_mine]
        out_sums.append(ring_step(after(out_sum.astype(BF16), *waits)))
        out_sum = out_sums[-1].astype(F32) + out_slots[k]
        if k == 2:
            do_mine, do_other, d_half = d_attended(
                core_ref,
                mine(d_low, 1),
                swap_core(others(d_low, 1)),
                after(attn_w, *sum(map(list, products), [])),
                batches,
            )
    d_query, *d_kv_slots = attend_back(
        q,
        kv_slots,
        do_mine,
        after(swap_core(do_other), out_sums[0], *sums),
        lse,
        limits,
        kpos,
        qpos,
        cosine,
        sine,
    )

    def owner_sum(chunks, route, *waits):
        summed = cube_scatter(chunks, route, *waits)
        rows = 2 * shard
        return ring_scatter([summed[k * rows : (k + 1) * rows] for k in range(chips)])

    def own_shard(summed, lanes):
        received = swap_core(others(summed, 0))
        kept_rows = mine(summed, 0)
        edges = [sum(lanes[:i]) for i in range(len(lanes) + 1)]
        return [
            by_core(kept_rows[:, lo:hi], received[:, lo:hi], 1)
            for lo, hi in zip(edges[:-1], edges[1:])
        ]

    passing = [ring_step(after(d_kv_slots[1], *out_sums[1:2]))]
    for k in range(2, chips):
        total = passing[-1].astype(F32) + d_kv_slots[k].astype(F32)
        passing.append(ring_step(total.astype(BF16)))
    grad_out = owner_sum(
        grad_chunks(out_starts, [attended, attended_oth], d_half, seq_size, chips), 1, passing[0]
    )
    (grad_out,) = own_shard(grad_out, [out_half])
    grad_query = owner_sum(grad_chunks(starts, [normed_a], d_query, seq_size, chips), 0)
    (grad_query,) = own_shard(grad_query, [query_half])
    out_last = ring_step(after(out_sum.astype(BF16), passing[1]))
    d_kv = unrotate(passing[-1], d_kv_slots[0], cosine_all, sine_all)
    d_normed_a, d_normed_oth = d_normed_rows(core_ref, d_query, d_kv, attn_w, out_half, batches)
    d_kv = after(d_kv, d_normed_oth)
    d_normed_a = d_normed_a + swap_core(d_normed_oth).astype(F32)
    x_own_f = x_own.astype(F32)
    inverse_a = rms_inverse(x_own_f)
    back_a, gain_a_part = rms_back(d_normed_a, x_own_f * inverse_a, inverse_a, gain_a)
    input_grad = d_resid + back_a
    gain_sum = jnp.concatenate([gain_a_part, gain_m_part], 0)
    gain_sum = gain_sum + swap_core(gain_sum)
    bit = 1
    while bit < seq_size:
        gain_sum = gain_sum + swap_seq(gain_sum, bit)
        bit *= 2
    gain_part = gain_sum
    for _ in range(chips - 1):
        gain_part = ring_step(gain_part)
        gain_sum = gain_sum + gain_part
    grad_kv = owner_sum(grad_chunks(starts, [normed_a], d_kv, seq_size, chips), 1)
    kv_parts = own_shard(after(grad_kv, gain_sum), [LANES] * (2 * kv_half // LANES))
    grad_kv = [
        jnp.concatenate(
            [part[:, :LANES] for part in kv_parts[i::2]]
            + [part[:, LANES:] for part in kv_parts[i::2]],
            axis=1,
        )
        for i in range(2)
    ]
    gain_sum = lax.dynamic_slice_in_dim(gain_sum, (seq_at * ctx_size + ctx_at) * shard, shard, 1)

    branch_m = out_slots[0] + out_last.astype(F32)
    activations = (residual + branch_m).astype(BF16)
    return (
        activations.reshape(tokens.shape),
        input_grad.reshape(tokens.shape),
        gain_sum[0],
        grad_query,
        grad_kv[0],
        grad_kv[1],
        grad_out,
        gain_sum[1],
        grad_gate,
        grad_up,
        grad_down,
    )


def solution(mesh):
    rows = P(None, "seq", "ctx", None)
    spread = P(("seq", "ctx"))
    spread_rows = P(("seq", "ctx"), None)
    return jax.shard_map(
        body,
        mesh=mesh,
        in_specs=(
            rows,
            P(None, "seq"),
            rows,
            spread,
            spread_rows,
            spread_rows,
            spread_rows,
            spread_rows,
            spread,
            P("seq", "ctx"),
            P("seq", "ctx"),
            P("ctx", "seq"),
        ),
        out_specs=(
            rows,
            rows,
            spread,
            spread_rows,
            spread_rows,
            spread_rows,
            spread_rows,
            spread,
            P("seq", "ctx"),
            P("seq", "ctx"),
            P("ctx", "seq"),
        ),
        check_vma=False,
    )
```

```python
import functools
import math

import jax
import jax.numpy as jnp
from jax import lax
from jax.experimental import pallas as pl
from jax.experimental.pallas import tpu as pltpu
from jax.sharding import PartitionSpec as P

HEAD_DIM = 64
LANES = 128
EPSILON = 1e-05
ROPE_BASE = 500000.0
MASKED = -1e30
WEIGHT = 6
VMEM_LIMIT = 56 * 1024 * 1024
F32 = jnp.float32
BF16 = jnp.bfloat16


def folded_order(count):
    return list(range(0, count, 2)) + list(range(1, count, 2))[::-1]


def swap_core(array):
    ctx = lax.axis_size("ctx")
    return lax.ppermute(array, "ctx", [(i, i ^ 1) for i in range(ctx)])


def swap_seq(array, bit):
    seq = lax.axis_size("seq")
    return lax.ppermute(array, "seq", [(i, i ^ bit) for i in range(seq)])


def ring_step(array):
    chips = lax.axis_size("ctx") // 2
    order = folded_order(chips)
    pairs = [
        (order[i] * 2 + core, order[(i + 1) % chips] * 2 + core)
        for i in range(chips)
        for core in range(2)
    ]
    return lax.ppermute(array, "ctx", pairs)


def ring_gather(array):
    slots = [array]
    for _ in range(lax.axis_size("ctx") // 2 - 1):
        slots.append(ring_step(slots[-1]))
    return slots


def ring_scatter(parts):
    chips = len(parts)
    total = parts[1 % chips].astype(F32)
    for k in range(2, chips + 1):
        total = ring_step(total.astype(BF16)).astype(F32) + parts[k % chips].astype(F32)
    return total


def cube_gather(array, route):
    seq = lax.axis_size("seq")
    bits = [1 << i for i in range(seq.bit_length() - 1)]
    pieces = {0: array}
    for bit in bits if route == 0 else bits[::-1]:
        pieces.update({r ^ bit: swap_seq(piece, bit) for r, piece in pieces.items()})
    return [pieces[r] for r in range(seq)]


def cube_scatter(chunks, route, *waits):
    seq = lax.axis_size("seq")
    bits = [1 << i for i in range(seq.bit_length() - 1)]
    held = dict(enumerate(chunks))
    for bit in bits if route == 0 else bits[::-1]:
        seen = waits if len(held) > 2 else ()
        held = {
            r: held[r].astype(F32)
            + after(swap_seq(held[r ^ bit].astype(BF16), bit), *seen).astype(F32)
            for r in held
            if not r & bit
        }
    return held[0]


def after(array, *others):
    return lax.optimization_barrier((array, *others))[0]


def scaled_frequency():
    half_dim = HEAD_DIM // 2
    base_freq = ROPE_BASE ** (-jnp.arange(half_dim, dtype=F32) * 2.0 / HEAD_DIM)
    wave = 2.0 * math.pi / base_freq
    smooth = (8192.0 / wave - 1.0) / 3.0
    middle = (1.0 - smooth) * base_freq / 32.0 + smooth * base_freq
    return jnp.where(wave < 2048.0, base_freq, jnp.where(wave > 8192.0, base_freq / 32.0, middle))


def rope_tables(positions):
    angles = positions.astype(F32)[:, None] * scaled_frequency()[None, :]
    cosine, sine = jnp.cos(angles), jnp.sin(angles)
    return (
        jnp.concatenate([cosine] * 4, axis=1),
        jnp.concatenate([-sine, sine, -sine, sine], axis=1),
    )


def rotate_lanes(values, cosine, sine):
    lane = lax.broadcasted_iota(jnp.int32, values.shape, 1)
    partner = jnp.where(
        (lane % HEAD_DIM) < HEAD_DIM // 2,
        pltpu.roll(values, LANES - HEAD_DIM // 2, 1),
        pltpu.roll(values, HEAD_DIM // 2, 1),
    )
    return values * cosine + partner * sine


SMEM = pltpu.SMEM
ANYWHERE = pl.BlockSpec(memory_space=pl.ANY)
SCALARS = pl.BlockSpec(memory_space=pltpu.SMEM)
PARAMS = pltpu.CompilerParams(vmem_limit_bytes=VMEM_LIMIT)
NT = (((1,), (1,)), ((), ()))


def cost(flops, nbytes, transcendentals=0):
    return pl.CostEstimate(
        flops=int(WEIGHT * flops), bytes_accessed=int(nbytes), transcendentals=int(transcendentals)
    )


def dot(left, right):
    return jnp.dot(left, right, preferred_element_type=F32)


def dot_nt(left, right):
    return lax.dot_general(left, right, NT, preferred_element_type=F32)


def transposed(values):
    return values.astype(F32).T.astype(BF16)


def pack_kernel(kv_half, core_ref, wq, wk, wv, wo, gains, mine, other):
    def fill(out, which):
        at = 0
        for source in (wo, wq):
            half = source.shape[1] // 2
            out[:, at : at + half] = source[:, which * half : (which + 1) * half]
            at += half
        for i in range(kv_half // LANES):
            for source in (wk, wv):
                lo = which * kv_half + i * LANES
                out[:, at : at + LANES] = source[:, lo : lo + LANES]
                at += LANES
        out[:, at : at + LANES] = gains[...]

    for core in range(2):

        @pl.when(core_ref[0] == core)
        def _():
            fill(mine, core)
            fill(other, 1 - core)


def pack(core, wq, wk, wv, wo, gains):
    rows = wq.shape[0]
    width = (wq.shape[1] + wk.shape[1] + wv.shape[1] + wo.shape[1]) // 2 + LANES
    shape = jax.ShapeDtypeStruct((rows, width), BF16)
    whole = [pl.BlockSpec(memory_space=pltpu.VMEM)] * 5
    return pl.pallas_call(
        functools.partial(pack_kernel, wk.shape[1] // 2),
        in_specs=[SCALARS] + whole,
        out_shape=[shape, shape],
        compiler_params=PARAMS,
        cost_estimate=cost(0, 8 * rows * width),
    )(core, wq, wk, wv, wo, gains)


def stack_kernel(edges, core_ref, mine, other, *outs):
    rows = mine.shape[0]
    for core in range(2):

        @pl.when(core_ref[0] == core)
        def _():
            for source, at in ((mine, core), (other, 1 - core)):
                for i, out in enumerate(outs):
                    out[at * rows : (at + 1) * rows] = source[:, edges[i] : edges[i + 1]]


def stack_pieces(core, mine, other, widths):
    rows = mine.shape[0]
    edges = [sum(widths[:i]) for i in range(len(widths) + 1)]
    return pl.pallas_call(
        functools.partial(stack_kernel, edges),
        in_specs=[SCALARS] + [pl.BlockSpec(memory_space=pltpu.VMEM)] * 2,
        out_shape=[jax.ShapeDtypeStruct((2 * rows, width), BF16) for width in widths],
        compiler_params=PARAMS,
        cost_estimate=cost(0, 8 * mine.size),
    )(core, mine, other)


def placing(starts, pieces, w, sems):
    return [
        pltpu.make_async_copy(
            piece, w.at[pl.ds(pl.multiple_of(starts[i], 16), piece.shape[0])], sems.at[i]
        )
        for i, piece in enumerate(pieces)
    ]


def kv_kernel(count, batches, *refs):
    core_ref, starts, x_own, x_oth, cos_ref, sin_ref = refs[:6]
    pieces = refs[6 : 6 + count]
    kv_ref, normed, gains_ref, w_out, w, sems = refs[6 + count :]
    first = w.shape[1] - LANES - kv_ref.shape[1]
    slots = normed.shape[0] // (2 * batches)
    arriving = placing(starts, pieces, w, sems)
    for copy in arriving:
        copy.start()
    for copy in arriving:
        copy.wait()
    leaving = pltpu.make_async_copy(w, w_out, sems.at[count])
    leaving.start()
    table = w[:, w.shape[1] - LANES :].astype(F32).T
    gains_ref[...] = table[:8]
    for source, which in ((x_own, core_ref[0]), (x_oth, 1 - core_ref[0])):
        for b in range(batches):
            x = source[b * slots : (b + 1) * slots].astype(F32)
            inverse = lax.rsqrt(jnp.mean(x * x, axis=-1, keepdims=True) + EPSILON)
            at = pl.multiple_of((2 * b + which) * slots, slots)
            normed[pl.ds(at, slots)] = (x * inverse * table[:1]).astype(BF16)
    block = 2 * LANES
    for at in range(0, kv_ref.shape[1], block):
        raw = dot(normed[...], w[:, first + at : first + at + block])
        turned = rotate_lanes(raw[:, :LANES], cos_ref[...], sin_ref[...])
        kv_ref[:, at : at + LANES] = turned.astype(BF16)
        kv_ref[:, at + LANES : at + block] = raw[:, LANES:].astype(BF16)
    leaving.wait()


def project_kv(core, starts, x_own, x_oth, cosine, sine, pieces, batches, kv_width):
    rows, depth = 2 * x_own.shape[0], x_own.shape[1]
    width = pieces[0].shape[1]
    count = len(pieces)
    vmem = pl.BlockSpec(memory_space=pltpu.VMEM)
    return pl.pallas_call(
        functools.partial(kv_kernel, count, batches),
        in_specs=[SCALARS, SCALARS] + [vmem] * 4 + [ANYWHERE] * count,
        out_specs=[vmem, vmem, vmem, ANYWHERE],
        out_shape=[
            jax.ShapeDtypeStruct((rows, kv_width), BF16),
            jax.ShapeDtypeStruct((rows, depth), BF16),
            jax.ShapeDtypeStruct((8, depth), F32),
            jax.ShapeDtypeStruct((depth, width), BF16),
        ],
        scratch_shapes=[
            pltpu.VMEM((depth, width), BF16),
            pltpu.SemaphoreType.DMA((count + 1,)),
        ],
        compiler_params=PARAMS,
        cost_estimate=cost(2 * rows * depth * width, 4 * rows * depth + 4 * depth * width),
    )(core, starts, x_own, x_oth, cosine, sine, *pieces)


def q_kernel(first, normed, cos_ref, sin_ref, w, q_ref, held, sems):
    block = 2 * LANES
    width = q_ref.shape[1]
    copies = [
        pltpu.make_async_copy(
            w.at[:, pl.ds(first + at, block)], held.at[:, pl.ds(at, block)], sems.at[at // block]
        )
        for at in range(0, width, block)
    ]
    for copy in copies:
        copy.start()
    for at in range(0, width, block):
        copies[at // block].wait()
        raw = dot(normed[...], held[:, at : at + block])
        for lo in range(0, block, LANES):
            turned = rotate_lanes(raw[:, lo : lo + LANES], cos_ref[...], sin_ref[...])
            q_ref[:, at + lo : at + lo + LANES] = (turned / math.sqrt(HEAD_DIM)).astype(BF16)


def project_q(normed, cosine, sine, w, first, width):
    rows, depth = normed.shape
    vmem = pl.BlockSpec(memory_space=pltpu.VMEM)
    return pl.pallas_call(
        functools.partial(q_kernel, first),
        in_specs=[vmem] * 3 + [ANYWHERE],
        out_specs=vmem,
        out_shape=jax.ShapeDtypeStruct((rows, width), BF16),
        scratch_shapes=[
            pltpu.VMEM((depth, width), BF16),
            pltpu.SemaphoreType.DMA((width // (2 * LANES),)),
        ],
        compiler_params=PARAMS,
        cost_estimate=cost(2 * rows * depth * width, 2 * rows * depth + 4 * depth * width),
    )(normed, cosine, sine, w)


def set_bias(limit_ref, kpos_ref, qpos_ref, bias):
    @pl.when(pl.program_id(1) == 0)
    def _():
        limit = limit_ref[pl.program_id(0)]
        allowed = (kpos_ref[...] <= qpos_ref[...]) & (kpos_ref[...] < limit)
        bias[...] = jnp.where(allowed, 0.0, MASKED)


def attend_kernel(chips, limit_ref, kpos_ref, qpos_ref, q_ref, *refs):
    slots, (out_ref, lse_ref, bias) = refs[:chips], refs[chips:]
    set_bias(limit_ref, kpos_ref, qpos_ref, bias)
    heads = q_ref.shape[1] // HEAD_DIM
    kv = jnp.concatenate([slot[...] for slot in slots], axis=0)
    q_t = transposed(q_ref[...])
    v_t = transposed(kv[:, LANES:])
    outs = []
    for h in range(heads):
        a = h * 2 // heads
        k_h = kv[:, a * HEAD_DIM : (a + 1) * HEAD_DIM]
        scores = dot(k_h, q_t[h * HEAD_DIM : (h + 1) * HEAD_DIM]) + bias[...]
        top = jnp.max(scores, axis=0, keepdims=True)
        shifted = jnp.exp(scores - top)
        total = jnp.sum(shifted, axis=0, keepdims=True)
        out_t = dot(v_t[a * HEAD_DIM : (a + 1) * HEAD_DIM], shifted.astype(BF16))
        outs.append(out_t / total)
        lse_ref[h : h + 1, :] = top + jnp.log(total)
    out_ref[...] = jnp.concatenate(outs, axis=0).T.astype(BF16)


def attention_specs(batches, chips, rows, keys, width, heads, pairs):
    def at(shape):
        return pl.BlockSpec(shape, lambda b, i, n: (b, i))

    return (
        [
            pl.BlockSpec((keys, 1), lambda b, i, n: (0, 0)),
            pl.BlockSpec((1, rows), lambda b, i, n: (0, 0)),
            at((rows, width)),
        ]
        + [at((rows, 2 * LANES))] * chips,
        at((rows, width)),
        pl.BlockSpec((heads, rows), lambda b, i, n: (b * pairs + i, 0)),
    )


def attend(q, kv_slots, limits, kpos, qpos):
    rows, keys, batches, chips = qpos.shape[1], kpos.shape[0], limits.shape[0], len(kv_slots)
    pairs = kv_slots[0].shape[1] // (2 * LANES)
    width = q.shape[1] // pairs
    heads = width // HEAD_DIM
    ins, out, lse = attention_specs(batches, chips, rows, keys, width, heads, pairs)
    return pl.pallas_call(
        functools.partial(attend_kernel, chips),
        grid_spec=pltpu.PrefetchScalarGridSpec(
            num_scalar_prefetch=1,
            grid=(batches, pairs),
            in_specs=ins,
            out_specs=[out, lse],
            scratch_shapes=[pltpu.VMEM((keys, rows), F32)],
        ),
        out_shape=[
            jax.ShapeDtypeStruct(q.shape, BF16),
            jax.ShapeDtypeStruct((batches * pairs * heads, rows), F32),
        ],
        compiler_params=PARAMS,
        cost_estimate=cost(
            16 * batches * rows * keys * q.shape[1],
            4 * q.size + 2 * chips * kv_slots[0].size,
            batches * rows * keys * q.shape[1] // HEAD_DIM,
        ),
    )(limits, kpos, qpos, q, *kv_slots)


def attend_back_kernel(chips, limit_ref, kpos_ref, qpos_ref, q_ref, *refs):
    slots = refs[:chips]
    do_mine, do_other, lse_ref, cos_ref, sin_ref, dq_ref = refs[chips : chips + 6]
    d_slots, bias = refs[chips + 6 : 2 * chips + 6], refs[2 * chips + 6]
    set_bias(limit_ref, kpos_ref, qpos_ref, bias)
    rows, width = q_ref.shape
    heads = width // HEAD_DIM
    per_kv = heads // 2
    kv = jnp.concatenate([slot[...] for slot in slots], axis=0)
    d_out = (do_mine[...] + do_other[...].astype(F32)).astype(BF16)
    q_t = transposed(q_ref[...])
    do_t = transposed(d_out)
    k_t = transposed(kv[:, :LANES])
    lane = lax.broadcasted_iota(jnp.int32, (kv.shape[0], LANES), 1)
    d_queries = []
    d_keys, d_values = [], []
    for a in range(2):
        k_h = kv[:, a * HEAD_DIM : (a + 1) * HEAD_DIM]
        v_h = kv[:, LANES + a * HEAD_DIM : LANES + (a + 1) * HEAD_DIM]
        dk_sum, dv_sum = [None, None], [None, None]
        for g in range(per_kv):
            h = a * per_kv + g
            head = slice(h * HEAD_DIM, (h + 1) * HEAD_DIM)
            pair = slice((h // 2) * LANES, (h // 2 + 1) * LANES)
            scores = dot(k_h, q_t[head]) + bias[...]
            probs = jnp.exp(scores - lse_ref[h : h + 1, :])
            d_probs = dot(v_h, do_t[head])
            mean = jnp.sum(d_probs * probs, axis=0, keepdims=True)
            d_scores = (probs * (d_probs - mean)).astype(BF16)
            d_queries.append(dot(k_t[a * HEAD_DIM : (a + 1) * HEAD_DIM], d_scores))
            dk_term = dot(d_scores, q_ref[:, pair])
            dv_term = dot(probs.astype(BF16), d_out[:, pair])
            e = h % 2
            dk_sum[e] = dk_term if dk_sum[e] is None else dk_sum[e] + dk_term
            dv_sum[e] = dv_term if dv_sum[e] is None else dv_sum[e] + dv_term
        for sums, kept in ((dk_sum, d_keys), (dv_sum, d_values)):
            mixed = jnp.where(lane < HEAD_DIM, sums[0], sums[1])
            kept.append(mixed + pltpu.roll(mixed, HEAD_DIM, 1))
    d_key = jnp.where(lane < HEAD_DIM, d_keys[0], d_keys[1])
    d_value = jnp.where(lane < HEAD_DIM, d_values[0], d_values[1])
    for k, d_slot in enumerate(d_slots):
        d_slot[:, :LANES] = d_key[k * rows : (k + 1) * rows].astype(BF16)
        d_slot[:, LANES:] = d_value[k * rows : (k + 1) * rows].astype(BF16)
    d_query = jnp.concatenate(d_queries, axis=0).T
    for at in range(width // LANES):
        cut = slice(at * LANES, (at + 1) * LANES)
        turned = rotate_lanes(d_query[:, cut], cos_ref[...], -sin_ref[...])
        dq_ref[:, cut] = (turned / math.sqrt(HEAD_DIM)).astype(BF16)


def attend_back(q, kv_slots, do_mine, do_other, lse, limits, kpos, qpos, cosine, sine):
    rows, keys, batches, chips = qpos.shape[1], kpos.shape[0], limits.shape[0], len(kv_slots)
    pairs = kv_slots[0].shape[1] // (2 * LANES)
    width = q.shape[1] // pairs
    heads = width // HEAD_DIM
    ins, out, lse_spec = attention_specs(batches, chips, rows, keys, width, heads, pairs)
    table = pl.BlockSpec((rows, LANES), lambda b, i, n: (0, 0))
    return pl.pallas_call(
        functools.partial(attend_back_kernel, chips),
        grid_spec=pltpu.PrefetchScalarGridSpec(
            num_scalar_prefetch=1,
            grid=(batches, pairs),
            in_specs=ins + [out, out, lse_spec, table, table],
            out_specs=[out] + ins[3 : 3 + chips],
            scratch_shapes=[pltpu.VMEM((keys, rows), F32)],
        ),
        out_shape=[jax.ShapeDtypeStruct(q.shape, BF16)]
        + [jax.ShapeDtypeStruct(slot.shape, BF16) for slot in kv_slots],
        compiler_params=PARAMS,
        cost_estimate=cost(
            40 * batches * rows * keys * q.shape[1],
            10 * q.size + 4 * chips * kv_slots[0].size,
            batches * rows * keys * q.shape[1] // HEAD_DIM,
        ),
    )(limits, kpos, qpos, q, *kv_slots, do_mine, do_other, lse, cosine, sine)


def unrotate_kernel(last_ref, own_ref, cos_ref, sin_ref, out_ref):
    total = last_ref[...].astype(F32) + own_ref[...].astype(F32)
    for at in range(total.shape[1] // LANES):
        cut = slice(at * LANES, (at + 1) * LANES)
        part = total[:, cut]
        if at % 2 == 0:
            part = rotate_lanes(part, cos_ref[...], -sin_ref[...])
        out_ref[:, cut] = part.astype(BF16)


def unrotate(last, own, cosine, sine):
    return pl.pallas_call(
        unrotate_kernel,
        out_shape=jax.ShapeDtypeStruct(own.shape, BF16),
        compiler_params=PARAMS,
        cost_estimate=cost(0, 6 * own.size),
    )(last, own, cosine, sine)


def split_rows(batches, core_ref, acc, own, other):
    slots = acc.shape[0] // (2 * batches)
    for out, which in ((own, core_ref[0]), (other, 1 - core_ref[0])):
        for b in range(batches):
            at = pl.multiple_of((2 * b + which) * slots, slots)
            out[b * slots : (b + 1) * slots] = acc[pl.ds(at, slots)].astype(out.dtype)


def out_kernel(batches, core_ref, o_mine, o_other, w_all, own, other, w, acc, sems):
    half, width = o_mine.shape[1], w.shape[1]
    block = 2 * LANES
    copies = [
        pltpu.make_async_copy(
            w_all.at[:, pl.ds(lo, block)], w.at[:, pl.ds(lo, block)], sems.at[lo // block]
        )
        for lo in range(0, width, block)
    ]
    for copy in copies:
        copy.start()
    rows_mine = pl.ds(pl.multiple_of(core_ref[0] * half, half), half)
    rows_other = pl.ds(pl.multiple_of((1 - core_ref[0]) * half, half), half)
    for lo in range(0, width, block):
        cut = slice(lo, lo + block)
        copies[lo // block].wait()
        acc[:, cut] = dot(o_mine[...], w[rows_mine, cut]) + dot(o_other[...], w[rows_other, cut])
    split_rows(batches, core_ref, acc, own, other)


def project_out(core, o_mine, o_other, w, width, batches):
    rows, half = o_mine.shape
    vmem = pl.BlockSpec(memory_space=pltpu.VMEM)
    part = jax.ShapeDtypeStruct((rows // 2, width), F32)
    return pl.pallas_call(
        functools.partial(out_kernel, batches),
        in_specs=[SCALARS, vmem, vmem, ANYWHERE],
        out_specs=[vmem, vmem],
        out_shape=[part, part],
        scratch_shapes=[
            pltpu.VMEM((2 * half, width), BF16),
            pltpu.VMEM((rows, width), F32),
            pltpu.SemaphoreType.DMA((width // (2 * LANES),)),
        ],
        compiler_params=PARAMS,
        cost_estimate=cost(4 * rows * half * width, 4 * half * width + 12 * rows * width),
    )(core, o_mine, o_other, w)


def hidden_units(x, d, gate, up, down_t, hidden_ref, d_gate_ref, d_up_ref):
    gate_val = dot(x[...], gate[...])
    up_val = dot(x[...], up[...])
    d_hidden = dot(d[...], down_t[...])
    sigmoid_g = 1.0 / (1.0 + jnp.exp(-gate_val))
    activated = gate_val * sigmoid_g
    slope = sigmoid_g * (1.0 + gate_val * (1.0 - sigmoid_g))
    hidden_ref[...] = (activated * up_val).astype(BF16)
    d_gate_ref[...] = (d_hidden * up_val * slope).astype(BF16)
    d_up_ref[...] = (d_hidden * activated).astype(BF16)


def first_hidden_kernel(per, filled, *refs):
    arrived = refs[: 2 * per]
    weights = refs[2 * per : 2 * per + 3]
    x, d, hidden_ref, d_gate_ref, d_up_ref, sems = refs[2 * per + 3 + filled :]
    rows = arrived[0].shape[0]

    @pl.when(pl.program_id(0) == 0)
    def _():
        copies = [
            pltpu.make_async_copy(
                arrived[2 * i + j], out.at[pl.ds(i * rows, rows)], sems.at[2 * i + j]
            )
            for i in range(per)
            for j, out in enumerate((x, d))
        ]
        for copy in copies:
            copy.start()
        for copy in copies:
            copy.wait()

    hidden_units(x, d, *weights, hidden_ref, d_gate_ref, d_up_ref)


def second_hidden_kernel(filled, x, d, gate, up, down_t, *refs):
    hidden_units(x, d, gate, up, down_t, *refs[filled:])


def hidden_group(at, groups, arrived, weights, kept, rows_of=None):
    width = weights.shape[0]
    hidden_width = weights.shape[1] // 3
    tile = 2 * LANES
    tiles = hidden_width // tile
    if rows_of is None:
        height = arrived[0].shape[0] * len(arrived) // 2
        per = len(arrived) // 2
        total = height * groups
        sources, source_specs = arrived, [ANYWHERE] * len(arrived)
        wide = [jax.ShapeDtypeStruct((total, width), BF16)] * 2
        scratch = [pltpu.SemaphoreType.DMA((2 * per,))]
    else:
        total = rows_of[0].shape[0]
        height = total // groups
        sources = list(rows_of)
        source_specs = [pl.BlockSpec((height, width), lambda j: (at, 0))] * 2
        wide, scratch = [], []
    narrow = [jax.ShapeDtypeStruct((total, hidden_width), BF16)] * 3
    filled = 0 if kept is None else len(wide) + 3
    kernel = (
        functools.partial(first_hidden_kernel, per, filled)
        if rows_of is None
        else functools.partial(second_hidden_kernel, filled)
    )
    first = len(sources) + 3
    return pl.pallas_call(
        kernel,
        grid=(tiles,),
        in_specs=source_specs
        + [
            pl.BlockSpec((width, tile), lambda j, skipped=i * tiles: (0, skipped + j))
            for i in range(3)
        ]
        + [ANYWHERE] * filled,
        out_specs=[pl.BlockSpec((height, width), lambda j: (at, 0))] * len(wide)
        + [pl.BlockSpec((height, tile), lambda j: (at, j))] * 3,
        out_shape=wide + narrow,
        scratch_shapes=scratch,
        input_output_aliases={first + i: i for i in range(filled)},
        compiler_params=PARAMS,
        cost_estimate=cost(
            6 * height * width * hidden_width,
            6 * width * hidden_width + 12 * height * width,
            height * hidden_width,
        ),
    )(*sources, weights, weights, weights, *([] if kept is None else kept))


def mlp_back_kernel(*refs):
    parts, weights = (refs[:3], refs[3:6]), refs[6:8]
    back_ref, out_ref, held_own, held_oth, sems = refs[8:]
    width, count = back_ref.shape[1], refs[0].shape[1]
    block = 4 * LANES
    steps = width // block
    copies = [
        pltpu.make_async_copy(
            weight.at[pl.ds(lo, block)],
            held.at[pl.ds(lo, block)],
            sems.at[i * steps + lo // block],
        )
        for i, (weight, held) in enumerate(zip(weights, (held_own, held_oth)))
        for lo in range(0, width, block)
    ]
    for step in range(steps):
        for i in range(2):
            copies[i * steps + step].start()
    for step in range(steps):
        cut = slice(step * block, (step + 1) * block)
        back, out = 0.0, 0.0
        for i, held in enumerate((held_own, held_oth)):
            copies[i * steps + step].wait()
            hidden, d_gate, d_up = parts[i]
            back += dot_nt(d_gate[...], held[cut, :count])
            back += dot_nt(d_up[...], held[cut, count : 2 * count])
            out += dot_nt(hidden[...], held[cut, 2 * count :])
        back_ref[:, cut] = back.astype(BF16)
        out_ref[:, cut] = out.astype(BF16)


def mlp_back(at, groups, own, other, weights, weights_oth):
    height, hidden_width = own[0].shape[0] // groups, own[0].shape[1]
    width = weights.shape[0]
    return pl.pallas_call(
        mlp_back_kernel,
        grid=(1,),
        in_specs=[pl.BlockSpec((height, hidden_width), lambda j: (at, 0))] * 6 + [ANYWHERE] * 2,
        out_specs=[pl.BlockSpec((height, width), lambda j: (0, 0))] * 2,
        out_shape=[jax.ShapeDtypeStruct((height, width), BF16)] * 2,
        scratch_shapes=[
            pltpu.VMEM(weights.shape, BF16),
            pltpu.VMEM(weights.shape, BF16),
            pltpu.SemaphoreType.DMA((2 * (width // (4 * LANES)),)),
        ],
        compiler_params=PARAMS,
        cost_estimate=cost(
            12 * height * width * hidden_width, 12 * width * hidden_width + 14 * height * width
        ),
    )(*own, *other, weights, weights_oth)


def d_attended_kernel(batches, other_blocks, core_ref, d_own, d_oth, w_ref, mine, other, d_rows):
    step = pl.program_id(0)
    slots = d_own.shape[0] // batches

    @pl.when(step == 0)
    def _():
        for source, which in ((d_own, core_ref[0]), (d_oth, 1 - core_ref[0])):
            for b in range(batches):
                at = pl.multiple_of((2 * b + which) * slots, slots)
                d_rows[pl.ds(at, slots)] = source[b * slots : (b + 1) * slots]

    term = dot_nt(d_rows[...], w_ref[...])

    @pl.when(step < other_blocks)
    def _():
        other[...] = term.astype(BF16)

    @pl.when(step >= other_blocks)
    def _():
        mine[...] = term


def d_attended(core, d_own, d_oth, w, batches):
    rows, width = 2 * d_own.shape[0], d_own.shape[1]
    heads_width = w.shape[0]
    block = 2 * LANES
    blocks = heads_width // 2 // block

    def whole(shape):
        return pl.BlockSpec(shape, lambda j, c: (0, 0))

    return pl.pallas_call(
        functools.partial(d_attended_kernel, batches, blocks),
        grid_spec=pltpu.PrefetchScalarGridSpec(
            num_scalar_prefetch=1,
            grid=(2 * blocks,),
            in_specs=[
                whole(d_own.shape),
                whole(d_own.shape),
                pl.BlockSpec((block, width), lambda j, c: ((j + (1 - c[0]) * blocks) % (2 * blocks), 0)),
            ],
            out_specs=[
                pl.BlockSpec((rows, block), lambda j, c: (0, jnp.maximum(j - blocks, 0))),
                pl.BlockSpec((rows, block), lambda j, c: (0, jnp.minimum(j, blocks - 1))),
                whole((rows, width)),
            ],
        ),
        out_shape=[
            jax.ShapeDtypeStruct((rows, heads_width // 2), F32),
            jax.ShapeDtypeStruct((rows, heads_width // 2), BF16),
            jax.ShapeDtypeStruct((rows, width), BF16),
        ],
        compiler_params=PARAMS,
        cost_estimate=cost(
            2 * rows * width * heads_width, 2 * width * heads_width + 6 * rows * heads_width
        ),
    )(core, d_own, d_oth, w)


def grad_kernel(count, parts, chips, starts, *refs):
    sources, right, outs, turned = refs[:count], refs[count], refs[count + 1 : -1], refs[-1]
    shard = turned.shape[0] // (parts * chips)
    at = 0
    for source in sources:
        for lo in range(0, source.shape[1], 4 * LANES):
            turned[at : at + 4 * LANES] = transposed(source[:, lo : lo + 4 * LANES])
            at += 4 * LANES
    for r in range(parts):
        left = jnp.concatenate(
            [
                turned[pl.ds(pl.multiple_of(starts[r * chips + k], 16), shard)]
                for k in range(chips)
            ],
            axis=0,
        )
        outs[r][...] = dot(left, right[...]).astype(BF16)


def grad_chunks(starts, sources, right, parts, chips):
    rows = right.shape[0]
    depth = sum(source.shape[1] for source in sources)
    shape = jax.ShapeDtypeStruct((depth // parts, right.shape[1]), BF16)
    vmem = pl.BlockSpec(memory_space=pltpu.VMEM)
    return pl.pallas_call(
        functools.partial(grad_kernel, len(sources), parts, chips),
        in_specs=[SCALARS] + [vmem] * (len(sources) + 1),
        out_shape=[shape] * parts,
        scratch_shapes=[pltpu.VMEM((depth, rows), BF16)],
        compiler_params=PARAMS,
        cost_estimate=cost(
            2 * rows * depth * right.shape[1], 2 * rows * depth + 2 * depth * right.shape[1]
        ),
    )(starts, *sources, right)


def d_normed_kernel(batches, core_ref, dq_ref, dkv_ref, wq_ref, wkv_ref, own, other, acc):
    acc[...] = dot_nt(dq_ref[...], wq_ref[...]) + dot_nt(dkv_ref[...], wkv_ref[...])
    split_rows(batches, core_ref, acc, own, other)


def d_normed_rows(core, dq, dkv, w, first, batches):
    rows, depth = dq.shape[0], w.shape[0]
    width = dq.shape[1] + dkv.shape[1]
    block = 4 * LANES
    q_at, kv_at = first // dq.shape[1], (first + dq.shape[1]) // dkv.shape[1]

    def whole(shape):
        return pl.BlockSpec(shape, lambda j: (0, 0))

    part = pl.BlockSpec((rows // 2, block), lambda j: (0, j))
    return pl.pallas_call(
        functools.partial(d_normed_kernel, batches),
        grid=(depth // block,),
        in_specs=[
            SCALARS,
            whole(dq.shape),
            whole(dkv.shape),
            pl.BlockSpec((block, dq.shape[1]), lambda j: (j, q_at)),
            pl.BlockSpec((block, dkv.shape[1]), lambda j: (j, kv_at)),
        ],
        out_specs=[part, part],
        out_shape=[
            jax.ShapeDtypeStruct((rows // 2, depth), F32),
            jax.ShapeDtypeStruct((rows // 2, depth), BF16),
        ],
        scratch_shapes=[pltpu.VMEM((rows, block), F32)],
        compiler_params=PARAMS,
        cost_estimate=cost(2 * rows * depth * width, 2 * depth * width + 4 * rows * depth),
    )(core, dq, dkv, w, w)


def rms_inverse(values):
    return lax.rsqrt(jnp.mean(values * values, axis=-1, keepdims=True) + EPSILON)


def rms_back(grad_in, plain, inverse, gain):
    scaled = grad_in * gain
    back = inverse * (scaled - plain * jnp.mean(scaled * plain, axis=-1, keepdims=True))
    return (back, jnp.sum(grad_in * plain, axis=0, keepdims=True))


def body(
    tokens,
    lengths,
    cotangent,
    attn_gain,
    w_query,
    w_key,
    w_value,
    w_out,
    mlp_gain,
    w_gate,
    w_up,
    w_down,
):
    batches, _, slot_count, model_width = tokens.shape
    seq_size, ctx_size = lax.axis_size("seq"), lax.axis_size("ctx")
    chips = ctx_size // 2
    seq_at, ctx_at = lax.axis_index("seq"), lax.axis_index("ctx")
    chip_at, core = ctx_at // 2, ctx_at % 2
    core_ref = core.reshape(1).astype(jnp.int32)
    order = folded_order(chips)
    shard = w_query.shape[0]
    query_half, kv_half = w_query.shape[1] // 2, w_key.shape[1] // 2
    out_half = model_width // 2
    chip_rows = 2 * slot_count
    own_rows = batches * slot_count
    limits = lengths[:, 0]

    def chip_back(k):
        index = jnp.int32(0)
        for place, chip in enumerate(order):
            index = jnp.where(chip_at == chip, order[(place - k) % chips], index)
        return index

    slot_chip = jnp.stack([chip_back(k) for k in range(chips)])
    rank = (seq_at ^ jnp.arange(seq_size))[:, None] * chips + slot_chip[None, :]
    starts = (rank * (2 * shard)).reshape(-1).astype(jnp.int32)
    out_starts = (starts + core * query_half) % (2 * query_half)

    def half(array, which, axis):
        size = array.shape[axis] // 2
        return lax.dynamic_slice_in_dim(array, which * size, size, axis)

    def mine(array, axis):
        return half(array, core, axis)

    def others(array, axis):
        return half(array, 1 - core, axis)

    def by_core(own, other, axis):
        return jnp.where(
            core == 0,
            jnp.concatenate([own, other], axis),
            jnp.concatenate([other, own], axis),
        )

    q_positions = chip_at * chip_rows + jnp.arange(chip_rows)
    cosine, sine = rope_tables(q_positions)
    cosine_all, sine_all = jnp.tile(cosine, (batches, 1)), jnp.tile(sine, (batches, 1))
    qpos = q_positions[None, :]
    kpos = (slot_chip[:, None] * chip_rows + jnp.arange(chip_rows)[None, :]).reshape(-1, 1)
    own_pos = ctx_at * slot_count + jnp.arange(slot_count)
    valid = (own_pos[None, :] < limits[:, None]).astype(F32).reshape(own_rows, 1)
    d_output = cotangent.reshape(own_rows, model_width).astype(F32) * valid
    d_rows = d_output.astype(BF16)

    gains = jnp.concatenate(
        [attn_gain[:, None], mlp_gain[:, None], jnp.zeros((shard, LANES - 2), BF16)], axis=1
    )
    x_own = tokens.reshape(own_rows, model_width)
    x_oth = swap_core(x_own)
    packed, to_other = pack(core_ref, w_query, w_key, w_value, w_out, gains)
    (piece_a,) = stack_pieces(core_ref, packed, swap_core(to_other), [packed.shape[1]])
    d_slots = [d_rows, ring_step(d_rows)]
    ring_a, cubes_a = [after(piece_a, x_oth)], []
    for k in range(chips):
        cubes_a.append(cube_gather(ring_a[k], k % 2))
        if k + 1 < chips:
            seen = [cubes_a[k - 1][1], cubes_a[k - 1][2]] if k else d_slots[1:2]
            ring_a.append(ring_step(after(ring_a[k], *seen)))
    mlp_w = jnp.concatenate([w_gate, w_up, w_down.T], axis=1)
    mlp_w = lax.all_gather(after(mlp_w, *sum(cubes_a, [])), "seq", axis=0, tiled=True)

    def flat(cubes):
        return [cubes[k][r] for r in range(seq_size) for k in range(chips)]

    kv, normed_a, gain_rows, attn_w = project_kv(
        core_ref, starts, x_own, x_oth, cosine_all, sine_all, flat(cubes_a), batches, 2 * kv_half
    )
    gain_a, gain_m = gain_rows[0:1], gain_rows[1:2]
    kv_slots = ring_gather(kv)
    q = project_q(
        normed_a, cosine_all, sine_all, attn_w, out_half, query_half
    )
    d_slots.append(ring_step(after(d_slots[-1], kv_slots[-1])))
    attended, lse = attend(q, kv_slots, limits, kpos, qpos)
    attended_oth = swap_core(after(attended, d_slots[2 % chips]))
    branch, branch_oth = project_out(
        core_ref, attended, attended_oth, attn_w, out_half, batches
    )

    branch_oth = swap_core(branch_oth)
    residual = x_own.astype(F32) + by_core(branch, branch_oth, 1)
    inverse_m = rms_inverse(residual)
    normed_m = (residual * inverse_m * gain_m).astype(BF16)
    x_slots = [normed_m, ring_step(normed_m)]
    x_slots.append(ring_step(x_slots[1]))
    mlp_w_oth = swap_core(after(mlp_w, x_slots[1 % chips]))
    per = 2 if chips % 2 == 0 else 1
    groups = chips // per
    kept, kept_oth, back_parts, out_slots, out_sums = None, None, [], [], []
    for g in range(groups):
        arrived = []
        for k in range(g * per, (g + 1) * per):
            arrived += [x_slots[k], d_slots[k]]
        kept = hidden_group(g, groups, arrived, mlp_w, kept)
        if g == 0 and len(x_slots) < chips:
            d_slots.append(ring_step(after(d_slots[-1], kept[0])))
        kept_oth = hidden_group(g, groups, None, mlp_w_oth, kept_oth, kept[:2])
        while len(x_slots) < chips:
            x_slots.append(ring_step(after(x_slots[-1], d_slots[-1], kept_oth[0])))
            if len(d_slots) < chips:
                d_slots.append(ring_step(d_slots[-1]))
        own, other = list(kept[2:]), list(kept_oth)
        if g == 0:
            own[0] = after(own[0], x_slots[min(2, chips - 1)])
        elif g == 1:
            back_first = ring_step(back_parts[1])
            own[0] = after(own[0], back_first)
        back, out = mlp_back(g, groups, own, other, mlp_w, mlp_w_oth)
        for i in range(per):
            rows = slice(i * own_rows, (i + 1) * own_rows)
            back_parts.append(back[rows])
            out_slots.append(out[rows].astype(F32))
    total, steps = back_parts[1 % chips].astype(F32), []
    for k in range(2, chips + 1):
        low = total.astype(BF16)
        if k == 3:
            kept = [after(array, low) for array in kept]
        steps.append(back_first if k == 2 and groups > 1 else ring_step(low))
        total = steps[-1].astype(F32) + back_parts[k % chips].astype(F32)
    d_normed = total
    x_all, d_all = kept[:2]

    def rows_product(left, right):
        return jnp.einsum("ri,rj->ij", left, right, preferred_element_type=F32).astype(BF16)

    def seq_sum(array, axis):
        return lax.psum_scatter(array, "seq", scatter_dimension=axis, tiled=True).astype(F32)

    products = [(rows_product(kept[2], d_all), rows_product(kept_oth[0], d_all))]
    for i in range(2):
        products.append(
            [
                rows_product(x_all, after(array, *steps[1 : 1 + i]))
                for array in (kept[3 + i], kept_oth[1 + i])
            ]
        )
    sums = [
        (own.astype(F32) + swap_core(other).astype(F32)).astype(BF16) for own, other in products
    ]
    grad_down, grad_gate, grad_up = (
        seq_sum(array, axis) for array, axis in zip(sums, (1, 0, 0))
    )

    plain_m = residual * inverse_m
    back_m, gain_m_part = rms_back(d_normed, plain_m, inverse_m, gain_m)
    d_resid = d_output + back_m
    d_low = d_resid.astype(BF16)
    out_sum = out_slots[1 % chips]
    for k in range(2, chips):
        waits = [d_low]
        if k > 2:
            waits = [do_mine]
        out_sums.append(ring_step(after(out_sum.astype(BF16), *waits)))
        out_sum = out_sums[-1].astype(F32) + out_slots[k]
        if k == 2:
            do_mine, do_other, d_half = d_attended(
                core_ref,
                mine(d_low, 1),
                swap_core(others(d_low, 1)),
                after(attn_w, *sum(map(list, products), [])),
                batches,
            )
    d_query, *d_kv_slots = attend_back(
        q,
        kv_slots,
        do_mine,
        after(swap_core(do_other), out_sums[0], *sums),
        lse,
        limits,
        kpos,
        qpos,
        cosine,
        sine,
    )

    def owner_sum(chunks, route, *waits):
        summed = cube_scatter(chunks, route, *waits)
        rows = 2 * shard
        return ring_scatter([summed[k * rows : (k + 1) * rows] for k in range(chips)])

    def own_shard(summed, lanes):
        received = swap_core(others(summed, 0))
        kept_rows = mine(summed, 0)
        edges = [sum(lanes[:i]) for i in range(len(lanes) + 1)]
        return [
            by_core(kept_rows[:, lo:hi], received[:, lo:hi], 1)
            for lo, hi in zip(edges[:-1], edges[1:])
        ]

    passing = [ring_step(after(d_kv_slots[1], *out_sums[1:2]))]
    for k in range(2, chips):
        total = passing[-1].astype(F32) + d_kv_slots[k].astype(F32)
        passing.append(ring_step(total.astype(BF16)))
    grad_out = owner_sum(
        grad_chunks(out_starts, [attended, attended_oth], d_half, seq_size, chips), 1, passing[0]
    )
    (grad_out,) = own_shard(grad_out, [out_half])
    grad_query = owner_sum(grad_chunks(starts, [normed_a], d_query, seq_size, chips), 0)
    (grad_query,) = own_shard(grad_query, [query_half])
    out_last = ring_step(after(out_sum.astype(BF16), passing[1]))
    d_kv = unrotate(passing[-1], d_kv_slots[0], cosine_all, sine_all)
    d_normed_a, d_normed_oth = d_normed_rows(core_ref, d_query, d_kv, attn_w, out_half, batches)
    d_kv = after(d_kv, d_normed_oth)
    d_normed_a = d_normed_a + swap_core(d_normed_oth).astype(F32)
    x_own_f = x_own.astype(F32)
    inverse_a = rms_inverse(x_own_f)
    back_a, gain_a_part = rms_back(d_normed_a, x_own_f * inverse_a, inverse_a, gain_a)
    input_grad = d_resid + back_a
    gain_sum = jnp.concatenate([gain_a_part, gain_m_part], 0)
    gain_sum = gain_sum + swap_core(gain_sum)
    bit = 1
    while bit < seq_size:
        gain_sum = gain_sum + swap_seq(gain_sum, bit)
        bit *= 2
    gain_part = gain_sum
    for _ in range(chips - 1):
        gain_part = ring_step(gain_part)
        gain_sum = gain_sum + gain_part
    grad_kv = owner_sum(grad_chunks(starts, [normed_a], d_kv, seq_size, chips), 1)
    kv_parts = own_shard(after(grad_kv, gain_sum), [LANES] * (2 * kv_half // LANES))
    grad_kv = [
        jnp.concatenate(
            [part[:, :LANES] for part in kv_parts[i::2]]
            + [part[:, LANES:] for part in kv_parts[i::2]],
            axis=1,
        )
        for i in range(2)
    ]
    gain_sum = lax.dynamic_slice_in_dim(gain_sum, (seq_at * ctx_size + ctx_at) * shard, shard, 1)

    branch_m = out_slots[0] + out_last.astype(F32)
    activations = (residual + branch_m).astype(BF16)
    return (
        activations.reshape(tokens.shape),
        input_grad.reshape(tokens.shape),
        gain_sum[0],
        grad_query,
        grad_kv[0],
        grad_kv[1],
        grad_out,
        gain_sum[1],
        grad_gate,
        grad_up,
        grad_down,
    )


def solution(mesh):
    rows = P(None, "seq", "ctx", None)
    spread = P(("seq", "ctx"))
    spread_rows = P(("seq", "ctx"), None)
    return jax.shard_map(
        body,
        mesh=mesh,
        in_specs=(
            rows,
            P(None, "seq"),
            rows,
            spread,
            spread_rows,
            spread_rows,
            spread_rows,
            spread_rows,
            spread,
            P("seq", "ctx"),
            P("seq", "ctx"),
            P("ctx", "seq"),
        ),
        out_specs=(
            rows,
            rows,
            spread,
            spread_rows,
            spread_rows,
            spread_rows,
            spread_rows,
            spread,
            P("seq", "ctx"),
            P("seq", "ctx"),
            P("ctx", "seq"),
        ),
        check_vma=False,
    )
```

```python
import functools
import math

import jax
import jax.numpy as jnp
from jax import lax
from jax.experimental import pallas as pl
from jax.experimental.pallas import tpu as pltpu
from jax.sharding import PartitionSpec as P

HEAD_DIM = 64
LANES = 128
EPSILON = 1e-05
ROPE_BASE = 500000.0
MASKED = -1e30
WEIGHT = 6
VMEM_LIMIT = 56 * 1024 * 1024
F32 = jnp.float32
BF16 = jnp.bfloat16


def folded_order(count):
    return list(range(0, count, 2)) + list(range(1, count, 2))[::-1]


def swap_core(array):
    ctx = lax.axis_size("ctx")
    return lax.ppermute(array, "ctx", [(i, i ^ 1) for i in range(ctx)])


def swap_seq(array, bit):
    seq = lax.axis_size("seq")
    return lax.ppermute(array, "seq", [(i, i ^ bit) for i in range(seq)])


def ring_step(array):
    chips = lax.axis_size("ctx") // 2
    order = folded_order(chips)
    pairs = [
        (order[i] * 2 + core, order[(i + 1) % chips] * 2 + core)
        for i in range(chips)
        for core in range(2)
    ]
    return lax.ppermute(array, "ctx", pairs)


def ring_gather(array):
    slots = [array]
    for _ in range(lax.axis_size("ctx") // 2 - 1):
        slots.append(ring_step(slots[-1]))
    return slots


def ring_scatter(parts):
    chips = len(parts)
    total = parts[1 % chips].astype(F32)
    for k in range(2, chips + 1):
        total = ring_step(total.astype(BF16)).astype(F32) + parts[k % chips].astype(F32)
    return total


def cube_gather(array, route, *waits):
    seq = lax.axis_size("seq")
    bits = [1 << i for i in range(seq.bit_length() - 1)]
    pieces = {0: array}
    for bit in bits if route == 0 else bits[::-1]:
        seen = waits if len(pieces) > 1 else ()
        pieces.update({r ^ bit: swap_seq(after(p, *seen), bit) for r, p in pieces.items()})
    return [pieces[r] for r in range(seq)]


def cube_scatter(chunks, route, *waits):
    seq = lax.axis_size("seq")
    bits = [1 << i for i in range(seq.bit_length() - 1)]
    held = dict(enumerate(chunks))
    for bit in bits if route == 0 else bits[::-1]:
        seen = waits if len(held) > 2 else ()
        held = {
            r: held[r].astype(F32)
            + after(swap_seq(held[r ^ bit].astype(BF16), bit), *seen).astype(F32)
            for r in held
            if not r & bit
        }
    return held[0]


def after(array, *others):
    return lax.optimization_barrier((array, *others))[0]


def scaled_frequency():
    half_dim = HEAD_DIM // 2
    base_freq = ROPE_BASE ** (-jnp.arange(half_dim, dtype=F32) * 2.0 / HEAD_DIM)
    wave = 2.0 * math.pi / base_freq
    smooth = (8192.0 / wave - 1.0) / 3.0
    middle = (1.0 - smooth) * base_freq / 32.0 + smooth * base_freq
    return jnp.where(wave < 2048.0, base_freq, jnp.where(wave > 8192.0, base_freq / 32.0, middle))


def rope_tables(positions):
    angles = positions.astype(F32)[:, None] * scaled_frequency()[None, :]
    cosine, sine = jnp.cos(angles), jnp.sin(angles)
    return (
        jnp.concatenate([cosine] * 4, axis=1),
        jnp.concatenate([-sine, sine, -sine, sine], axis=1),
    )


def rotate_lanes(values, cosine, sine):
    lane = lax.broadcasted_iota(jnp.int32, values.shape, 1)
    partner = jnp.where(
        (lane % HEAD_DIM) < HEAD_DIM // 2,
        pltpu.roll(values, LANES - HEAD_DIM // 2, 1),
        pltpu.roll(values, HEAD_DIM // 2, 1),
    )
    return values * cosine + partner * sine


SMEM = pltpu.SMEM
ANYWHERE = pl.BlockSpec(memory_space=pl.ANY)
SCALARS = pl.BlockSpec(memory_space=pltpu.SMEM)
PARAMS = pltpu.CompilerParams(vmem_limit_bytes=VMEM_LIMIT)
NT = (((1,), (1,)), ((), ()))


def cost(flops, nbytes, transcendentals=0):
    return pl.CostEstimate(
        flops=int(WEIGHT * flops), bytes_accessed=int(nbytes), transcendentals=int(transcendentals)
    )


def dot(left, right):
    return jnp.dot(left, right, preferred_element_type=F32)


def dot_nt(left, right):
    return lax.dot_general(left, right, NT, preferred_element_type=F32)


def transposed(values):
    return values.astype(F32).T.astype(BF16)


def pack_kernel(kv_half, core_ref, wq, wk, wv, wo, gains, mine, other):
    def fill(out, which):
        at = 0
        for source in (wo, wq):
            half = source.shape[1] // 2
            out[:, at : at + half] = source[:, which * half : (which + 1) * half]
            at += half
        for i in range(kv_half // LANES):
            for source in (wk, wv):
                lo = which * kv_half + i * LANES
                out[:, at : at + LANES] = source[:, lo : lo + LANES]
                at += LANES
        out[:, at : at + LANES] = gains[...]

    for core in range(2):

        @pl.when(core_ref[0] == core)
        def _():
            fill(mine, core)
            fill(other, 1 - core)


def pack(core, wq, wk, wv, wo, gains):
    rows = wq.shape[0]
    width = (wq.shape[1] + wk.shape[1] + wv.shape[1] + wo.shape[1]) // 2 + LANES
    shape = jax.ShapeDtypeStruct((rows, width), BF16)
    whole = [pl.BlockSpec(memory_space=pltpu.VMEM)] * 5
    return pl.pallas_call(
        functools.partial(pack_kernel, wk.shape[1] // 2),
        in_specs=[SCALARS] + whole,
        out_shape=[shape, shape],
        compiler_params=PARAMS,
        cost_estimate=cost(0, 8 * rows * width),
    )(core, wq, wk, wv, wo, gains)


def stack_kernel(edges, core_ref, mine, other, *outs):
    rows = mine.shape[0]
    for core in range(2):

        @pl.when(core_ref[0] == core)
        def _():
            for source, at in ((mine, core), (other, 1 - core)):
                for i, out in enumerate(outs):
                    out[at * rows : (at + 1) * rows] = source[:, edges[i] : edges[i + 1]]


def stack_pieces(core, mine, other, widths):
    rows = mine.shape[0]
    edges = [sum(widths[:i]) for i in range(len(widths) + 1)]
    return pl.pallas_call(
        functools.partial(stack_kernel, edges),
        in_specs=[SCALARS] + [pl.BlockSpec(memory_space=pltpu.VMEM)] * 2,
        out_shape=[jax.ShapeDtypeStruct((2 * rows, width), BF16) for width in widths],
        compiler_params=PARAMS,
        cost_estimate=cost(0, 8 * mine.size),
    )(core, mine, other)


def placing(starts, pieces, w, sems):
    return [
        pltpu.make_async_copy(
            piece, w.at[pl.ds(pl.multiple_of(starts[i], 16), piece.shape[0])], sems.at[i]
        )
        for i, piece in enumerate(pieces)
    ]


def kv_kernel(count, batches, *refs):
    core_ref, starts, x_own, x_oth, cos_ref, sin_ref = refs[:6]
    pieces = refs[6 : 6 + count]
    kv_ref, normed, gains_ref, w_out, w, sems = refs[6 + count :]
    first = w.shape[1] - LANES - kv_ref.shape[1]
    slots = normed.shape[0] // (2 * batches)
    arriving = placing(starts, pieces, w, sems)
    for copy in arriving:
        copy.start()
    for copy in arriving:
        copy.wait()
    leaving = pltpu.make_async_copy(w, w_out, sems.at[count])
    leaving.start()
    table = w[:, w.shape[1] - LANES :].astype(F32).T
    gains_ref[...] = table[:8]
    for source, which in ((x_own, core_ref[0]), (x_oth, 1 - core_ref[0])):
        for b in range(batches):
            x = source[b * slots : (b + 1) * slots].astype(F32)
            inverse = lax.rsqrt(jnp.mean(x * x, axis=-1, keepdims=True) + EPSILON)
            at = pl.multiple_of((2 * b + which) * slots, slots)
            normed[pl.ds(at, slots)] = (x * inverse * table[:1]).astype(BF16)
    block = 2 * LANES
    for at in range(0, kv_ref.shape[1], block):
        raw = dot(normed[...], w[:, first + at : first + at + block])
        turned = rotate_lanes(raw[:, :LANES], cos_ref[...], sin_ref[...])
        kv_ref[:, at : at + LANES] = turned.astype(BF16)
        kv_ref[:, at + LANES : at + block] = raw[:, LANES:].astype(BF16)
    leaving.wait()


def project_kv(core, starts, x_own, x_oth, cosine, sine, pieces, batches, kv_width):
    rows, depth = 2 * x_own.shape[0], x_own.shape[1]
    width = pieces[0].shape[1]
    count = len(pieces)
    vmem = pl.BlockSpec(memory_space=pltpu.VMEM)
    return pl.pallas_call(
        functools.partial(kv_kernel, count, batches),
        in_specs=[SCALARS, SCALARS] + [vmem] * 4 + [ANYWHERE] * count,
        out_specs=[vmem, vmem, vmem, ANYWHERE],
        out_shape=[
            jax.ShapeDtypeStruct((rows, kv_width), BF16),
            jax.ShapeDtypeStruct((rows, depth), BF16),
            jax.ShapeDtypeStruct((8, depth), F32),
            jax.ShapeDtypeStruct((depth, width), BF16),
        ],
        scratch_shapes=[
            pltpu.VMEM((depth, width), BF16),
            pltpu.SemaphoreType.DMA((count + 1,)),
        ],
        compiler_params=PARAMS,
        cost_estimate=cost(2 * rows * depth * width, 4 * rows * depth + 4 * depth * width),
    )(core, starts, x_own, x_oth, cosine, sine, *pieces)


def q_kernel(first, normed, cos_ref, sin_ref, w, q_ref, held, sems):
    block = 2 * LANES
    width = q_ref.shape[1]
    copies = [
        pltpu.make_async_copy(
            w.at[:, pl.ds(first + at, block)], held.at[:, pl.ds(at, block)], sems.at[at // block]
        )
        for at in range(0, width, block)
    ]
    for copy in copies:
        copy.start()
    for at in range(0, width, block):
        copies[at // block].wait()
        raw = dot(normed[...], held[:, at : at + block])
        for lo in range(0, block, LANES):
            turned = rotate_lanes(raw[:, lo : lo + LANES], cos_ref[...], sin_ref[...])
            q_ref[:, at + lo : at + lo + LANES] = (turned / math.sqrt(HEAD_DIM)).astype(BF16)


def project_q(normed, cosine, sine, w, first, width):
    rows, depth = normed.shape
    vmem = pl.BlockSpec(memory_space=pltpu.VMEM)
    return pl.pallas_call(
        functools.partial(q_kernel, first),
        in_specs=[vmem] * 3 + [ANYWHERE],
        out_specs=vmem,
        out_shape=jax.ShapeDtypeStruct((rows, width), BF16),
        scratch_shapes=[
            pltpu.VMEM((depth, width), BF16),
            pltpu.SemaphoreType.DMA((width // (2 * LANES),)),
        ],
        compiler_params=PARAMS,
        cost_estimate=cost(2 * rows * depth * width, 2 * rows * depth + 4 * depth * width),
    )(normed, cosine, sine, w)


def set_bias(limit_ref, kpos_ref, qpos_ref, bias):
    @pl.when(pl.program_id(1) == 0)
    def _():
        limit = limit_ref[pl.program_id(0)]
        allowed = (kpos_ref[...] <= qpos_ref[...]) & (kpos_ref[...] < limit)
        bias[...] = jnp.where(allowed, 0.0, MASKED)


def attend_kernel(chips, limit_ref, kpos_ref, qpos_ref, q_ref, *refs):
    slots, (out_ref, lse_ref, bias) = refs[:chips], refs[chips:]
    set_bias(limit_ref, kpos_ref, qpos_ref, bias)
    heads = q_ref.shape[1] // HEAD_DIM
    kv = jnp.concatenate([slot[...] for slot in slots], axis=0)
    q_t = transposed(q_ref[...])
    v_t = transposed(kv[:, LANES:])
    outs = []
    for h in range(heads):
        a = h * 2 // heads
        k_h = kv[:, a * HEAD_DIM : (a + 1) * HEAD_DIM]
        scores = dot(k_h, q_t[h * HEAD_DIM : (h + 1) * HEAD_DIM]) + bias[...]
        top = jnp.max(scores, axis=0, keepdims=True)
        shifted = jnp.exp(scores - top)
        total = jnp.sum(shifted, axis=0, keepdims=True)
        out_t = dot(v_t[a * HEAD_DIM : (a + 1) * HEAD_DIM], shifted.astype(BF16))
        outs.append(out_t / total)
        lse_ref[h : h + 1, :] = top + jnp.log(total)
    out_ref[...] = jnp.concatenate(outs, axis=0).T.astype(BF16)


def attention_specs(batches, chips, rows, keys, width, heads, pairs):
    def at(shape):
        return pl.BlockSpec(shape, lambda b, i, n: (b, i))

    return (
        [
            pl.BlockSpec((keys, 1), lambda b, i, n: (0, 0)),
            pl.BlockSpec((1, rows), lambda b, i, n: (0, 0)),
            at((rows, width)),
        ]
        + [at((rows, 2 * LANES))] * chips,
        at((rows, width)),
        pl.BlockSpec((heads, rows), lambda b, i, n: (b * pairs + i, 0)),
    )


def attend(q, kv_slots, limits, kpos, qpos):
    rows, keys, batches, chips = qpos.shape[1], kpos.shape[0], limits.shape[0], len(kv_slots)
    pairs = kv_slots[0].shape[1] // (2 * LANES)
    width = q.shape[1] // pairs
    heads = width // HEAD_DIM
    ins, out, lse = attention_specs(batches, chips, rows, keys, width, heads, pairs)
    return pl.pallas_call(
        functools.partial(attend_kernel, chips),
        grid_spec=pltpu.PrefetchScalarGridSpec(
            num_scalar_prefetch=1,
            grid=(batches, pairs),
            in_specs=ins,
            out_specs=[out, lse],
            scratch_shapes=[pltpu.VMEM((keys, rows), F32)],
        ),
        out_shape=[
            jax.ShapeDtypeStruct(q.shape, BF16),
            jax.ShapeDtypeStruct((batches * pairs * heads, rows), F32),
        ],
        compiler_params=PARAMS,
        cost_estimate=cost(
            16 * batches * rows * keys * q.shape[1],
            4 * q.size + 2 * chips * kv_slots[0].size,
            batches * rows * keys * q.shape[1] // HEAD_DIM,
        ),
    )(limits, kpos, qpos, q, *kv_slots)


def attend_back_kernel(chips, limit_ref, kpos_ref, qpos_ref, q_ref, *refs):
    slots = refs[:chips]
    do_mine, do_other, lse_ref, cos_ref, sin_ref, dq_ref = refs[chips : chips + 6]
    d_slots, bias = refs[chips + 6 : 2 * chips + 6], refs[2 * chips + 6]
    set_bias(limit_ref, kpos_ref, qpos_ref, bias)
    rows, width = q_ref.shape
    heads = width // HEAD_DIM
    per_kv = heads // 2
    kv = jnp.concatenate([slot[...] for slot in slots], axis=0)
    d_out = (do_mine[...] + do_other[...].astype(F32)).astype(BF16)
    q_t = transposed(q_ref[...])
    do_t = transposed(d_out)
    k_t = transposed(kv[:, :LANES])
    lane = lax.broadcasted_iota(jnp.int32, (kv.shape[0], LANES), 1)
    d_queries = []
    d_keys, d_values = [], []
    for a in range(2):
        k_h = kv[:, a * HEAD_DIM : (a + 1) * HEAD_DIM]
        v_h = kv[:, LANES + a * HEAD_DIM : LANES + (a + 1) * HEAD_DIM]
        dk_sum, dv_sum = [None, None], [None, None]
        for g in range(per_kv):
            h = a * per_kv + g
            head = slice(h * HEAD_DIM, (h + 1) * HEAD_DIM)
            pair = slice((h // 2) * LANES, (h // 2 + 1) * LANES)
            scores = dot(k_h, q_t[head]) + bias[...]
            probs = jnp.exp(scores - lse_ref[h : h + 1, :])
            d_probs = dot(v_h, do_t[head])
            mean = jnp.sum(d_probs * probs, axis=0, keepdims=True)
            d_scores = (probs * (d_probs - mean)).astype(BF16)
            d_queries.append(dot(k_t[a * HEAD_DIM : (a + 1) * HEAD_DIM], d_scores))
            dk_term = dot(d_scores, q_ref[:, pair])
            dv_term = dot(probs.astype(BF16), d_out[:, pair])
            e = h % 2
            dk_sum[e] = dk_term if dk_sum[e] is None else dk_sum[e] + dk_term
            dv_sum[e] = dv_term if dv_sum[e] is None else dv_sum[e] + dv_term
        for sums, kept in ((dk_sum, d_keys), (dv_sum, d_values)):
            mixed = jnp.where(lane < HEAD_DIM, sums[0], sums[1])
            kept.append(mixed + pltpu.roll(mixed, HEAD_DIM, 1))
    d_key = jnp.where(lane < HEAD_DIM, d_keys[0], d_keys[1])
    d_value = jnp.where(lane < HEAD_DIM, d_values[0], d_values[1])
    for k, d_slot in enumerate(d_slots):
        d_slot[:, :LANES] = d_key[k * rows : (k + 1) * rows].astype(BF16)
        d_slot[:, LANES:] = d_value[k * rows : (k + 1) * rows].astype(BF16)
    d_query = jnp.concatenate(d_queries, axis=0).T
    for at in range(width // LANES):
        cut = slice(at * LANES, (at + 1) * LANES)
        turned = rotate_lanes(d_query[:, cut], cos_ref[...], -sin_ref[...])
        dq_ref[:, cut] = (turned / math.sqrt(HEAD_DIM)).astype(BF16)


def attend_back(q, kv_slots, do_mine, do_other, lse, limits, kpos, qpos, cosine, sine):
    rows, keys, batches, chips = qpos.shape[1], kpos.shape[0], limits.shape[0], len(kv_slots)
    pairs = kv_slots[0].shape[1] // (2 * LANES)
    width = q.shape[1] // pairs
    heads = width // HEAD_DIM
    ins, out, lse_spec = attention_specs(batches, chips, rows, keys, width, heads, pairs)
    table = pl.BlockSpec((rows, LANES), lambda b, i, n: (0, 0))
    return pl.pallas_call(
        functools.partial(attend_back_kernel, chips),
        grid_spec=pltpu.PrefetchScalarGridSpec(
            num_scalar_prefetch=1,
            grid=(batches, pairs),
            in_specs=ins + [out, out, lse_spec, table, table],
            out_specs=[out] + ins[3 : 3 + chips],
            scratch_shapes=[pltpu.VMEM((keys, rows), F32)],
        ),
        out_shape=[jax.ShapeDtypeStruct(q.shape, BF16)]
        + [jax.ShapeDtypeStruct(slot.shape, BF16) for slot in kv_slots],
        compiler_params=PARAMS,
        cost_estimate=cost(
            40 * batches * rows * keys * q.shape[1],
            10 * q.size + 4 * chips * kv_slots[0].size,
            batches * rows * keys * q.shape[1] // HEAD_DIM,
        ),
    )(limits, kpos, qpos, q, *kv_slots, do_mine, do_other, lse, cosine, sine)


def unrotate_kernel(last_ref, own_ref, cos_ref, sin_ref, out_ref):
    total = last_ref[...].astype(F32) + own_ref[...].astype(F32)
    for at in range(total.shape[1] // LANES):
        cut = slice(at * LANES, (at + 1) * LANES)
        part = total[:, cut]
        if at % 2 == 0:
            part = rotate_lanes(part, cos_ref[...], -sin_ref[...])
        out_ref[:, cut] = part.astype(BF16)


def unrotate(last, own, cosine, sine):
    return pl.pallas_call(
        unrotate_kernel,
        out_shape=jax.ShapeDtypeStruct(own.shape, BF16),
        compiler_params=PARAMS,
        cost_estimate=cost(0, 6 * own.size),
    )(last, own, cosine, sine)


def split_rows(batches, core_ref, acc, own, other):
    slots = acc.shape[0] // (2 * batches)
    for out, which in ((own, core_ref[0]), (other, 1 - core_ref[0])):
        for b in range(batches):
            at = pl.multiple_of((2 * b + which) * slots, slots)
            out[b * slots : (b + 1) * slots] = acc[pl.ds(at, slots)].astype(out.dtype)


def out_kernel(batches, core_ref, o_mine, o_other, w_all, own, other, w, acc, sems):
    half, width = o_mine.shape[1], w.shape[1]
    block = 2 * LANES
    copies = [
        pltpu.make_async_copy(
            w_all.at[:, pl.ds(lo, block)], w.at[:, pl.ds(lo, block)], sems.at[lo // block]
        )
        for lo in range(0, width, block)
    ]
    for copy in copies:
        copy.start()
    rows_mine = pl.ds(pl.multiple_of(core_ref[0] * half, half), half)
    rows_other = pl.ds(pl.multiple_of((1 - core_ref[0]) * half, half), half)
    for lo in range(0, width, block):
        cut = slice(lo, lo + block)
        copies[lo // block].wait()
        acc[:, cut] = dot(o_mine[...], w[rows_mine, cut]) + dot(o_other[...], w[rows_other, cut])
    split_rows(batches, core_ref, acc, own, other)


def project_out(core, o_mine, o_other, w, width, batches):
    rows, half = o_mine.shape
    vmem = pl.BlockSpec(memory_space=pltpu.VMEM)
    part = jax.ShapeDtypeStruct((rows // 2, width), F32)
    return pl.pallas_call(
        functools.partial(out_kernel, batches),
        in_specs=[SCALARS, vmem, vmem, ANYWHERE],
        out_specs=[vmem, vmem],
        out_shape=[part, part],
        scratch_shapes=[
            pltpu.VMEM((2 * half, width), BF16),
            pltpu.VMEM((rows, width), F32),
            pltpu.SemaphoreType.DMA((width // (2 * LANES),)),
        ],
        compiler_params=PARAMS,
        cost_estimate=cost(4 * rows * half * width, 4 * half * width + 12 * rows * width),
    )(core, o_mine, o_other, w)


def hidden_units(x, d, gate, up, down_t, hidden_ref, d_gate_ref, d_up_ref):
    gate_val = dot(x[...], gate[...])
    up_val = dot(x[...], up[...])
    d_hidden = dot(d[...], down_t[...])
    sigmoid_g = 1.0 / (1.0 + jnp.exp(-gate_val))
    activated = gate_val * sigmoid_g
    slope = sigmoid_g * (1.0 + gate_val * (1.0 - sigmoid_g))
    hidden_ref[...] = (activated * up_val).astype(BF16)
    d_gate_ref[...] = (d_hidden * up_val * slope).astype(BF16)
    d_up_ref[...] = (d_hidden * activated).astype(BF16)


def first_hidden_kernel(per, filled, *refs):
    arrived = refs[: 2 * per]
    weights = refs[2 * per : 2 * per + 3]
    x, d, hidden_ref, d_gate_ref, d_up_ref, sems = refs[2 * per + 3 + filled :]
    rows = arrived[0].shape[0]

    @pl.when(pl.program_id(0) == 0)
    def _():
        copies = [
            pltpu.make_async_copy(
                arrived[2 * i + j], out.at[pl.ds(i * rows, rows)], sems.at[2 * i + j]
            )
            for i in range(per)
            for j, out in enumerate((x, d))
        ]
        for copy in copies:
            copy.start()
        for copy in copies:
            copy.wait()

    hidden_units(x, d, *weights, hidden_ref, d_gate_ref, d_up_ref)


def second_hidden_kernel(filled, x, d, gate, up, down_t, *refs):
    hidden_units(x, d, gate, up, down_t, *refs[filled:])


def hidden_group(at, groups, arrived, weights, kept, rows_of=None):
    width = weights.shape[0]
    hidden_width = weights.shape[1] // 3
    tile = 2 * LANES
    tiles = hidden_width // tile
    if rows_of is None:
        height = arrived[0].shape[0] * len(arrived) // 2
        per = len(arrived) // 2
        total = height * groups
        sources, source_specs = arrived, [ANYWHERE] * len(arrived)
        wide = [jax.ShapeDtypeStruct((total, width), BF16)] * 2
        scratch = [pltpu.SemaphoreType.DMA((2 * per,))]
    else:
        total = rows_of[0].shape[0]
        height = total // groups
        sources = list(rows_of)
        source_specs = [pl.BlockSpec((height, width), lambda j: (at, 0))] * 2
        wide, scratch = [], []
    narrow = [jax.ShapeDtypeStruct((total, hidden_width), BF16)] * 3
    filled = 0 if kept is None else len(wide) + 3
    kernel = (
        functools.partial(first_hidden_kernel, per, filled)
        if rows_of is None
        else functools.partial(second_hidden_kernel, filled)
    )
    first = len(sources) + 3
    return pl.pallas_call(
        kernel,
        grid=(tiles,),
        in_specs=source_specs
        + [
            pl.BlockSpec((width, tile), lambda j, skipped=i * tiles: (0, skipped + j))
            for i in range(3)
        ]
        + [ANYWHERE] * filled,
        out_specs=[pl.BlockSpec((height, width), lambda j: (at, 0))] * len(wide)
        + [pl.BlockSpec((height, tile), lambda j: (at, j))] * 3,
        out_shape=wide + narrow,
        scratch_shapes=scratch,
        input_output_aliases={first + i: i for i in range(filled)},
        compiler_params=PARAMS,
        cost_estimate=cost(
            6 * height * width * hidden_width,
            6 * width * hidden_width + 12 * height * width,
            height * hidden_width,
        ),
    )(*sources, weights, weights, weights, *([] if kept is None else kept))


def mlp_back_kernel(*refs):
    parts, weights = (refs[:3], refs[3:6]), refs[6:8]
    back_ref, out_ref, held_own, held_oth, sems = refs[8:]
    width, count = back_ref.shape[1], refs[0].shape[1]
    block = 4 * LANES
    steps = width // block
    copies = [
        pltpu.make_async_copy(
            weight.at[pl.ds(lo, block)],
            held.at[pl.ds(lo, block)],
            sems.at[i * steps + lo // block],
        )
        for i, (weight, held) in enumerate(zip(weights, (held_own, held_oth)))
        for lo in range(0, width, block)
    ]
    for step in range(steps):
        for i in range(2):
            copies[i * steps + step].start()
    for step in range(steps):
        cut = slice(step * block, (step + 1) * block)
        back, out = 0.0, 0.0
        for i, held in enumerate((held_own, held_oth)):
            copies[i * steps + step].wait()
            hidden, d_gate, d_up = parts[i]
            back += dot_nt(d_gate[...], held[cut, :count])
            back += dot_nt(d_up[...], held[cut, count : 2 * count])
            out += dot_nt(hidden[...], held[cut, 2 * count :])
        back_ref[:, cut] = back.astype(BF16)
        out_ref[:, cut] = out.astype(BF16)


def mlp_back(at, groups, own, other, weights, weights_oth):
    height, hidden_width = own[0].shape[0] // groups, own[0].shape[1]
    width = weights.shape[0]
    return pl.pallas_call(
        mlp_back_kernel,
        grid=(1,),
        in_specs=[pl.BlockSpec((height, hidden_width), lambda j: (at, 0))] * 6 + [ANYWHERE] * 2,
        out_specs=[pl.BlockSpec((height, width), lambda j: (0, 0))] * 2,
        out_shape=[jax.ShapeDtypeStruct((height, width), BF16)] * 2,
        scratch_shapes=[
            pltpu.VMEM(weights.shape, BF16),
            pltpu.VMEM(weights.shape, BF16),
            pltpu.SemaphoreType.DMA((2 * (width // (4 * LANES)),)),
        ],
        compiler_params=PARAMS,
        cost_estimate=cost(
            12 * height * width * hidden_width, 12 * width * hidden_width + 14 * height * width
        ),
    )(*own, *other, weights, weights_oth)


def d_attended_kernel(batches, other_blocks, core_ref, d_own, d_oth, w_ref, mine, other, d_rows):
    step = pl.program_id(0)
    slots = d_own.shape[0] // batches

    @pl.when(step == 0)
    def _():
        for source, which in ((d_own, core_ref[0]), (d_oth, 1 - core_ref[0])):
            for b in range(batches):
                at = pl.multiple_of((2 * b + which) * slots, slots)
                d_rows[pl.ds(at, slots)] = source[b * slots : (b + 1) * slots]

    term = dot_nt(d_rows[...], w_ref[...])

    @pl.when(step < other_blocks)
    def _():
        other[...] = term.astype(BF16)

    @pl.when(step >= other_blocks)
    def _():
        mine[...] = term


def d_attended(core, d_own, d_oth, w, batches):
    rows, width = 2 * d_own.shape[0], d_own.shape[1]
    heads_width = w.shape[0]
    block = 2 * LANES
    blocks = heads_width // 2 // block

    def whole(shape):
        return pl.BlockSpec(shape, lambda j, c: (0, 0))

    return pl.pallas_call(
        functools.partial(d_attended_kernel, batches, blocks),
        grid_spec=pltpu.PrefetchScalarGridSpec(
            num_scalar_prefetch=1,
            grid=(2 * blocks,),
            in_specs=[
                whole(d_own.shape),
                whole(d_own.shape),
                pl.BlockSpec((block, width), lambda j, c: ((j + (1 - c[0]) * blocks) % (2 * blocks), 0)),
            ],
            out_specs=[
                pl.BlockSpec((rows, block), lambda j, c: (0, jnp.maximum(j - blocks, 0))),
                pl.BlockSpec((rows, block), lambda j, c: (0, jnp.minimum(j, blocks - 1))),
                whole((rows, width)),
            ],
        ),
        out_shape=[
            jax.ShapeDtypeStruct((rows, heads_width // 2), F32),
            jax.ShapeDtypeStruct((rows, heads_width // 2), BF16),
            jax.ShapeDtypeStruct((rows, width), BF16),
        ],
        compiler_params=PARAMS,
        cost_estimate=cost(
            2 * rows * width * heads_width, 2 * width * heads_width + 6 * rows * heads_width
        ),
    )(core, d_own, d_oth, w)


def grad_kernel(count, parts, chips, starts, *refs):
    sources, right, outs, turned = refs[:count], refs[count], refs[count + 1 : -1], refs[-1]
    shard = turned.shape[0] // (parts * chips)
    at = 0
    for source in sources:
        for lo in range(0, source.shape[1], 4 * LANES):
            turned[at : at + 4 * LANES] = transposed(source[:, lo : lo + 4 * LANES])
            at += 4 * LANES
    for r in range(parts):
        left = jnp.concatenate(
            [
                turned[pl.ds(pl.multiple_of(starts[r * chips + k], 16), shard)]
                for k in range(chips)
            ],
            axis=0,
        )
        outs[r][...] = dot(left, right[...]).astype(BF16)


def grad_chunks(starts, sources, right, parts, chips):
    rows = right.shape[0]
    depth = sum(source.shape[1] for source in sources)
    shape = jax.ShapeDtypeStruct((depth // parts, right.shape[1]), BF16)
    vmem = pl.BlockSpec(memory_space=pltpu.VMEM)
    return pl.pallas_call(
        functools.partial(grad_kernel, len(sources), parts, chips),
        in_specs=[SCALARS] + [vmem] * (len(sources) + 1),
        out_shape=[shape] * parts,
        scratch_shapes=[pltpu.VMEM((depth, rows), BF16)],
        compiler_params=PARAMS,
        cost_estimate=cost(
            2 * rows * depth * right.shape[1], 2 * rows * depth + 2 * depth * right.shape[1]
        ),
    )(starts, *sources, right)


def d_normed_kernel(batches, core_ref, dq_ref, dkv_ref, wq_ref, wkv_ref, own, other, acc):
    acc[...] = dot_nt(dq_ref[...], wq_ref[...]) + dot_nt(dkv_ref[...], wkv_ref[...])
    split_rows(batches, core_ref, acc, own, other)


def d_normed_rows(core, dq, dkv, w, first, batches):
    rows, depth = dq.shape[0], w.shape[0]
    width = dq.shape[1] + dkv.shape[1]
    block = 4 * LANES
    q_at, kv_at = first // dq.shape[1], (first + dq.shape[1]) // dkv.shape[1]

    def whole(shape):
        return pl.BlockSpec(shape, lambda j: (0, 0))

    part = pl.BlockSpec((rows // 2, block), lambda j: (0, j))
    return pl.pallas_call(
        functools.partial(d_normed_kernel, batches),
        grid=(depth // block,),
        in_specs=[
            SCALARS,
            whole(dq.shape),
            whole(dkv.shape),
            pl.BlockSpec((block, dq.shape[1]), lambda j: (j, q_at)),
            pl.BlockSpec((block, dkv.shape[1]), lambda j: (j, kv_at)),
        ],
        out_specs=[part, part],
        out_shape=[
            jax.ShapeDtypeStruct((rows // 2, depth), F32),
            jax.ShapeDtypeStruct((rows // 2, depth), BF16),
        ],
        scratch_shapes=[pltpu.VMEM((rows, block), F32)],
        compiler_params=PARAMS,
        cost_estimate=cost(2 * rows * depth * width, 2 * depth * width + 4 * rows * depth),
    )(core, dq, dkv, w, w)


def rms_inverse(values):
    return lax.rsqrt(jnp.mean(values * values, axis=-1, keepdims=True) + EPSILON)


def rms_back(grad_in, plain, inverse, gain):
    scaled = grad_in * gain
    back = inverse * (scaled - plain * jnp.mean(scaled * plain, axis=-1, keepdims=True))
    return (back, jnp.sum(grad_in * plain, axis=0, keepdims=True))


def body(
    tokens,
    lengths,
    cotangent,
    attn_gain,
    w_query,
    w_key,
    w_value,
    w_out,
    mlp_gain,
    w_gate,
    w_up,
    w_down,
):
    batches, _, slot_count, model_width = tokens.shape
    seq_size, ctx_size = lax.axis_size("seq"), lax.axis_size("ctx")
    chips = ctx_size // 2
    seq_at, ctx_at = lax.axis_index("seq"), lax.axis_index("ctx")
    chip_at, core = ctx_at // 2, ctx_at % 2
    core_ref = core.reshape(1).astype(jnp.int32)
    order = folded_order(chips)
    shard = w_query.shape[0]
    query_half, kv_half = w_query.shape[1] // 2, w_key.shape[1] // 2
    out_half = model_width // 2
    chip_rows = 2 * slot_count
    own_rows = batches * slot_count
    limits = lengths[:, 0]

    def chip_back(k):
        index = jnp.int32(0)
        for place, chip in enumerate(order):
            index = jnp.where(chip_at == chip, order[(place - k) % chips], index)
        return index

    slot_chip = jnp.stack([chip_back(k) for k in range(chips)])
    rank = (seq_at ^ jnp.arange(seq_size))[:, None] * chips + slot_chip[None, :]
    starts = (rank * (2 * shard)).reshape(-1).astype(jnp.int32)
    out_starts = (starts + core * query_half) % (2 * query_half)

    def half(array, which, axis):
        size = array.shape[axis] // 2
        return lax.dynamic_slice_in_dim(array, which * size, size, axis)

    def mine(array, axis):
        return half(array, core, axis)

    def others(array, axis):
        return half(array, 1 - core, axis)

    def by_core(own, other, axis):
        return jnp.where(
            core == 0,
            jnp.concatenate([own, other], axis),
            jnp.concatenate([other, own], axis),
        )

    q_positions = chip_at * chip_rows + jnp.arange(chip_rows)
    cosine, sine = rope_tables(q_positions)
    cosine_all, sine_all = jnp.tile(cosine, (batches, 1)), jnp.tile(sine, (batches, 1))
    qpos = q_positions[None, :]
    kpos = (slot_chip[:, None] * chip_rows + jnp.arange(chip_rows)[None, :]).reshape(-1, 1)
    own_pos = ctx_at * slot_count + jnp.arange(slot_count)
    valid = (own_pos[None, :] < limits[:, None]).astype(F32).reshape(own_rows, 1)
    d_output = cotangent.reshape(own_rows, model_width).astype(F32) * valid
    d_rows = d_output.astype(BF16)

    gains = jnp.concatenate(
        [attn_gain[:, None], mlp_gain[:, None], jnp.zeros((shard, LANES - 2), BF16)], axis=1
    )
    x_own = tokens.reshape(own_rows, model_width)
    x_oth = swap_core(x_own)
    packed, to_other = pack(core_ref, w_query, w_key, w_value, w_out, gains)
    (piece_a,) = stack_pieces(core_ref, packed, swap_core(to_other), [packed.shape[1]])
    ring_a, cubes_a = [after(piece_a, x_oth)], []
    for k in range(chips):
        waits = []
        if k + 1 == chips:
            d_slots = [d_rows, ring_step(after(d_rows, ring_a[-1]))]
            waits = [d_slots[1]]
        cubes_a.append(cube_gather(ring_a[k], k % 2, *waits))
        if k + 1 < chips:
            seen = [cubes_a[k - 1][1], cubes_a[k - 1][2]] if k else []
            ring_a.append(ring_step(after(ring_a[k], *seen)))
    mlp_w = jnp.concatenate([w_gate, w_up, w_down.T], axis=1)
    mlp_w = lax.all_gather(after(mlp_w, *sum(cubes_a, [])), "seq", axis=0, tiled=True)

    def flat(cubes):
        return [cubes[k][r] for r in range(seq_size) for k in range(chips)]

    kv, normed_a, gain_rows, attn_w = project_kv(
        core_ref, starts, x_own, x_oth, cosine_all, sine_all, flat(cubes_a), batches, 2 * kv_half
    )
    gain_a, gain_m = gain_rows[0:1], gain_rows[1:2]
    kv_slots = ring_gather(kv)
    q = project_q(
        normed_a, cosine_all, sine_all, attn_w, out_half, query_half
    )
    for k in range(2, chips):
        d_slots.append(ring_step(after(d_slots[-1], *([kv_slots[-1]] if k == 2 else []))))
    attended, lse = attend(q, kv_slots, limits, kpos, qpos)
    attended_oth = swap_core(after(attended, d_slots[2 % chips]))
    branch, branch_oth = project_out(
        core_ref, attended, attended_oth, attn_w, out_half, batches
    )

    branch_oth = after(swap_core(branch_oth), d_slots[-1])
    residual = x_own.astype(F32) + by_core(branch, branch_oth, 1)
    inverse_m = rms_inverse(residual)
    normed_m = (residual * inverse_m * gain_m).astype(BF16)
    x_slots = [normed_m]
    for k in range(1, min(chips, 3)):
        x_slots.append(ring_step(x_slots[-1]))
    mlp_w_oth = swap_core(after(mlp_w, x_slots[1 % chips]))
    per = 2 if chips % 2 == 0 else 1
    groups = chips // per
    kept, kept_oth, back_parts, out_slots, out_sums = None, None, [], [], []
    for g in range(groups):
        arrived = []
        for k in range(g * per, (g + 1) * per):
            arrived += [x_slots[k], d_slots[k]]
        kept = hidden_group(g, groups, arrived, mlp_w, kept)
        while len(x_slots) < chips:
            x_slots.append(ring_step(after(x_slots[-1], kept[0])))
        kept_oth = hidden_group(g, groups, None, mlp_w_oth, kept_oth, kept[:2])
        own, other = list(kept[2:]), list(kept_oth)
        if g == 0:
            own[0] = after(own[0], x_slots[min(2, chips - 1)])
        elif g == 1:
            back_first = ring_step(back_parts[1])
            own[0] = after(own[0], back_first)
        back, out = mlp_back(g, groups, own, other, mlp_w, mlp_w_oth)
        for i in range(per):
            rows = slice(i * own_rows, (i + 1) * own_rows)
            back_parts.append(back[rows])
            out_slots.append(out[rows].astype(F32))
    total, steps = back_parts[1 % chips].astype(F32), []
    for k in range(2, chips + 1):
        low = total.astype(BF16)
        if k == 3:
            kept = [after(array, low) for array in kept]
        steps.append(back_first if k == 2 and groups > 1 else ring_step(low))
        total = steps[-1].astype(F32) + back_parts[k % chips].astype(F32)
    d_normed = total
    x_all, d_all = kept[:2]

    def rows_product(left, right):
        return jnp.einsum("ri,rj->ij", left, right, preferred_element_type=F32).astype(BF16)

    def seq_sum(array, axis):
        return lax.psum_scatter(array, "seq", scatter_dimension=axis, tiled=True).astype(F32)

    products = [(rows_product(kept[2], d_all), rows_product(kept_oth[0], d_all))]
    for i in range(2):
        products.append(
            [
                rows_product(x_all, after(array, *steps[1 : 1 + i]))
                for array in (kept[3 + i], kept_oth[1 + i])
            ]
        )
    sums = [
        (own.astype(F32) + swap_core(other).astype(F32)).astype(BF16) for own, other in products
    ]
    grad_down, grad_gate, grad_up = (
        seq_sum(array, axis) for array, axis in zip(sums, (1, 0, 0))
    )

    plain_m = residual * inverse_m
    back_m, gain_m_part = rms_back(d_normed, plain_m, inverse_m, gain_m)
    d_resid = d_output + back_m
    d_low = d_resid.astype(BF16)
    out_sum = out_slots[1 % chips]
    for k in range(2, chips):
        waits = [d_low]
        if k > 2:
            waits = [do_mine]
        out_sums.append(ring_step(after(out_sum.astype(BF16), *waits)))
        out_sum = out_sums[-1].astype(F32) + out_slots[k]
        if k == 2:
            do_mine, do_other, d_half = d_attended(
                core_ref,
                mine(d_low, 1),
                swap_core(others(d_low, 1)),
                after(attn_w, *sum(map(list, products), [])),
                batches,
            )
    d_query, *d_kv_slots = attend_back(
        q,
        kv_slots,
        do_mine,
        after(swap_core(do_other), out_sums[0], *sums),
        lse,
        limits,
        kpos,
        qpos,
        cosine,
        sine,
    )

    def owner_sum(chunks, route, *waits):
        summed = cube_scatter(chunks, route, *waits)
        rows = 2 * shard
        return ring_scatter([summed[k * rows : (k + 1) * rows] for k in range(chips)])

    def own_shard(summed, lanes):
        received = swap_core(others(summed, 0))
        kept_rows = mine(summed, 0)
        edges = [sum(lanes[:i]) for i in range(len(lanes) + 1)]
        return [
            by_core(kept_rows[:, lo:hi], received[:, lo:hi], 1)
            for lo, hi in zip(edges[:-1], edges[1:])
        ]

    passing = [ring_step(after(d_kv_slots[1], *out_sums[1:2]))]
    for k in range(2, chips):
        total = passing[-1].astype(F32) + d_kv_slots[k].astype(F32)
        passing.append(ring_step(total.astype(BF16)))
    grad_out = owner_sum(
        grad_chunks(out_starts, [attended, attended_oth], d_half, seq_size, chips), 1, passing[0]
    )
    (grad_out,) = own_shard(grad_out, [out_half])
    grad_query = owner_sum(grad_chunks(starts, [normed_a], d_query, seq_size, chips), 0)
    (grad_query,) = own_shard(grad_query, [query_half])
    out_last = ring_step(after(out_sum.astype(BF16), passing[1]))
    d_kv = unrotate(passing[-1], d_kv_slots[0], cosine_all, sine_all)
    d_normed_a, d_normed_oth = d_normed_rows(core_ref, d_query, d_kv, attn_w, out_half, batches)
    d_kv = after(d_kv, d_normed_oth)
    d_normed_a = d_normed_a + swap_core(d_normed_oth).astype(F32)
    x_own_f = x_own.astype(F32)
    inverse_a = rms_inverse(x_own_f)
    back_a, gain_a_part = rms_back(d_normed_a, x_own_f * inverse_a, inverse_a, gain_a)
    input_grad = d_resid + back_a
    gain_sum = jnp.concatenate([gain_a_part, gain_m_part], 0)
    gain_sum = gain_sum + swap_core(gain_sum)
    bit = 1
    while bit < seq_size:
        gain_sum = gain_sum + swap_seq(gain_sum, bit)
        bit *= 2
    gain_part = gain_sum
    for _ in range(chips - 1):
        gain_part = ring_step(gain_part)
        gain_sum = gain_sum + gain_part
    grad_kv = owner_sum(grad_chunks(starts, [normed_a], d_kv, seq_size, chips), 1)
    kv_parts = own_shard(after(grad_kv, gain_sum), [LANES] * (2 * kv_half // LANES))
    grad_kv = [
        jnp.concatenate(
            [part[:, :LANES] for part in kv_parts[i::2]]
            + [part[:, LANES:] for part in kv_parts[i::2]],
            axis=1,
        )
        for i in range(2)
    ]
    gain_sum = lax.dynamic_slice_in_dim(gain_sum, (seq_at * ctx_size + ctx_at) * shard, shard, 1)

    branch_m = out_slots[0] + out_last.astype(F32)
    activations = (residual + branch_m).astype(BF16)
    return (
        activations.reshape(tokens.shape),
        input_grad.reshape(tokens.shape),
        gain_sum[0],
        grad_query,
        grad_kv[0],
        grad_kv[1],
        grad_out,
        gain_sum[1],
        grad_gate,
        grad_up,
        grad_down,
    )


def solution(mesh):
    rows = P(None, "seq", "ctx", None)
    spread = P(("seq", "ctx"))
    spread_rows = P(("seq", "ctx"), None)
    return jax.shard_map(
        body,
        mesh=mesh,
        in_specs=(
            rows,
            P(None, "seq"),
            rows,
            spread,
            spread_rows,
            spread_rows,
            spread_rows,
            spread_rows,
            spread,
            P("seq", "ctx"),
            P("seq", "ctx"),
            P("ctx", "seq"),
        ),
        out_specs=(
            rows,
            rows,
            spread,
            spread_rows,
            spread_rows,
            spread_rows,
            spread_rows,
            spread,
            P("seq", "ctx"),
            P("seq", "ctx"),
            P("ctx", "seq"),
        ),
        check_vma=False,
    )
```
